128 devices in a mesh: head: 8 (over x_hi, y), blk: 16 (over x_lo, z, core).
Axes of the slice: x: 4 (x_hi: 2, x_lo: 2; x = x_hi * 2 + x_lo), y: 4, z: 4, core: 2. Of those that a mesh axis runs over, the one named last changes fastest.
Arguments:
- tokens: bfloat16 [16384, 1024], P(('blk', 'head')), may hold values from -24 to 24
- cotangent: bfloat16 [16384, 1024], P(('blk', 'head')), may hold values from -6 to 6
- segments: int32 [16384], replicated, may hold values from 0 to 6, as said below
- attn_gain: bfloat16 [1024], P(('head', 'blk')), may hold values from 0.5 to 1.5
- w_query: bfloat16 [1024, 2048], P(('head', 'blk')), may hold values from -0.1875 to 0.1875
- key_matrix: bfloat16 [1024, 1024], P(('head', 'blk')), may hold values from -0.1875 to 0.1875
- value_matrix: bfloat16 [1024, 1024], P(('head', 'blk')), may hold values from -0.1875 to 0.1875
- query_gain: bfloat16 [128], P(('head', 'blk')), may hold values from 1 to 2
- key_gain: bfloat16 [128], P(('head', 'blk')), may hold values from 1 to 2
- w_out: bfloat16 [2048, 1024], P(('head', 'blk')), may hold values from -2 to 2
- ffn_gain: bfloat16 [1024], P(('head', 'blk')), may hold values from 0.5 to 1.5
- w_gate: bfloat16 [1024, 3072], P(('head', 'blk')), may hold values from -0.1875 to 0.1875
- w_up: bfloat16 [1024, 3072], P(('head', 'blk')), may hold values from -0.1875 to 0.1875
- w_down: bfloat16 [3072, 1024], P(('head', 'blk')), may hold values from -0.109375 to 0.109375
Outputs:
- output: bfloat16 [16384, 1024], P(('blk', 'head'))
- input_grad: bfloat16 [16384, 1024], P(('blk', 'head'))
- grad_attn_gain: float32 [1024], P(('head', 'blk'))
- grad_query: float32 [1024, 2048], P(('head', 'blk'))
- grad_key: float32 [1024, 1024], P(('head', 'blk'))
- grad_value: float32 [1024, 1024], P(('head', 'blk'))
- grad_query_gain: float32 [128], P(('head', 'blk'))
- grad_key_gain: float32 [128], P(('head', 'blk'))
- grad_out: float32 [2048, 1024], P(('head', 'blk'))
- grad_ffn_gain: float32 [1024], P(('head', 'blk'))
- grad_gate: float32 [1024, 3072], P(('head', 'blk'))
- grad_up: float32 [1024, 3072], P(('head', 'blk'))
- grad_down: float32 [3072, 1024], P(('head', 'blk'))
The draws below stay inside these ranges and needn't reach their ends.
Inputs may be any that keep to these rules, and one draw needn't show every extreme that they name: `segments`: ids never fall along the sequence; one document starts within the first 1024 tokens and ends within the last 1024 tokens, the others lie inside those two stretches.
All inputs are finite; a program needn't handle non-finite values.
Results may differ from the reference program's by a relative error of at most 0.035.
Values may be sent and summed in bfloat16 or wider, within the bound.
A program may use at most 128 MiB of HBM per device.

```python
import jax
import jax.numpy as jnp
from jax import lax

MODEL_WIDTH = 1024
QUERY_HEADS = 16
KEY_VALUE_HEADS = 8
HEAD_SIZE = 128
FF = 3072
ATTENTION_SPAN = 1024
TOK_DEV = 128
BLOCK = 1024
TOKENS = 16384
N_HEAD = 8


def draw_segments(key, part):
    key = jax.random.fold_in(key, 11)
    early_key, later_key = jax.random.split(key)
    early_cuts = jax.random.randint(early_key, (3,), 1, BLOCK, dtype=jnp.int32)
    later_cuts = jax.random.randint(later_key, (3,), TOKENS - BLOCK + 1, TOKENS, dtype=jnp.int32)
    bounds = jnp.concatenate([early_cuts, later_cuts])
    places = jnp.arange(TOKENS, dtype=jnp.int32)
    return jnp.sum((places[:, None] >= bounds[None, :]).astype(jnp.int32), axis=1)


def raised(values, stream_key, source, target, shards_of, factor):
    def block_of(dim):
        return (jnp.arange(values.shape[dim]) // (values.shape[dim] // shards_of)).reshape((-1,) + (1,) * (values.ndim - 1 - dim))

    one_side = jax.random.permutation(stream_key, shards_of)[block_of(target)]
    second = (block_of(target) + shards_of // 2) % shards_of
    return jnp.where((block_of(source) == one_side) | (block_of(source) == second), factor * values, values)


def levels(key, dims, shards, smallest, top_value):
    loudness = 1.0
    for position, blocks in shards:
        steps = jax.random.uniform(jax.random.fold_in(jax.random.fold_in(key, 6), position), (blocks,), jnp.float32, smallest / len(shards), top_value / len(shards))
        loudness = loudness * jnp.repeat(jnp.exp(steps), dims[position] // blocks).reshape((-1,) + (1,) * (len(dims) - 1 - position))
    return loudness


def noise(rng, extent, deviation, reach, cuts=(), kind=jnp.bfloat16):
    loudness = levels(rng, extent, cuts, -0.22, 0.18) if cuts else 1.0
    drawn = jax.random.normal(rng, extent, jnp.float32) * deviation * loudness
    return jnp.minimum(jnp.maximum(drawn, -reach), reach).astype(kind)


def bell_draw_with(own_key, dims, scale, reach, cuts, heavy, kind=jnp.bfloat16):
    entries = scale * jax.random.normal(own_key, dims, jnp.float32)
    if cuts:
        entries = entries * levels(own_key, dims, cuts, -0.22, 0.18)
    return jnp.clip(raised(entries, jax.random.fold_in(own_key, 3), *heavy), -reach, reach).astype(kind)


def setup_inputs(seed: int = 0) -> dict:
    splits = jax.random.split(jax.random.key(seed), 15)
    return {
        "tokens": bell_draw_with(splits[0], (TOKENS, MODEL_WIDTH), 1.0, 24.0, ((0, 128),), (0, 1, 128, 5.5)),
        "cotangent": noise(splits[1], (TOKENS, MODEL_WIDTH), 1.0, 6.0, ((0, 128),)),
        "segments": draw_segments(jax.random.fold_in(splits[14], 71), 0),
        "attn_gain": jnp.clip(0.5 + 1.0 * jax.random.uniform(splits[3], (MODEL_WIDTH,), jnp.float32) ** levels(splits[3], (MODEL_WIDTH,), ((0, 128),), -0.2, 0.2), 0.5, 1.5).astype(jnp.bfloat16),
        "w_query": noise(splits[4], (MODEL_WIDTH, QUERY_HEADS * HEAD_SIZE), MODEL_WIDTH ** -0.5, 0.1875, ((0, 128),)),
        "key_matrix": noise(splits[5], (MODEL_WIDTH, KEY_VALUE_HEADS * HEAD_SIZE), MODEL_WIDTH ** -0.5, 0.1875, ((0, 128),)),
        "value_matrix": noise(splits[6], (MODEL_WIDTH, KEY_VALUE_HEADS * HEAD_SIZE), MODEL_WIDTH ** -0.5, 0.1875, ((0, 128),)),
        "query_gain": jnp.clip(1.0 + 1.0 * jax.random.uniform(splits[7], (HEAD_SIZE,), jnp.float32) ** levels(splits[7], (HEAD_SIZE,), ((0, 128),), -0.2, 0.2), 1.0, 2.0).astype(jnp.bfloat16),
        "key_gain": jnp.clip(1.0 + 1.0 * jax.random.uniform(splits[8], (HEAD_SIZE,), jnp.float32) ** levels(splits[8], (HEAD_SIZE,), ((0, 128),), -0.2, 0.2), 1.0, 2.0).astype(jnp.bfloat16),
        "w_out": noise(splits[9], (QUERY_HEADS * HEAD_SIZE, MODEL_WIDTH), (QUERY_HEADS * HEAD_SIZE // 256) ** -0.5, 2.0, ((0, 128),)),
        "ffn_gain": jnp.clip(0.5 + 1.0 * jax.random.uniform(splits[10], (MODEL_WIDTH,), jnp.float32) ** levels(splits[10], (MODEL_WIDTH,), ((0, 128),), -0.2, 0.2), 0.5, 1.5).astype(jnp.bfloat16),
        "w_gate": noise(splits[11], (MODEL_WIDTH, FF), MODEL_WIDTH ** -0.5, 0.1875, ((0, 128),)),
        "w_up": noise(splits[12], (MODEL_WIDTH, FF), MODEL_WIDTH ** -0.5, 0.1875, ((0, 128),)),
        "w_down": noise(splits[13], (FF, MODEL_WIDTH), FF ** -0.5, 0.109375, ((0, 128),)),
    }


@jax.custom_vjp
def lower_part(v):
    return lax.optimization_barrier(v.astype(jnp.bfloat16)).astype(jnp.float32)

@jax.custom_vjp
def lower_part_backward(v):
    return v

def low_keep(v):
    return (lower_part(v), None)

def low_pass(kept, grad):
    return (grad,)

def back_keep(v):
    return (v, None)

def back_low(kept, grad):
    return (lower_part(grad),)
lower_part.defvjp(low_keep, low_pass)
lower_part_backward.defvjp(back_keep, back_low)
norm_eps = 1e-06
rope_base = 1000000.0
tile_most = 512
masked_score = -1e+30
highest = lax.Precision.HIGHEST

def matrix_product(left, right):
    return jnp.dot(left, right, precision=highest)

def rms_scale(value_rows):
    return lax.rsqrt(lax.optimization_barrier(jnp.mean(value_rows * value_rows, axis=-1, keepdims=True)) + norm_eps)

def rotary_tables(first_row, row_count):
    places = (first_row + jnp.arange(row_count, dtype=jnp.int32)).astype(jnp.float32)
    inverse_freq = rope_base ** (-jnp.arange(0, HEAD_SIZE, 2, dtype=jnp.float32) / HEAD_SIZE)
    angles = places[:, None] * inverse_freq[None, :]
    angles = jnp.concatenate([angles, angles], axis=-1)
    return (jnp.cos(angles)[:, None, :], jnp.sin(angles)[:, None, :])

def rotate_half(value_rows):
    half_width = value_rows.shape[-1] // 2
    return jnp.concatenate([-value_rows[..., half_width:], value_rows[..., :half_width]], axis=-1)

def head_prep(raw_heads, gain_vec, cos_table, sin_table):
    normed = raw_heads * rms_scale(raw_heads) * gain_vec
    return normed * cos_table + rotate_half(normed) * sin_table

def attention(query_rows, key_rows, value_rows, segments):
    token_total_count = query_rows.shape[0]
    tile_rows = min(tile_most, TOK_DEV * N_HEAD)
    tile_count = token_total_count // tile_rows
    slab_rows = tile_rows + ATTENTION_SPAN
    query_cluster = QUERY_HEADS // KEY_VALUE_HEADS
    attn_scale = HEAD_SIZE ** (-0.5)
    key_rows_padded = jnp.concatenate([jnp.zeros((ATTENTION_SPAN, KEY_VALUE_HEADS, HEAD_SIZE), jnp.float32), key_rows], axis=0)
    value_rows_padded = jnp.concatenate([jnp.zeros((ATTENTION_SPAN, KEY_VALUE_HEADS, HEAD_SIZE), jnp.float32), value_rows], axis=0)
    seg_pad = jnp.concatenate([jnp.full((ATTENTION_SPAN,), -1, jnp.int32), segments])
    query_clustered = query_rows.reshape(token_total_count, KEY_VALUE_HEADS, query_cluster, HEAD_SIZE)

    def one_tile(offset):
        q_tile = lax.dynamic_slice_in_dim(query_clustered, offset, tile_rows, 0)
        k_slab = lax.dynamic_slice_in_dim(key_rows_padded, offset, slab_rows, 0)
        v_slab = lax.dynamic_slice_in_dim(value_rows_padded, offset, slab_rows, 0)
        seg_rows = lax.dynamic_slice_in_dim(segments, offset, tile_rows, 0)
        seg_keys = lax.dynamic_slice_in_dim(seg_pad, offset, slab_rows, 0)
        key_gap = jnp.arange(tile_rows, dtype=jnp.int32)[:, None] + ATTENTION_SPAN - jnp.arange(slab_rows, dtype=jnp.int32)[None, :]
        allowed = (key_gap >= 0) & (key_gap < ATTENTION_SPAN) & (seg_rows[:, None] == seg_keys[None, :])
        scores = lower_part_backward(jnp.einsum('qkgd,ckd->kgqc', q_tile, k_slab, precision=highest) * attn_scale)
        scores = jnp.where(allowed[None, None], scores, masked_score)
        row_peak = lax.optimization_barrier(jnp.max(scores, axis=-1, keepdims=True))
        exp_scores = jnp.exp(scores - row_peak)
        attn_probs = lower_part(exp_scores / lax.optimization_barrier(jnp.sum(exp_scores, axis=-1, keepdims=True)))
        tile_out = jnp.einsum('kgqc,ckd->qkgd', attn_probs, v_slab, precision=highest)
        return tile_out.reshape(tile_rows, QUERY_HEADS * HEAD_SIZE)
    offsets = jnp.arange(tile_count, dtype=jnp.int32) * tile_rows
    blocks_out = lax.map(jax.checkpoint(one_tile), offsets)
    return blocks_out.reshape(token_total_count, QUERY_HEADS * HEAD_SIZE)

def layer_forward(x_float, attn_g, w_q, key_weight, value_weight, q_gain, k_gain, w_o, ffn_g, w_g, w_u, w_d, segments):
    token_total_count = x_float.shape[0]
    x_unit = x_float * rms_scale(x_float)
    input_normalized = lower_part(x_unit * attn_g)
    q_raw = lower_part_backward(matrix_product(input_normalized, w_q)).reshape(token_total_count, QUERY_HEADS, HEAD_SIZE)
    key_unrotated = lower_part_backward(matrix_product(input_normalized, key_weight)).reshape(token_total_count, KEY_VALUE_HEADS, HEAD_SIZE)
    value_every = lower_part_backward(lower_part(matrix_product(input_normalized, value_weight))).reshape(token_total_count, KEY_VALUE_HEADS, HEAD_SIZE)
    cos_table, sin_table = rotary_tables(0, token_total_count)
    query_rows = lower_part_backward(lower_part(head_prep(q_raw, q_gain, cos_table, sin_table)))
    key_rows = lower_part_backward(lower_part(head_prep(key_unrotated, k_gain, cos_table, sin_table)))
    attended = lower_part_backward(lower_part(attention(query_rows, key_rows, value_every, segments)))
    mid_sum = x_float + lower_part_backward(matrix_product(attended, w_o))
    mid_unit = mid_sum * rms_scale(mid_sum)
    mid_normed = lower_part(mid_unit * ffn_g)
    gate_val = lower_part_backward(matrix_product(mid_normed, w_g))
    up_val = lower_part_backward(matrix_product(mid_normed, w_u))
    hidden = lower_part(jax.nn.silu(gate_val) * up_val)
    return mid_sum + lower_part_backward(matrix_product(hidden, w_d))

def reference(tokens, cotangent, segments, attn_gain, w_query, key_matrix, value_matrix, query_gain, key_gain, w_out, ffn_gain, w_gate, w_up, w_down):
    floats = tuple((array.astype(jnp.float32) for array in (tokens, attn_gain, w_query, key_matrix, value_matrix, query_gain, key_gain, w_out, ffn_gain, w_gate, w_up, w_down)))

    def forward(*pieces):
        return layer_forward(*pieces, segments)
    result, pull_back = jax.vjp(forward, *floats)
    grad_list = pull_back(cotangent.astype(jnp.float32))
    return (result.astype(jnp.bfloat16), grad_list[0].astype(jnp.bfloat16), grad_list[1], grad_list[2], grad_list[3], grad_list[4], grad_list[5], grad_list[6], grad_list[7], grad_list[8], grad_list[9], grad_list[10], grad_list[11])
```

```python
import functools

import jax
import jax.numpy as jnp
import numpy as np
from jax import lax
from jax.experimental import pallas as pl
from jax.experimental.pallas import tpu as pltpu
from jax.sharding import PartitionSpec as P

HEAD_SIZE = 128
SPAN = 1024
CHUNK = 512
EPS = 1e-06
ROPE_BASE = 1000000.0
MASKED = -1e30
MESH = pl.DeviceIdType.MESH
BF = jnp.bfloat16
F32 = jnp.float32
VMEM = pl.BlockSpec(memory_space=pltpu.VMEM)
HBM = pl.BlockSpec(memory_space=pl.ANY)
DMA = pltpu.SemaphoreType.DMA
VMEM_LIMIT = 58 * 2**20


def coords():
    h = lax.axis_index("head")
    b = lax.axis_index("blk")
    x = 2 * lax.div(h, 4) + lax.div(b, 8)
    return x, lax.rem(h, 4), lax.rem(lax.div(b, 2), 4), lax.rem(b, 2)


def device(x, y, z, c):
    return (lax.div(x, 2) * 4 + y, lax.rem(x, 2) * 8 + z * 2 + c)


def wrap4(v):
    return lax.rem(v + 8, 4)


def send(src, dst, send_sem, recv_sem, to):
    copy = pltpu.make_async_remote_copy(
        src_ref=src, dst_ref=dst, send_sem=send_sem, recv_sem=recv_sem, device_id=to, device_id_type=MESH
    )
    copy.start()
    return copy


def arrived(dst, sem, anyone):
    pltpu.make_async_remote_copy(
        src_ref=dst, dst_ref=dst, send_sem=sem, recv_sem=sem, device_id=anyone, device_id_type=MESH
    ).wait_recv()


def meet(peers):
    barrier = pltpu.get_barrier_semaphore()
    for peer in peers:
        pl.semaphore_signal(barrier, inc=1, device_id=peer, device_id_type=MESH)
    pl.semaphore_wait(barrier, len(peers))


def params(collective_id):
    return pltpu.CompilerParams(
        collective_id=collective_id, has_side_effects=True, vmem_limit_bytes=VMEM_LIMIT
    )


def gather_kernel(
    tok, cot, wq, wk, wv, wg, wu, gains, wo, wd,
    xs, cs, wa, wb, wof, wdf,
    sa, sb, ysend, yrecv, lsem, p1s, p1r, p2s, p2r, cos, cor,
):
    x, y, z, c = coords()
    for r in range(4):
        for g in range(2):
            h = g * 4 + r
            sa[r, :, g * 256 : g * 256 + 256] = wq[:, h * 256 : h * 256 + 256]
            sa[r, :, 512 + g * 128 : 640 + g * 128] = wk[:, h * 128 : h * 128 + 128]
            sa[r, :, 768 + g * 128 : 896 + g * 128] = wv[:, h * 128 : h * 128 + 128]
            sb[r, :, g * 384 : g * 384 + 384] = wg[:, h * 384 : h * 384 + 384]
            sb[r, :, 768 + g * 384 : 1152 + g * 384] = wu[:, h * 384 : h * 384 + 384]
        sa[r, :, 1024:1152] = gains[...]

    d = 1 - c

    def along(j, k):
        return wrap4(x + j * d + k * c), wrap4(z + j * c + k * d)

    def to(j, k):
        px, pz = along(j, k)
        return device(px, y, pz, c)

    across = device(x, y, z, 1 - c)
    ring = [device(x, wrap4(y + k), z, c) for k in range(1, 4)]
    meet(ring + [to(k, 0) for k in range(1, 4)] + [to(0, k) for k in range(1, 4)] + [across])

    def slot(ref, wide, px, pz, core):
        b = lax.rem(px, 2) * 8 + pz * 2 + core
        if wide:
            return ref.at[lax.div(px, 2), :, b]
        return ref.at[lax.div(px, 2), b]

    def piece(n, j, k):
        px, pz = along(-j, -k)
        ref, wide = arrays[n]
        return slot(ref, wide, px, pz, c)

    def piece_across(n, j, k):
        px, pz = wrap4(x - j * c - k * d), wrap4(z - j * d - k * c)
        ref, wide = arrays[n]
        return slot(ref, wide, px, pz, 1 - c)

    arrays = [(wa, True), (wof, False), (wb, True), (wdf, False)]
    sends = []
    locals_ = []
    b = lax.rem(x, 2) * 8 + z * 2 + c
    xh = lax.div(x, 2)

    def keep(src, dst, n):
        copy = pltpu.make_async_copy(src, dst, lsem.at[n])
        copy.start()
        return copy

    def ring_out(n, src_of, dst):
        for k in range(1, 4):
            sends.append(send(src_of(wrap4(y + k)), dst(y), ysend.at[n, k - 1], yrecv.at[n, k - 1], ring[k - 1]))
        return keep(src_of(y), dst(y), n)

    def ring_in(n, dst):
        for k in range(1, 4):
            arrived(dst(wrap4(y - k)), yrecv.at[n, k - 1], ring[0])

    at_a = lambda r: wa.at[xh, r, b]
    at_b = lambda r: wb.at[xh, r, b]
    own_a = ring_out(0, lambda r: sa.at[r], at_a)
    own_x = ring_out(2, lambda r: tok, lambda r: xs.at[r])
    own_b = ring_out(1, lambda r: sb.at[r], at_b)
    own_c = ring_out(3, lambda r: cot, lambda r: cs.at[r])
    own_o = keep(wo, slot(wof, False, x, z, c), 4)
    own_d = keep(wd, slot(wdf, False, x, z, c), 5)

    def own_sends(n, src):
        for k in range(1, 4):
            sends.append(send(src, piece(n, 0, 0), p1s.at[n, k - 1], p1r.at[n, k - 1], to(k, 0)))
        for k in range(1, 4):
            sends.append(send(src, piece(n, 0, 0), p2s.at[n, 0, k - 1], p2r.at[n, 0, k - 1], to(0, k)))
        sends.append(send(src, piece(n, 0, 0), cos.at[n, 0, 0], cor.at[n, 0, 0], across))

    def pass_on(n, j):
        arrived(piece(n, j, 0), p1r.at[n, j - 1], across)
        for k in range(1, 4):
            sends.append(
                send(piece(n, j, 0), piece(n, j, 0), p2s.at[n, j, k - 1], p2r.at[n, j, k - 1], to(0, k))
            )
        sends.append(send(piece(n, j, 0), piece(n, j, 0), cos.at[n, j, 0], cor.at[n, j, 0], across))

    def pass_across(n, j, k):
        arrived(piece(n, j, k), p2r.at[n, j, k - 1], across)
        sends.append(send(piece(n, j, k), piece(n, j, k), cos.at[n, j, k], cor.at[n, j, k], across))

    own_sends(1, wo)
    ring_in(0, at_a)
    own_a.wait()
    own_sends(0, piece(0, 0, 0))
    for j in range(1, 4):
        pass_on(0, j)
        pass_on(1, j)
    own_sends(3, wd)
    ring_in(1, at_b)
    own_b.wait()
    own_sends(2, piece(2, 0, 0))
    for n in (0, 1):
        for j in range(4):
            for k in range(1, 4):
                pass_across(n, j, k)
    for j in range(1, 4):
        pass_on(2, j)
        pass_on(3, j)
    for n in (2, 3):
        for j in range(4):
            for k in range(1, 4):
                pass_across(n, j, k)
    ring_in(2, lambda r: xs.at[r])
    ring_in(3, lambda r: cs.at[r])
    for n in range(4):
        for j in range(4):
            for k in range(4):
                arrived(piece_across(n, j, k), cor.at[n, j, k], across)
    for copy in (own_x, own_c, own_o, own_d):
        copy.wait()
    for copy in sends:
        copy.wait_send()


def gather_all(tok, cot, wq, wk, wv, wg, wu, gains, wo, wd):
    sds = jax.ShapeDtypeStruct
    return pl.pallas_call(
        gather_kernel,
        out_shape=(
            sds((4, 128, 1024), BF),
            sds((4, 128, 1024), BF),
            sds((2, 4, 16, 8, 1152), BF),
            sds((2, 4, 16, 8, 1536), BF),
            sds((2, 16, 16, 1024), BF),
            sds((2, 16, 24, 1024), BF),
        ),
        in_specs=[HBM, HBM] + [VMEM] * 6 + [HBM, HBM],
        out_specs=(HBM,) * 6,
        scratch_shapes=[
            pltpu.VMEM((4, 8, 1152), BF),
            pltpu.VMEM((4, 8, 1536), BF),
            DMA((4, 3)),
            DMA((4, 3)),
            DMA((6,)),
            DMA((4, 3)),
            DMA((4, 3)),
            DMA((4, 4, 3)),
            DMA((4, 4, 3)),
            DMA((4, 4, 4)),
            DMA((4, 4, 4)),
        ],
        compiler_params=params(0),
        name="gather_all",
    )(tok, cot, wq, wk, wv, wg, wu, gains, wo, wd)


def ring_gather_kernel(src, out, ssem, rsem, lsem):
    x, y, z, c = coords()
    ring = [device(x, wrap4(y + k), z, c) for k in range(1, 4)]
    meet(ring)
    copies = [send(src, out.at[y], ssem.at[k], rsem.at[k], ring[k]) for k in range(3)]
    own = pltpu.make_async_copy(src, out.at[y], lsem)
    own.start()
    for k in range(3):
        arrived(out.at[wrap4(y - k - 1)], rsem.at[k], ring[0])
    own.wait()
    for copy in copies:
        copy.wait_send()


def ring_gather(rows, collective_id):
    return pl.pallas_call(
        ring_gather_kernel,
        out_shape=jax.ShapeDtypeStruct((4,) + rows.shape, rows.dtype),
        in_specs=[HBM],
        out_specs=HBM,
        scratch_shapes=[DMA((3,)), DMA((3,)), DMA],
        compiler_params=params(collective_id),
        name="ring_gather",
    )(rows)


def ring_sum_kernel(part, out, land, ssem, rsem):
    x, y, z, c = coords()
    ring = [device(x, wrap4(y + k), z, c) for k in range(1, 4)]
    meet(ring)
    copies = [
        send(part.at[wrap4(y + k + 1)], land.at[k], ssem.at[k], rsem.at[k], ring[k]) for k in range(3)
    ]
    for copy in copies:
        copy.wait()
    total = part[y].astype(F32)
    for k in range(3):
        total = total + land[k].astype(F32)
    out[...] = total


def ring_sum(part, collective_id):
    rows, cols = part.shape[1:]
    return pl.pallas_call(
        ring_sum_kernel,
        out_shape=jax.ShapeDtypeStruct((rows, cols), F32),
        in_specs=[VMEM],
        out_specs=VMEM,
        scratch_shapes=[pltpu.VMEM((3, rows, cols), BF), DMA((3,)), DMA((3,))],
        compiler_params=params(collective_id),
        name="ring_sum",
    )(part)


def chunk_device(step):
    h = lax.axis_index("head")
    chunk = lax.rem(2 * lax.axis_index("blk") + lax.div(h, 4) + step + 32, 32)
    return (lax.rem(chunk, 2) * 4 + lax.rem(h, 4), lax.div(chunk, 2))


def halo_kernel(kv, out, ssem, rsem, lsem):
    meet([chunk_device(s) for s in (-2, -1, 1, 2)])
    far = send(kv, out.at[0], ssem.at[0], rsem.at[0], chunk_device(2))
    near = send(kv, out.at[1], ssem.at[1], rsem.at[1], chunk_device(1))
    own = pltpu.make_async_copy(kv, out.at[2], lsem)
    own.start()
    far.wait()
    near.wait()
    own.wait()


def halo(kv, collective_id):
    return pl.pallas_call(
        halo_kernel,
        out_shape=jax.ShapeDtypeStruct((3,) + kv.shape, kv.dtype),
        in_specs=[HBM],
        out_specs=HBM,
        scratch_shapes=[DMA((2,)), DMA((2,)), DMA],
        compiler_params=params(collective_id),
        name="halo",
    )(kv)


def halo_back_kernel(dkv, out, land, ssem, rsem):
    meet([chunk_device(s) for s in (-2, -1, 1, 2)])
    far = send(dkv.at[0], land.at[0], ssem.at[0], rsem.at[0], chunk_device(-2))
    near = send(dkv.at[1], land.at[1], ssem.at[1], rsem.at[1], chunk_device(-1))
    far.wait()
    near.wait()
    out[...] = dkv[2].astype(F32) + land[0].astype(F32) + land[1].astype(F32)


def halo_back(dkv, collective_id):
    return pl.pallas_call(
        halo_back_kernel,
        out_shape=jax.ShapeDtypeStruct(dkv.shape[1:], F32),
        in_specs=[VMEM],
        out_specs=VMEM,
        scratch_shapes=[pltpu.VMEM((2,) + dkv.shape[1:], BF), DMA((2,)), DMA((2,))],
        compiler_params=params(collective_id),
        name="halo_back",
    )(dkv)


GRADS = ((8, 1152, 4), (8, 1536, 4), (16, 1024, 1), (24, 1024, 1))


def grads_kernel(ga, gb, go, gd, oq, ok, ov, og, ou, oo, od, ogain, *scratch):
    n_arr = len(GRADS)
    rc, lc, sa, lb, sb, l2, sd, ry = [scratch[i * n_arr : (i + 1) * n_arr] for i in range(8)]
    csem, crec, lsem, p2s, p2r, p1s, p1r, ys, yr = scratch[8 * n_arr :]
    x, y, z, c = coords()
    d = 1 - c

    def to(j, k):
        return device(wrap4(x + j * d + k * c), y, wrap4(z + j * c + k * d), c)

    across = device(x, y, z, 1 - c)
    ring = [device(x, wrap4(y + k), z, c) for k in range(1, 4)]
    meet(ring + [to(k, 0) for k in range(1, 4)] + [to(0, k) for k in range(1, 4)] + [across])
    p1 = x * d + z * c
    p2 = x * c + z * d
    ins = (ga, gb, go, gd)
    over, kept = [], []
    for n in range(n_arr):
        over.append(send(ins[n].at[:, 1 - c], rc[n], csem.at[n], crec.at[n], across))
        own = pltpu.make_async_copy(ins[n].at[:, c], lc[n], lsem.at[n])
        own.start()
        kept.append(own)

    first, second, third = [], [], []
    for n, (rows, cols, cut) in enumerate(GRADS):
        over[n].wait_recv()
        kept[n].wait()

        def add_cores(i, _, n=n, cut=cut):
            a2, a1, r = lax.div(i, 4 * cut), lax.rem(lax.div(i, cut), 4), lax.rem(i, cut)
            px, pz = a1 * d + a2 * c, a1 * c + a2 * d
            at = ((lax.div(px, 2) * cut + r) * 2 + lax.rem(px, 2)) * 4 + pz
            sa[n][a2, a1, r] = (rc[n][at].astype(F32) + lc[n][at].astype(F32)).astype(BF)
            return 0

        lax.fori_loop(0, 16 * cut, add_cores, 0)
        for k in range(1, 4):
            first.append(
                send(sa[n].at[wrap4(p2 + k)], lb[n].at[k - 1], p2s.at[n, k - 1], p2r.at[n, k - 1], to(0, k))
            )
    for n, (rows, cols, cut) in enumerate(GRADS):
        for k in range(3):
            first[3 * n + k].wait_recv()

        def add_second(i, _, n=n, cut=cut):
            a1, r = lax.div(i, cut), lax.rem(i, cut)
            total = sa[n][p2, a1, r].astype(F32)
            for k in range(3):
                total = total + lb[n][k, a1, r].astype(F32)
            sb[n][a1, r] = total.astype(BF)
            return 0

        lax.fori_loop(0, 4 * cut, add_second, 0)
        for k in range(1, 4):
            second.append(
                send(sb[n].at[wrap4(p1 + k)], l2[n].at[k - 1], p1s.at[n, k - 1], p1r.at[n, k - 1], to(k, 0))
            )
    for n, (rows, cols, cut) in enumerate(GRADS):
        for k in range(3):
            second[3 * n + k].wait_recv()
        for r in range(cut):
            total = sb[n][p1, r].astype(F32)
            for k in range(3):
                total = total + l2[n][k, r].astype(F32)
            if cut == 1:
                (oo if n == 2 else od)[...] = total
            else:
                sd[n][r] = total.astype(BF)
        if cut > 1:
            for k in range(1, 4):
                third.append(
                    send(sd[n].at[wrap4(y + k)], ry[n].at[y], ys.at[n, k - 1], yr.at[n, k - 1], ring[k - 1])
                )
            ry[n][y] = sd[n][y]
    for copy in third:
        copy.wait_recv()
    gain = jnp.zeros((8, 128), F32)
    for r in range(4):
        for g in range(2):
            h = g * 4 + r
            oq[:, h * 256 : h * 256 + 256] = ry[0][r, :, g * 256 : g * 256 + 256].astype(F32)
            ok[:, h * 128 : h * 128 + 128] = ry[0][r, :, 512 + g * 128 : 640 + g * 128].astype(F32)
            ov[:, h * 128 : h * 128 + 128] = ry[0][r, :, 768 + g * 128 : 896 + g * 128].astype(F32)
            og[:, h * 384 : h * 384 + 384] = ry[1][r, :, g * 384 : g * 384 + 384].astype(F32)
            ou[:, h * 384 : h * 384 + 384] = ry[1][r, :, 768 + g * 384 : 1152 + g * 384].astype(F32)
        gain = gain + ry[0][r, :, 1024:1152].astype(F32)
    ogain[...] = gain
    for copy in over + first + second + third:
        copy.wait_send()


def grads_out(ga, gb, go, gd):
    sds = jax.ShapeDtypeStruct
    scratch = []
    for lead in (
        lambda cut: (16 * cut,),
        lambda cut: (16 * cut,),
        lambda cut: (4, 4, cut),
        lambda cut: (3, 4, cut),
        lambda cut: (4, cut),
        lambda cut: (3, cut),
        lambda cut: (cut,),
        lambda cut: (cut,),
    ):
        for rows, cols, cut in GRADS:
            scratch.append(pltpu.VMEM(lead(cut) + (rows, cols), BF))
    n = len(GRADS)
    scratch += [DMA((n,)), DMA((n,)), DMA((n,))] + [DMA((n, 3))] * 6
    return pl.pallas_call(
        grads_kernel,
        out_shape=(
            sds((8, 2048), F32),
            sds((8, 1024), F32),
            sds((8, 1024), F32),
            sds((8, 3072), F32),
            sds((8, 3072), F32),
            sds((16, 1024), F32),
            sds((24, 1024), F32),
            sds((8, 128), F32),
        ),
        in_specs=[HBM] * 4,
        out_specs=(VMEM,) * 8,
        scratch_shapes=scratch,
        compiler_params=params(1),
        name="grads_out",
    )(ga, gb, go, gd)


def rms_scale(rows):
    return lax.rsqrt(jnp.mean(rows * rows, axis=-1, keepdims=True) + EPS)


def norm_back(d_normed, unit, scale, gain):
    d_unit = d_normed * gain
    return scale * (d_unit - unit * jnp.mean(d_unit * unit, axis=-1, keepdims=True))


def rope_tables():
    freq = ROPE_BASE ** (-np.arange(0, HEAD_SIZE, 2, dtype=np.float64) / HEAD_SIZE)
    freq = np.concatenate([freq, freq])
    inner = np.arange(CHUNK)[:, None] * freq[None, :]
    outer = (np.arange(32) * CHUNK)[:, None] * freq[None, :]
    return [f(a).astype(np.float32) for a in (inner, outer) for f in (np.cos, np.sin)]


def rotate_half(rows):
    half = rows.shape[-1] // 2
    return jnp.concatenate([-rows[..., half:], rows[..., :half]], axis=-1)


def head_prep(raw, gain, cos, sin):
    normed = raw * rms_scale(raw) * gain
    return normed * cos + rotate_half(normed) * sin


def dot(a, b, ca, cb):
    return lax.dot_general(a, b, (((ca,), (cb,)), ((), ())), preferred_element_type=F32)


def local(
    tokens, cotangent, segments, attn_gain, w_query, key_matrix, value_matrix, query_gain, key_gain,
    w_out, ffn_gain, w_gate, w_up, w_down,
):
    y = lax.rem(lax.axis_index("head"), 4)
    chunk = 2 * lax.axis_index("blk") + lax.div(lax.axis_index("head"), 4)
    own_gains = jnp.concatenate(
        [
            attn_gain[:, None],
            ffn_gain[:, None],
            jnp.broadcast_to(query_gain[None, :], (8, 1)),
            jnp.broadcast_to(key_gain[None, :], (8, 1)),
            jnp.zeros((8, 124), BF),
        ],
        axis=1,
    )
    xs, cs, wa, wb, wo, wd = gather_all(
        tokens, cotangent, w_query, key_matrix, value_matrix, w_gate, w_up, own_gains, w_out, w_down
    )
    wa = wa.reshape(1024, 1152)
    wb = wb.reshape(1024, 1536)
    wo = wo.reshape(512, 1024)
    wd = wd.reshape(768, 1024)
    cot = cs.reshape(CHUNK, 1024)
    gains = wa[:, 1024:1028].astype(F32)
    attn_g, ffn_g = gains[:, 0], gains[:, 1]
    q_gain, k_gain = gains[::8, 2], gains[::8, 3]

    x = xs.reshape(CHUNK, 1024).astype(F32)
    scale_one = rms_scale(x)
    x_normed = (x * scale_one * attn_g).astype(BF)
    raw = dot(x_normed, wa[:, :1024], 1, 0)
    q_raw = raw[:, :512].reshape(CHUNK, 4, HEAD_SIZE)
    k_raw = raw[:, 512:768].reshape(CHUNK, 2, HEAD_SIZE)
    v = raw[:, 768:1024].astype(BF)
    in_cos, in_sin, out_cos, out_sin = rope_tables()
    c0 = lax.dynamic_slice_in_dim(jnp.asarray(out_cos), chunk, 1, 0)
    s0 = lax.dynamic_slice_in_dim(jnp.asarray(out_sin), chunk, 1, 0)
    cos = (c0 * in_cos - s0 * in_sin)[:, None, :]
    sin = (s0 * in_cos + c0 * in_sin)[:, None, :]

    def prep(q, k, qg, kg):
        return head_prep(q, qg, cos, sin), head_prep(k, kg, cos, sin)

    (q_rot, k_rot), prep_back = jax.vjp(prep, q_raw, k_raw, q_gain, k_gain)
    q = q_rot.astype(BF)
    k = k_rot.astype(BF).reshape(CHUNK, 256)
    kv = halo(jnp.concatenate([k, v], axis=1), 2).reshape(3 * CHUNK, 512)
    k_ext = kv[:, :256].reshape(3 * CHUNK, 2, HEAD_SIZE)
    v_ext = kv[:, 256:].reshape(3 * CHUNK, 2, HEAD_SIZE)
    q4 = q.reshape(CHUNK, 2, 2, HEAD_SIZE)

    padded = jnp.concatenate([jnp.full((2 * CHUNK,), -1, jnp.int32), segments])
    seg_keys = lax.dynamic_slice_in_dim(padded, chunk * CHUNK, 3 * CHUNK, 0)
    seg_rows = seg_keys[2 * CHUNK :]
    begins = jnp.sum((seg_keys[None, :] < seg_rows[:, None]).astype(jnp.int32), axis=1)
    row = jnp.arange(CHUNK, dtype=jnp.int32)
    low = jnp.maximum(begins, row + 1)
    column = jnp.arange(3 * CHUNK, dtype=jnp.int32)[None, :]
    allowed = (column >= low[:, None]) & (column <= row[:, None] + SPAN)
    attn_scale = HEAD_SIZE ** (-0.5)
    scores = jnp.einsum("qkgd,ckd->kgqc", q4, k_ext, preferred_element_type=F32) * attn_scale
    scores = jnp.where(allowed[None, None], scores, MASKED)
    peak = jnp.max(scores, axis=-1, keepdims=True)
    weight = jnp.exp(scores - peak)
    total = jnp.sum(weight, axis=-1, keepdims=True)
    soft = weight / total
    probs = soft.astype(BF)
    attended = jnp.einsum("kgqc,ckd->qkgd", probs, v_ext, preferred_element_type=F32)
    attended = attended.astype(BF).reshape(CHUNK, 512)

    part = dot(attended, wo, 1, 0).astype(BF).reshape(4, 128, 1024)
    x_own = tokens.astype(F32)
    mid_sum = x_own + ring_sum(part, 3)
    scale_two = rms_scale(mid_sum)
    mid_unit = mid_sum * scale_two
    mid = ring_gather((mid_unit * ffn_g).astype(BF), 4).reshape(CHUNK, 1024)
    gate_up = dot(mid, wb, 1, 0)
    gate, up = gate_up[:, :768], gate_up[:, 768:]
    sig = jax.nn.sigmoid(gate)
    act = gate * sig
    hidden = (act * up).astype(BF)
    out_part = dot(hidden, wd, 1, 0).astype(BF).reshape(4, 128, 1024)
    output = (mid_sum + ring_sum(out_part, 5)).astype(BF)
    d_hidden = dot(cot, wd, 1, 1)
    d_gate = (d_hidden * up * sig * (1.0 + gate * (1.0 - sig))).astype(BF)
    d_up = (d_hidden * act).astype(BF)
    d_gu = jnp.concatenate([d_gate, d_up], axis=1)
    d_mid_normed = ring_sum(dot(d_gu, wb, 1, 1).astype(BF).reshape(4, 128, 1024), 6)
    d_mid = cotangent.astype(F32) + norm_back(d_mid_normed, mid_unit, scale_two, ffn_g)
    d_branch = ring_gather(d_mid.astype(BF), 7).reshape(CHUNK, 1024)
    d_att = dot(d_branch, wo, 1, 1).astype(BF)
    d4 = d_att.reshape(CHUNK, 2, 2, HEAD_SIZE)

    d_v = jnp.einsum("kgqc,qkgd->ckd", probs, d4, preferred_element_type=F32)
    d_probs = jnp.einsum("qkgd,ckd->kgqc", d4, v_ext, preferred_element_type=F32)
    inner = jnp.sum(soft * d_probs, axis=-1, keepdims=True)
    d_scores = (soft * (d_probs - inner)).astype(BF)
    d_q = jnp.einsum("kgqc,ckd->qkgd", d_scores, k_ext, preferred_element_type=F32) * attn_scale
    d_k = jnp.einsum("kgqc,qkgd->ckd", d_scores, q4, preferred_element_type=F32) * attn_scale
    d_kv = jnp.concatenate([d_k.reshape(3 * CHUNK, 256), d_v.reshape(3 * CHUNK, 256)], axis=1)
    d_kv = halo_back(d_kv.astype(BF).reshape(3, CHUNK, 512), 8)
    d_kv = d_kv.astype(BF)
    d_q_raw, d_k_raw, g_qg, g_kg = prep_back(
        (
            d_q.astype(BF).astype(F32).reshape(CHUNK, 4, HEAD_SIZE),
            d_kv[:, :256].astype(F32).reshape(CHUNK, 2, HEAD_SIZE),
        )
    )
    d_qkv = jnp.concatenate(
        [
            d_q_raw.astype(BF).reshape(CHUNK, 512),
            d_k_raw.astype(BF).reshape(CHUNK, 256),
            d_kv[:, 256:],
        ],
        axis=1,
    )
    d_x_normed = ring_sum(dot(d_qkv, wa[:, :1024], 1, 1).astype(BF).reshape(4, 128, 1024), 9)
    scale_own = rms_scale(x_own)
    unit_own = x_own * scale_own
    input_grad = (d_mid + norm_back(d_x_normed, unit_own, scale_own, attn_g)).astype(BF)

    g_attn = jnp.sum(d_x_normed * unit_own, axis=0)
    g_ffn = jnp.sum(d_mid_normed * mid_unit, axis=0)
    g_gains = jnp.concatenate(
        [
            g_attn[:, None],
            g_ffn[:, None],
            jnp.repeat(g_qg, 8)[:, None],
            jnp.repeat(g_kg, 8)[:, None],
            jnp.zeros((1024, 124), F32),
        ],
        axis=1,
    ).astype(BF)
    ga = jnp.concatenate([dot(x_normed, d_qkv, 0, 0).astype(BF), g_gains], axis=1)
    gb = dot(mid, d_gu, 0, 0).astype(BF)
    go = dot(attended, d_branch, 0, 0).astype(BF)
    gd = dot(hidden, cot, 0, 0).astype(BF)
    oq, ok, ov, og, ou, oo, od, ogain = grads_out(
        ga.reshape(64, 2, 8, 1152),
        gb.reshape(64, 2, 8, 1536),
        go.reshape(16, 2, 16, 1024),
        gd.reshape(16, 2, 24, 1024),
    )
    return (
        output,
        input_grad,
        ogain[:, 0],
        oq,
        ok,
        ov,
        ogain[0, 2:3],
        ogain[0, 3:4],
        oo,
        ogain[:, 1],
        og,
        ou,
        od,
    )


def solution(mesh):
    rows = P(("blk", "head"), None)
    cut = P(("head", "blk"), None)
    vec = P(("head", "blk"))
    return jax.shard_map(
        local,
        mesh=mesh,
        in_specs=(rows, rows, P(), vec, cut, cut, cut, vec, vec, cut, vec, cut, cut, cut),
        out_specs=(rows, rows, vec, cut, cut, cut, vec, vec, cut, vec, cut, cut, cut),
        check_vma=False,
    )
```

```python
import functools

import jax
import jax.numpy as jnp
import numpy as np
from jax import lax
from jax.experimental import pallas as pl
from jax.experimental.pallas import tpu as pltpu
from jax.sharding import PartitionSpec as P

HEAD_SIZE = 128
SPAN = 1024
CHUNK = 512
EPS = 1e-06
ROPE_BASE = 1000000.0
MASKED = -1e30
MESH = pl.DeviceIdType.MESH
BF = jnp.bfloat16
F32 = jnp.float32
VMEM = pl.BlockSpec(memory_space=pltpu.VMEM)
HBM = pl.BlockSpec(memory_space=pl.ANY)
DMA = pltpu.SemaphoreType.DMA
VMEM_LIMIT = 58 * 2**20


def coords():
    h = lax.axis_index("head")
    b = lax.axis_index("blk")
    x = 2 * lax.div(h, 4) + lax.div(b, 8)
    return x, lax.rem(h, 4), lax.rem(lax.div(b, 2), 4), lax.rem(b, 2)


def device(x, y, z, c):
    return (lax.div(x, 2) * 4 + y, lax.rem(x, 2) * 8 + z * 2 + c)


def wrap4(v):
    return lax.rem(v + 8, 4)


def send(src, dst, send_sem, recv_sem, to):
    copy = pltpu.make_async_remote_copy(
        src_ref=src, dst_ref=dst, send_sem=send_sem, recv_sem=recv_sem, device_id=to, device_id_type=MESH
    )
    copy.start()
    return copy


def arrived(dst, sem, anyone):
    pltpu.make_async_remote_copy(
        src_ref=dst, dst_ref=dst, send_sem=sem, recv_sem=sem, device_id=anyone, device_id_type=MESH
    ).wait_recv()


def meet(peers):
    barrier = pltpu.get_barrier_semaphore()
    for peer in peers:
        pl.semaphore_signal(barrier, inc=1, device_id=peer, device_id_type=MESH)
    pl.semaphore_wait(barrier, len(peers))


def params(collective_id):
    return pltpu.CompilerParams(
        collective_id=collective_id, has_side_effects=True, vmem_limit_bytes=VMEM_LIMIT
    )


def gather_kernel(
    tok, cot, wq, wk, wv, wg, wu, gains, wo, wd,
    xs, cs, wa, wb, wof, wdf,
    sa, sb, ysend, yrecv, lsem, p1s, p1r, p2s, p2r, cos, cor,
):
    x, y, z, c = coords()
    for r in range(4):
        for g in range(2):
            h = g * 4 + r
            sa[r, :, g * 256 : g * 256 + 256] = wq[:, h * 256 : h * 256 + 256]
            sa[r, :, 512 + g * 128 : 640 + g * 128] = wk[:, h * 128 : h * 128 + 128]
            sa[r, :, 768 + g * 128 : 896 + g * 128] = wv[:, h * 128 : h * 128 + 128]
            sb[r, :, g * 384 : g * 384 + 384] = wg[:, h * 384 : h * 384 + 384]
            sb[r, :, 768 + g * 384 : 1152 + g * 384] = wu[:, h * 384 : h * 384 + 384]
        sa[r, :, 1024:1152] = gains[...]

    d = 1 - c

    def along(j, k):
        return wrap4(x + j * d + k * c), wrap4(z + j * c + k * d)

    def to(j, k):
        px, pz = along(j, k)
        return device(px, y, pz, c)

    across = device(x, y, z, 1 - c)
    ring = [device(x, wrap4(y + k), z, c) for k in range(1, 4)]
    meet(ring + [to(k, 0) for k in range(1, 4)] + [to(0, k) for k in range(1, 4)] + [across])

    def slot(ref, wide, px, pz, core):
        b = lax.rem(px, 2) * 8 + pz * 2 + core
        if wide:
            return ref.at[lax.div(px, 2), :, b]
        return ref.at[lax.div(px, 2), b]

    def piece(n, j, k):
        px, pz = along(-j, -k)
        ref, wide = arrays[n]
        return slot(ref, wide, px, pz, c)

    def piece_across(n, j, k):
        px, pz = wrap4(x - j * c - k * d), wrap4(z - j * d - k * c)
        ref, wide = arrays[n]
        return slot(ref, wide, px, pz, 1 - c)

    arrays = [(wa, True), (wof, False), (wb, True), (wdf, False)]
    sends = []
    locals_ = []
    b = lax.rem(x, 2) * 8 + z * 2 + c
    xh = lax.div(x, 2)

    def keep(src, dst, n):
        copy = pltpu.make_async_copy(src, dst, lsem.at[n])
        copy.start()
        return copy

    def ring_out(n, src_of, dst):
        for k in range(1, 4):
            sends.append(send(src_of(wrap4(y + k)), dst(y), ysend.at[n, k - 1], yrecv.at[n, k - 1], ring[k - 1]))
        return keep(src_of(y), dst(y), n)

    def ring_in(n, dst):
        for k in range(1, 4):
            arrived(dst(wrap4(y - k)), yrecv.at[n, k - 1], ring[0])

    at_a = lambda r: wa.at[xh, r, b]
    at_b = lambda r: wb.at[xh, r, b]
    own_a = ring_out(0, lambda r: sa.at[r], at_a)
    own_x = ring_out(2, lambda r: tok, lambda r: xs.at[r])
    own_b = ring_out(1, lambda r: sb.at[r], at_b)
    own_c = ring_out(3, lambda r: cot, lambda r: cs.at[r])
    own_o = keep(wo, slot(wof, False, x, z, c), 4)
    own_d = keep(wd, slot(wdf, False, x, z, c), 5)

    def own_sends(n, src):
        for k in range(1, 4):
            sends.append(send(src, piece(n, 0, 0), p1s.at[n, k - 1], p1r.at[n, k - 1], to(k, 0)))
        for k in range(1, 4):
            sends.append(send(src, piece(n, 0, 0), p2s.at[n, 0, k - 1], p2r.at[n, 0, k - 1], to(0, k)))
        sends.append(send(src, piece(n, 0, 0), cos.at[n, 0, 0], cor.at[n, 0, 0], across))

    def pass_on(n, j):
        arrived(piece(n, j, 0), p1r.at[n, j - 1], across)
        for k in range(1, 4):
            sends.append(
                send(piece(n, j, 0), piece(n, j, 0), p2s.at[n, j, k - 1], p2r.at[n, j, k - 1], to(0, k))
            )
        sends.append(send(piece(n, j, 0), piece(n, j, 0), cos.at[n, j, 0], cor.at[n, j, 0], across))

    def pass_across(n, j, k):
        arrived(piece(n, j, k), p2r.at[n, j, k - 1], across)
        sends.append(send(piece(n, j, k), piece(n, j, k), cos.at[n, j, k], cor.at[n, j, k], across))

    own_sends(1, wo)
    ring_in(0, at_a)
    own_a.wait()
    own_sends(0, piece(0, 0, 0))
    for j in range(1, 4):
        pass_on(0, j)
        pass_on(1, j)
    own_sends(3, wd)
    ring_in(1, at_b)
    own_b.wait()
    own_sends(2, piece(2, 0, 0))
    for n in (0, 1):
        for j in range(4):
            for k in range(1, 4):
                pass_across(n, j, k)
    for j in range(1, 4):
        pass_on(2, j)
        pass_on(3, j)
    for n in (2, 3):
        for j in range(4):
            for k in range(1, 4):
                pass_across(n, j, k)
    ring_in(2, lambda r: xs.at[r])
    ring_in(3, lambda r: cs.at[r])
    for n in range(4):
        for j in range(4):
            for k in range(4):
                arrived(piece_across(n, j, k), cor.at[n, j, k], across)
    for copy in (own_x, own_c, own_o, own_d):
        copy.wait()
    for copy in sends:
        copy.wait_send()


def gather_all(tok, cot, wq, wk, wv, wg, wu, gains, wo, wd):
    sds = jax.ShapeDtypeStruct
    return pl.pallas_call(
        gather_kernel,
        out_shape=(
            sds((4, 128, 1024), BF),
            sds((4, 128, 1024), BF),
            sds((2, 4, 16, 8, 1152), BF),
            sds((2, 4, 16, 8, 1536), BF),
            sds((2, 16, 16, 1024), BF),
            sds((2, 16, 24, 1024), BF),
        ),
        in_specs=[HBM, HBM] + [VMEM] * 6 + [HBM, HBM],
        out_specs=(HBM,) * 6,
        scratch_shapes=[
            pltpu.VMEM((4, 8, 1152), BF),
            pltpu.VMEM((4, 8, 1536), BF),
            DMA((4, 3)),
            DMA((4, 3)),
            DMA((6,)),
            DMA((4, 3)),
            DMA((4, 3)),
            DMA((4, 4, 3)),
            DMA((4, 4, 3)),
            DMA((4, 4, 4)),
            DMA((4, 4, 4)),
        ],
        compiler_params=params(0),
        name="gather_all",
    )(tok, cot, wq, wk, wv, wg, wu, gains, wo, wd)


def ring_sum_kernel(part, out, land, ssem, rsem):
    x, y, z, c = coords()
    ring = [device(x, wrap4(y + k), z, c) for k in range(1, 4)]
    meet(ring)
    copies = [
        send(part.at[wrap4(y + k + 1)], land.at[k], ssem.at[k], rsem.at[k], ring[k]) for k in range(3)
    ]
    for copy in copies:
        copy.wait()
    total = part[y].astype(F32)
    for k in range(3):
        total = total + land[k].astype(F32)
    out[...] = total


def ring_sum(part, collective_id):
    rows, cols = part.shape[1:]
    return pl.pallas_call(
        ring_sum_kernel,
        out_shape=jax.ShapeDtypeStruct((rows, cols), F32),
        in_specs=[VMEM],
        out_specs=VMEM,
        scratch_shapes=[pltpu.VMEM((3, rows, cols), BF), DMA((3,)), DMA((3,))],
        compiler_params=params(collective_id),
        name="ring_sum",
    )(part)


def chunk_device(step):
    h = lax.axis_index("head")
    chunk = lax.rem(2 * lax.axis_index("blk") + lax.div(h, 4) + step + 32, 32)
    return (lax.rem(chunk, 2) * 4 + lax.rem(h, 4), lax.div(chunk, 2))


def halo_kernel(kv, out, ssem, rsem, lsem):
    meet([chunk_device(s) for s in (-2, -1, 1, 2)])
    far = send(kv, out.at[0], ssem.at[0], rsem.at[0], chunk_device(2))
    near = send(kv, out.at[1], ssem.at[1], rsem.at[1], chunk_device(1))
    own = pltpu.make_async_copy(kv, out.at[2], lsem)
    own.start()
    far.wait()
    near.wait()
    own.wait()


def halo(kv, collective_id):
    return pl.pallas_call(
        halo_kernel,
        out_shape=jax.ShapeDtypeStruct((3,) + kv.shape, kv.dtype),
        in_specs=[HBM],
        out_specs=HBM,
        scratch_shapes=[DMA((2,)), DMA((2,)), DMA],
        compiler_params=params(collective_id),
        name="halo",
    )(kv)


def halo_back_kernel(dkv, out, land, ssem, rsem):
    meet([chunk_device(s) for s in (-2, -1, 1, 2)])
    far = send(dkv.at[0], land.at[0], ssem.at[0], rsem.at[0], chunk_device(-2))
    near = send(dkv.at[1], land.at[1], ssem.at[1], rsem.at[1], chunk_device(-1))
    far.wait()
    near.wait()
    out[...] = dkv[2].astype(F32) + land[0].astype(F32) + land[1].astype(F32)


def halo_back(dkv, collective_id):
    return pl.pallas_call(
        halo_back_kernel,
        out_shape=jax.ShapeDtypeStruct(dkv.shape[1:], F32),
        in_specs=[VMEM],
        out_specs=VMEM,
        scratch_shapes=[pltpu.VMEM((2,) + dkv.shape[1:], BF), DMA((2,)), DMA((2,))],
        compiler_params=params(collective_id),
        name="halo_back",
    )(dkv)


class Sums:
    def __init__(self, grad, rows, cols, cut, refs):
        self.grad, self.rows, self.cols, self.cut = grad, rows, cols, cut
        (self.rc, self.sa, self.lb, self.sb, self.l2, self.sd, self.ry, self.ss, self.rs) = refs
        x, y, z, c = coords()
        self.y, self.c, self.d = y, c, 1 - c
        d = self.d
        self.across = device(x, y, z, d)
        self.ring = [device(x, wrap4(y + k), z, c) for k in range(1, 4)]
        self.to_first = [device(wrap4(x + k * d), y, wrap4(z + k * c), c) for k in range(1, 4)]
        self.to_second = [device(wrap4(x + k * c), y, wrap4(z + k * d), c) for k in range(1, 4)]
        self.p1 = x * d + z * c
        self.p2 = x * c + z * d
        self.sends = []

    @staticmethod
    def scratch(rows, cols, cut):
        buffers = [(16 * cut,), (4, 4, cut), (3, 4, cut), (4, cut), (3, cut), (cut,), (cut,)]
        return [pltpu.VMEM(lead + (rows, cols), BF) for lead in buffers] + [DMA((10,)), DMA((10,))]

    def start(self):
        self.over = send(self.grad.at[:, self.d], self.rc, self.ss.at[9], self.rs.at[9], self.across)
        self.sends.append(self.over)

    def cores(self):
        self.over.wait_recv()
        c, d, cut = self.c, self.d, self.cut

        def add(i, _):
            a2, a1, r = lax.div(i, 4 * cut), lax.rem(lax.div(i, cut), 4), lax.rem(i, cut)
            px, pz = a1 * d + a2 * c, a1 * c + a2 * d
            at = ((lax.div(px, 2) * cut + r) * 2 + lax.rem(px, 2)) * 4 + pz
            self.sa[a2, a1, r] = (self.rc[at].astype(F32) + self.grad[at, c].astype(F32)).astype(BF)
            return 0

        lax.fori_loop(0, 16 * cut, add, 0)
        self.hop = [
            send(self.sa.at[wrap4(self.p2 + k + 1)], self.lb.at[k], self.ss.at[k], self.rs.at[k], self.to_second[k])
            for k in range(3)
        ]
        self.sends += self.hop

    def second(self):
        for copy in self.hop:
            copy.wait_recv()

        def add(i, _):
            a1, r = lax.div(i, self.cut), lax.rem(i, self.cut)
            total = self.sa[self.p2, a1, r].astype(F32)
            for k in range(3):
                total = total + self.lb[k, a1, r].astype(F32)
            self.sb[a1, r] = total.astype(BF)
            return 0

        lax.fori_loop(0, 4 * self.cut, add, 0)
        self.hop = [
            send(self.sb.at[wrap4(self.p1 + k + 1)], self.l2.at[k], self.ss.at[3 + k], self.rs.at[3 + k], self.to_first[k])
            for k in range(3)
        ]
        self.sends += self.hop

    def first(self, out=None):
        for copy in self.hop:
            copy.wait_recv()
        for r in range(self.cut):
            total = self.sb[self.p1, r].astype(F32)
            for k in range(3):
                total = total + self.l2[k, r].astype(F32)
            if out is not None:
                out[...] = total
            else:
                self.sd[r] = total.astype(BF)
        if out is None:
            y = self.y
            self.hop = [
                send(self.sd.at[wrap4(y + k + 1)], self.ry.at[y], self.ss.at[6 + k], self.rs.at[6 + k], self.ring[k])
                for k in range(3)
            ]
            self.sends += self.hop
            self.ry[y] = self.sd[y]

    def owners(self):
        for copy in self.hop:
            copy.wait_recv()

    def done(self):
        for copy in self.sends:
            copy.wait_send()


def greet_all():
    x, y, z, c = coords()
    peers = [device(x, wrap4(y + k), z, c) for k in range(1, 4)]
    peers += [device(wrap4(x + k), y, z, c) for k in range(1, 4)]
    peers += [device(x, y, wrap4(z + k), c) for k in range(1, 4)]
    meet(peers + [device(x, y, z, 1 - c)])


def grads_kernel(ga, go, oq, ok, ov, oo, ogain, *scratch):
    a = Sums(ga, 8, 1152, 4, scratch[:9])
    o = Sums(go, 16, 1024, 1, scratch[9:18])
    greet_all()
    for s in (a, o):
        s.start()
    for s in (a, o):
        s.cores()
    for s in (a, o):
        s.second()
    a.first()
    o.first(oo)
    a.owners()
    gain = jnp.zeros((8, 128), F32)
    for r in range(4):
        for g in range(2):
            h = g * 4 + r
            oq[:, h * 256 : h * 256 + 256] = a.ry[r, :, g * 256 : g * 256 + 256].astype(F32)
            ok[:, h * 128 : h * 128 + 128] = a.ry[r, :, 512 + g * 128 : 640 + g * 128].astype(F32)
            ov[:, h * 128 : h * 128 + 128] = a.ry[r, :, 768 + g * 128 : 896 + g * 128].astype(F32)
        gain = gain + a.ry[r, :, 1024:1152].astype(F32)
    ogain[...] = gain
    a.done()
    o.done()


def grads_out(ga, go):
    sds = jax.ShapeDtypeStruct
    return pl.pallas_call(
        grads_kernel,
        out_shape=(
            sds((8, 2048), F32),
            sds((8, 1024), F32),
            sds((8, 1024), F32),
            sds((16, 1024), F32),
            sds((8, 128), F32),
        ),
        in_specs=[VMEM] * 2,
        out_specs=(VMEM,) * 5,
        scratch_shapes=Sums.scratch(8, 1152, 4) + Sums.scratch(16, 1024, 1),
        compiler_params=params(1),
        name="grads_out",
    )(ga, go)


def middle_kernel(
    att, tok, cot, wo, wb, wd, gain,
    out, dmid, datt, gffn, go, og, ou, od,
    part, land1, acc, unit, mid, dhid, dgu, hid, dpart, land2, dbr, opart, land3, gbs, gds, ssem, rsem,
    *scratch,
):
    x, y, z, c = coords()
    ring = [device(x, wrap4(y + k), z, c) for k in range(1, 4)]
    sb = Sums(gbs, 8, 1536, 4, scratch[:9])
    sd = Sums(gds, 24, 1024, 1, scratch[9:18])
    greet_all()
    sends = []

    def ring_send(n, k, src, dst):
        sends.append(send(src, dst, ssem.at[n, k - 1], rsem.at[n, k - 1], ring[k - 1]))

    def ring_wait(n, k, dst):
        arrived(dst, rsem.at[n, k - 1], ring[0])

    for k in (2, 1, 3, 0):
        p = dot(att[wrap4(y + k)], wo[...], 1, 0)
        if k:
            part[k - 1] = p.astype(BF)
            ring_send(0, k, part.at[k - 1], land1.at[k - 1])
        else:
            acc[...] = p + tok[...].astype(F32)
    for r in range(4):
        dhid[r] = dot(cot[r], wd[...], 1, 1)
    for k in (1, 3, 2):
        ring_wait(0, k, land1.at[k - 1])
    total = acc[...]
    for k in range(3):
        total = total + land1[k].astype(F32)
    acc[...] = total
    scale = rms_scale(total)
    unit[...] = total * scale
    mid[y] = (total * scale * gain[...]).astype(BF)
    for k in (2, 1, 3):
        ring_send(1, k, mid.at[y], mid.at[y])

    for k in (0, 1, 3, 2):
        r = wrap4(y - k)
        if k:
            ring_wait(1, k, mid.at[r])
        gu = dot(mid[r], wb[...], 1, 0)
        gate, up = gu[:, :768], gu[:, 768:]
        sig = 1.0 / (1.0 + jnp.exp(-gate))
        act = gate * sig
        dh = dhid[r]
        hid[r] = (act * up).astype(BF)
        dgu[r, :, :768] = (dh * up * sig * (1.0 + gate * (1.0 - sig))).astype(BF)
        dgu[r, :, 768:] = (dh * act).astype(BF)
        p = dot(dgu[r], wb[...], 1, 1)
        if k:
            dpart[k - 1] = p.astype(BF)
            ring_send(2, 4 - k, dpart.at[k - 1], land2.at[3 - k])
        else:
            dmid[...] = p

    for k in (1, 3, 2):
        ring_wait(2, k, land2.at[k - 1])
    total = dmid[...]
    for k in range(3):
        total = total + land2[k].astype(F32)
    gffn[...] = jnp.sum(total * unit[...], axis=0, keepdims=True)
    total = total * gain[...]
    mean = jnp.mean(total * unit[...], axis=-1, keepdims=True)
    total = cot[y].astype(F32) + rms_scale(acc[...]) * (total - unit[...] * mean)
    dmid[...] = total
    dbr[y] = total.astype(BF)
    for k in (2, 1, 3):
        ring_send(3, k, dbr.at[y], dbr.at[y])

    def gate_up_rows(f, _):
        cols = pl.ds(pl.multiple_of(f * 128, 128), 128)
        rows = mid[:, :, cols].reshape(CHUNK, 128)
        g = dot(rows, dgu[...].reshape(CHUNK, 1536), 0, 0)
        gbs[pl.ds(f * 8, 8)] = g.reshape(8, 2, 8, 1536).astype(BF)
        return 0

    lax.fori_loop(0, 8, gate_up_rows, 0)
    sb.start()

    def down_rows(f, _):
        cols = pl.ds(pl.multiple_of(f * 384, 384), 384)
        rows = hid[:, :, cols].reshape(CHUNK, 384)
        g = dot(rows, cot[...].reshape(CHUNK, 1024), 0, 0)
        gds[pl.ds(f * 8, 8)] = g.reshape(8, 2, 24, 1024).astype(BF)
        return 0

    lax.fori_loop(0, 2, down_rows, 0)
    sd.start()
    for k in (2, 1, 3, 0):
        p = dot(hid[wrap4(y + k)], wd[...], 1, 0)
        if k:
            opart[k - 1] = p.astype(BF)
            ring_send(4, k, opart.at[k - 1], land3.at[k - 1])
        else:
            acc[...] = acc[...] + p
    sb.cores()
    sd.cores()
    for k in (0, 1, 3, 2):
        r = wrap4(y - k)
        if k:
            ring_wait(3, k, dbr.at[r])
        datt[r] = dot(dbr[r], wo[...], 1, 1).astype(BF)

    def out_rows(f, _):
        cols = pl.ds(pl.multiple_of(f * 256, 256), 256)
        rows = att[:, :, cols].reshape(CHUNK, 256)
        g = dot(rows, dbr[...].reshape(CHUNK, 1024), 0, 0)
        go[pl.ds(f * 8, 8)] = g.reshape(8, 2, 16, 1024).astype(BF)
        return 0

    lax.fori_loop(0, 2, out_rows, 0)
    for k in (1, 3, 2):
        ring_wait(4, k, land3.at[k - 1])
    total = acc[...]
    for k in range(3):
        total = total + land3[k].astype(F32)
    out[...] = total.astype(BF)
    sb.second()
    sd.second()
    sb.first()
    sd.first(od)
    sb.owners()
    for r in range(4):
        for g in range(2):
            h = g * 4 + r
            og[:, h * 384 : h * 384 + 384] = sb.ry[r, :, g * 384 : g * 384 + 384].astype(F32)
            ou[:, h * 384 : h * 384 + 384] = sb.ry[r, :, 768 + g * 384 : 1152 + g * 384].astype(F32)
    sb.done()
    sd.done()
    for copy in sends:
        copy.wait_send()


def middle(att, tok, cot, wo, wb, wd, gain):
    sds = jax.ShapeDtypeStruct
    block = (128, 1024)
    return pl.pallas_call(
        middle_kernel,
        out_shape=(
            sds(block, BF),
            sds(block, F32),
            sds((4, 128, 512), BF),
            sds((1, 1024), F32),
            sds((16, 2, 16, 1024), BF),
            sds((8, 3072), F32),
            sds((8, 3072), F32),
            sds((24, 1024), F32),
        ),
        in_specs=[VMEM] * 7,
        out_specs=(VMEM,) * 8,
        scratch_shapes=[
            pltpu.VMEM((3,) + block, BF),
            pltpu.VMEM((3,) + block, BF),
            pltpu.VMEM(block, F32),
            pltpu.VMEM(block, F32),
            pltpu.VMEM((4,) + block, BF),
            pltpu.VMEM((4, 128, 768), F32),
            pltpu.VMEM((4, 128, 1536), BF),
            pltpu.VMEM((4, 128, 768), BF),
            pltpu.VMEM((3,) + block, BF),
            pltpu.VMEM((3,) + block, BF),
            pltpu.VMEM((4,) + block, BF),
            pltpu.VMEM((3,) + block, BF),
            pltpu.VMEM((3,) + block, BF),
            pltpu.VMEM((64, 2, 8, 1536), BF),
            pltpu.VMEM((16, 2, 24, 1024), BF),
            DMA((5, 3)),
            DMA((5, 3)),
        ]
        + Sums.scratch(8, 1536, 4)
        + Sums.scratch(24, 1024, 1),
        compiler_params=params(3),
        name="middle",
    )(att, tok, cot, wo, wb, wd, gain)


def rms_scale(rows):
    return lax.rsqrt(jnp.mean(rows * rows, axis=-1, keepdims=True) + EPS)


def norm_back(d_normed, unit, scale, gain):
    d_unit = d_normed * gain
    return scale * (d_unit - unit * jnp.mean(d_unit * unit, axis=-1, keepdims=True))


def rope_tables():
    freq = ROPE_BASE ** (-np.arange(0, HEAD_SIZE, 2, dtype=np.float64) / HEAD_SIZE)
    freq = np.concatenate([freq, freq])
    inner = np.arange(CHUNK)[:, None] * freq[None, :]
    outer = (np.arange(32) * CHUNK)[:, None] * freq[None, :]
    return [f(a).astype(np.float32) for a in (inner, outer) for f in (np.cos, np.sin)]


def rotate_half(rows):
    half = rows.shape[-1] // 2
    return jnp.concatenate([-rows[..., half:], rows[..., :half]], axis=-1)


def head_prep(raw, gain, cos, sin):
    normed = raw * rms_scale(raw) * gain
    return normed * cos + rotate_half(normed) * sin


def dot(a, b, ca, cb):
    return lax.dot_general(a, b, (((ca,), (cb,)), ((), ())), preferred_element_type=F32)


def local(
    tokens, cotangent, segments, attn_gain, w_query, key_matrix, value_matrix, query_gain, key_gain,
    w_out, ffn_gain, w_gate, w_up, w_down,
):
    y = lax.rem(lax.axis_index("head"), 4)
    chunk = 2 * lax.axis_index("blk") + lax.div(lax.axis_index("head"), 4)
    own_gains = jnp.concatenate(
        [
            attn_gain[:, None],
            ffn_gain[:, None],
            jnp.broadcast_to(query_gain[None, :], (8, 1)),
            jnp.broadcast_to(key_gain[None, :], (8, 1)),
            jnp.zeros((8, 124), BF),
        ],
        axis=1,
    )
    xs, cs, wa, wb, wo, wd = gather_all(
        tokens, cotangent, w_query, key_matrix, value_matrix, w_gate, w_up, own_gains, w_out, w_down
    )
    wa = wa.reshape(1024, 1152)
    wb = wb.reshape(1024, 1536)
    wo = wo.reshape(512, 1024)
    wd = wd.reshape(768, 1024)
    gains = wa[:, 1024:1028].astype(F32)
    attn_g, ffn_g = gains[:, 0], gains[:, 1]
    q_gain, k_gain = gains[::8, 2], gains[::8, 3]

    x = xs.reshape(CHUNK, 1024).astype(F32)
    scale_one = rms_scale(x)
    x_normed = (x * scale_one * attn_g).astype(BF)
    raw = dot(x_normed, wa[:, :1024], 1, 0)
    q_raw = raw[:, :512].reshape(CHUNK, 4, HEAD_SIZE)
    k_raw = raw[:, 512:768].reshape(CHUNK, 2, HEAD_SIZE)
    v = raw[:, 768:1024].astype(BF)
    in_cos, in_sin, out_cos, out_sin = rope_tables()
    c0 = lax.dynamic_slice_in_dim(jnp.asarray(out_cos), chunk, 1, 0)
    s0 = lax.dynamic_slice_in_dim(jnp.asarray(out_sin), chunk, 1, 0)
    cos = (c0 * in_cos - s0 * in_sin)[:, None, :]
    sin = (s0 * in_cos + c0 * in_sin)[:, None, :]

    def prep(q, k, qg, kg):
        return head_prep(q, qg, cos, sin), head_prep(k, kg, cos, sin)

    (q_rot, k_rot), prep_back = jax.vjp(prep, q_raw, k_raw, q_gain, k_gain)
    q = q_rot.astype(BF)
    k = k_rot.astype(BF).reshape(CHUNK, 256)
    kv = halo(jnp.concatenate([k, v], axis=1), 2).reshape(3 * CHUNK, 512)
    k_ext = kv[:, :256].reshape(3 * CHUNK, 2, HEAD_SIZE)
    v_ext = kv[:, 256:].reshape(3 * CHUNK, 2, HEAD_SIZE)
    q4 = q.reshape(CHUNK, 2, 2, HEAD_SIZE)

    padded = jnp.concatenate([jnp.full((2 * CHUNK,), -1, jnp.int32), segments])
    seg_keys = lax.dynamic_slice_in_dim(padded, chunk * CHUNK, 3 * CHUNK, 0)
    seg_rows = seg_keys[2 * CHUNK :]
    begins = jnp.sum((seg_keys[None, :] < seg_rows[:, None]).astype(jnp.int32), axis=1)
    row = jnp.arange(CHUNK, dtype=jnp.int32)
    low = jnp.maximum(begins, row + 1)
    column = jnp.arange(3 * CHUNK, dtype=jnp.int32)[None, :]
    allowed = (column >= low[:, None]) & (column <= row[:, None] + SPAN)
    attn_scale = HEAD_SIZE ** (-0.5)
    scores = jnp.einsum("qkgd,ckd->kgqc", q4, k_ext, preferred_element_type=F32) * attn_scale
    scores = jnp.where(allowed[None, None], scores, MASKED)
    peak = jnp.max(scores, axis=-1, keepdims=True)
    weight = jnp.exp(scores - peak)
    total = jnp.sum(weight, axis=-1, keepdims=True)
    soft = weight / total
    probs = soft.astype(BF)
    attended = jnp.einsum("kgqc,ckd->qkgd", probs, v_ext, preferred_element_type=F32)
    attended = attended.astype(BF).reshape(CHUNK, 512)

    x_own = tokens.astype(F32)
    output, d_mid, d_att, g_ffn, go, og, ou, od = middle(
        attended.reshape(4, 128, 512), tokens, cs, wo, wb, wd, ffn_g[None, :]
    )
    d4 = d_att.reshape(CHUNK, 2, 2, HEAD_SIZE)

    d_v = jnp.einsum("kgqc,qkgd->ckd", probs, d4, preferred_element_type=F32)
    d_probs = jnp.einsum("qkgd,ckd->kgqc", d4, v_ext, preferred_element_type=F32)
    inner = jnp.sum(soft * d_probs, axis=-1, keepdims=True)
    d_scores = (soft * (d_probs - inner)).astype(BF)
    d_q = jnp.einsum("kgqc,ckd->qkgd", d_scores, k_ext, preferred_element_type=F32) * attn_scale
    d_k = jnp.einsum("kgqc,qkgd->ckd", d_scores, q4, preferred_element_type=F32) * attn_scale
    d_kv = jnp.concatenate([d_k.reshape(3 * CHUNK, 256), d_v.reshape(3 * CHUNK, 256)], axis=1)
    d_kv = halo_back(d_kv.astype(BF).reshape(3, CHUNK, 512), 8)
    d_kv = d_kv.astype(BF)
    d_q_raw, d_k_raw, g_qg, g_kg = prep_back(
        (
            d_q.astype(BF).astype(F32).reshape(CHUNK, 4, HEAD_SIZE),
            d_kv[:, :256].astype(F32).reshape(CHUNK, 2, HEAD_SIZE),
        )
    )
    d_qkv = jnp.concatenate(
        [
            d_q_raw.astype(BF).reshape(CHUNK, 512),
            d_k_raw.astype(BF).reshape(CHUNK, 256),
            d_kv[:, 256:],
        ],
        axis=1,
    )
    d_x_normed = ring_sum(dot(d_qkv, wa[:, :1024], 1, 1).astype(BF).reshape(4, 128, 1024), 9)
    scale_own = rms_scale(x_own)
    unit_own = x_own * scale_own
    input_grad = (d_mid + norm_back(d_x_normed, unit_own, scale_own, attn_g)).astype(BF)

    g_attn = jnp.sum(d_x_normed * unit_own, axis=0)
    g_gains = jnp.concatenate(
        [
            g_attn[:, None],
            g_ffn[0][:, None],
            jnp.repeat(g_qg, 8)[:, None],
            jnp.repeat(g_kg, 8)[:, None],
            jnp.zeros((1024, 124), F32),
        ],
        axis=1,
    ).astype(BF)
    ga = jnp.concatenate([dot(x_normed, d_qkv, 0, 0).astype(BF), g_gains], axis=1)
    oq, ok, ov, oo, ogain = grads_out(ga.reshape(64, 2, 8, 1152), go)
    return (
        output,
        input_grad,
        ogain[:, 0],
        oq,
        ok,
        ov,
        ogain[0, 2:3],
        ogain[0, 3:4],
        oo,
        ogain[:, 1],
        og,
        ou,
        od,
    )


def solution(mesh):
    rows = P(("blk", "head"), None)
    cut = P(("head", "blk"), None)
    vec = P(("head", "blk"))
    return jax.shard_map(
        local,
        mesh=mesh,
        in_specs=(rows, rows, P(), vec, cut, cut, cut, vec, vec, cut, vec, cut, cut, cut),
        out_specs=(rows, rows, vec, cut, cut, cut, vec, vec, cut, vec, cut, cut, cut),
        check_vma=False,
    )
```

```python
import math

import jax
import jax.numpy as jnp
import numpy as np
from jax import lax
from jax.experimental import pallas as pl
from jax.experimental.pallas import tpu as pltpu
from jax.sharding import PartitionSpec as P

HEAD_SIZE = 128
SPAN = 1024
CHUNK = 512
EPS = 1e-06
ROPE_BASE = 1000000.0
MASKED = -1e30
MESH = pl.DeviceIdType.MESH
BF = jnp.bfloat16
F32 = jnp.float32
VMEM = pl.BlockSpec(memory_space=pltpu.VMEM)
HBM = pl.BlockSpec(memory_space=pl.ANY)
DMA = pltpu.SemaphoreType.DMA
VMEM_LIMIT = 58 * 2**20


def coords():
    h = lax.axis_index("head")
    b = lax.axis_index("blk")
    x = 2 * lax.div(h, 4) + lax.div(b, 8)
    return x, lax.rem(h, 4), lax.rem(lax.div(b, 2), 4), lax.rem(b, 2)


def device(x, y, z, c):
    return (lax.div(x, 2) * 4 + y, lax.rem(x, 2) * 8 + z * 2 + c)


def wrap4(v):
    return lax.rem(v + 8, 4)


def send(src, dst, send_sem, recv_sem, to):
    copy = pltpu.make_async_remote_copy(
        src_ref=src, dst_ref=dst, send_sem=send_sem, recv_sem=recv_sem, device_id=to, device_id_type=MESH
    )
    copy.start()
    return copy


def arrived(dst, sem, anyone):
    pltpu.make_async_remote_copy(
        src_ref=dst, dst_ref=dst, send_sem=sem, recv_sem=sem, device_id=anyone, device_id_type=MESH
    ).wait_recv()


def meet(peers):
    barrier = pltpu.get_barrier_semaphore()
    for peer in peers:
        pl.semaphore_signal(barrier, inc=1, device_id=peer, device_id_type=MESH)
    pl.semaphore_wait(barrier, len(peers))


def params(collective_id):
    return pltpu.CompilerParams(
        collective_id=collective_id, has_side_effects=True, vmem_limit_bytes=VMEM_LIMIT
    )


def chunk_number():
    return 2 * lax.axis_index("blk") + lax.div(lax.axis_index("head"), 4)


def chunk_device(step):
    chunk = lax.rem(chunk_number() + step + 32, 32)
    return (lax.rem(chunk, 2) * 4 + lax.rem(lax.axis_index("head"), 4), lax.div(chunk, 2))


def greet_all(chunks=False):
    x, y, z, c = coords()
    peers = [device(x, wrap4(y + k), z, c) for k in range(1, 4)]
    peers += [device(wrap4(x + k), y, z, c) for k in range(1, 4)]
    peers += [device(x, y, wrap4(z + k), c) for k in range(1, 4)]
    peers += [device(x, y, z, 1 - c)]
    if chunks:
        peers += [chunk_device(s) for s in (-2, -1, 1, 2)]
    meet(peers)


def dot(a, b, ca, cb):
    return lax.dot_general(a, b, (((ca,), (cb,)), ((), ())), preferred_element_type=F32)


def rms_scale(rows):
    return lax.rsqrt(jnp.mean(rows * rows, axis=-1, keepdims=True) + EPS)


def rope_tables():
    freq = ROPE_BASE ** (-np.arange(0, HEAD_SIZE, 2, dtype=np.float64) / HEAD_SIZE)
    freq = np.concatenate([freq, freq])
    sign = np.where(np.arange(HEAD_SIZE) < 64, -1.0, 1.0)
    inner = np.arange(CHUNK)[:, None] * freq[None, :]
    outer = (np.arange(32) * CHUNK)[:, None] * freq[None, :]
    tables = [f(a) * s for a in (inner, outer) for f, s in ((np.cos, 1.0), (np.sin, sign))]
    return [jnp.asarray(t.astype(np.float32)) for t in tables]


def rope_here(ic, isn, oc, osn, cos, sin):
    n = chunk_number()
    c0, s0 = oc[pl.ds(n, 1), :], osn[pl.ds(n, 1), :]
    cos[...] = c0 * ic[...] - s0 * isn[...]
    sin[...] = s0 * ic[...] + c0 * isn[...]


def rope(rows, cos, sin):
    return rows * cos + pltpu.roll(rows, 64, 1) * sin


def rope_back(rows, cos, sin):
    return rows * cos + pltpu.roll(rows * sin, 64, 1)


def prep_back(d, raw, gain, cos, sin):
    scale = rms_scale(raw)
    unit = raw * scale
    d = rope_back(d, cos, sin)
    d_gain = jnp.sum(d * unit, axis=0, keepdims=True)
    d = d * gain
    return scale * (d - unit * jnp.mean(d * unit, axis=-1, keepdims=True)), d_gain


REACH = (((0, 512), (256, 256)), ((0, 512), (0, 512)), ((0, 256), (0, 512)))
EXP_SCALE = HEAD_SIZE ** (-0.5) * math.log2(math.e)


def allowed(low, slot, t):
    first, count = REACH[slot][t]
    place = lax.broadcasted_iota(jnp.int32, (count, 512), 0) + (slot * CHUNK + first)
    ok = place >= low[t]
    if slot == 2:
        query = lax.rem(lax.broadcasted_iota(jnp.int32, (1, 512), 1), 256) + (t * 256 + SPAN)
        ok = ok & (place <= query)
    return ok


def attend(q, kvx, low, peak, total, acc, slot, fresh):
    def group(g, _):
        for t in range(2):
            first, count = REACH[slot][t]
            keys = kvx[g, slot, first : first + count]
            values = kvx[2 + g, slot, first : first + count]
            s = dot(keys, q[g, t], 1, 1)
            s = jnp.where(allowed(low, slot, t), s, MASKED)
            top = jnp.max(s, axis=0, keepdims=True)
            if not fresh:
                before = peak[g, t]
                top = jnp.maximum(top, before)
                fade = jnp.exp2((before - top) * EXP_SCALE)
            p = jnp.exp2((s - top) * EXP_SCALE)
            add = jnp.sum(p, axis=0, keepdims=True)
            o = dot(values, p.astype(BF), 0, 0)
            if not fresh:
                add = add + total[g, t] * fade
                o = o + acc[g, t] * fade
            peak[g, t] = top
            total[g, t] = add
            acc[g, t] = o
        return 0

    lax.fori_loop(0, 2, group, 0)


def attend_back(q, kvx, low, lse, do, inner, dq, dkv, slot, fresh):
    def group(g, _):
        for t in range(2):
            first, count = REACH[slot][t]
            rows = slice(first, first + count)
            keys = kvx[g, slot, rows]
            values = kvx[2 + g, slot, rows]
            s = dot(keys, q[g, t], 1, 1)
            p = jnp.where(allowed(low, slot, t), jnp.exp2(s * EXP_SCALE - lse[g, t]), 0.0)
            dp = dot(values, do[g, t], 1, 1)
            ds = (p * (dp - inner[g, t])).astype(BF)
            dv = dot(p.astype(BF), do[g, t], 1, 0)
            dk = dot(ds, q[g, t], 1, 0)
            whole = count == CHUNK
            if whole and (t == 0 or slot == 2):
                other = slice(0, 256)
                if t == 0:
                    dkv[g, slot] = dk
                    dkv[2 + g, slot] = dv
                else:
                    dkv[g, slot, other] = dkv[g, slot, other] + dk[other]
                    dkv[2 + g, slot, other] = dkv[2 + g, slot, other] + dv[other]
                    dkv[g, slot, 256:] = dk[256:]
                    dkv[2 + g, slot, 256:] = dv[256:]
            elif t == 0:
                dkv[g, slot, rows] = dk
                dkv[2 + g, slot, rows] = dv
            else:
                dkv[g, slot, rows] = dkv[g, slot, rows] + dk
                dkv[2 + g, slot, rows] = dkv[2 + g, slot, rows] + dv
            d = dot(keys, ds, 0, 0)
            dq[g, t] = d if fresh else dq[g, t] + d
        return 0

    lax.fori_loop(0, 2, group, 0)


class Pieces:
    def __init__(self, ref, wide, ssem, rsem):
        self.ref, self.wide, self.ssem, self.rsem = ref, wide, ssem, rsem
        self.x, self.y, self.z, self.c = x, y, z, c = coords()
        self.d = 1 - c
        self.across = device(x, y, z, 1 - c)
        self.ring = [device(x, wrap4(y + k), z, c) for k in range(1, 4)]
        self.sends = []

    @staticmethod
    def semaphores():
        return [DMA((34,)), DMA((34,))]

    def slot(self, px, pz, core):
        b = lax.rem(px, 2) * 8 + pz * 2 + core
        if self.wide:
            return self.ref.at[lax.div(px, 2), :, b]
        return self.ref.at[lax.div(px, 2), b]

    def piece(self, j, k):
        c, d = self.c, self.d
        return self.slot(wrap4(self.x - j * d - k * c), wrap4(self.z - j * c - k * d), c)

    def piece_across(self, j, k):
        c, d = self.c, self.d
        return self.slot(wrap4(self.x - j * c - k * d), wrap4(self.z - j * d - k * c), d)

    def send(self, src, dst, n, to):
        self.sends.append(send(src, dst, self.ssem.at[n], self.rsem.at[n], to))

    def first(self, k):
        return device(wrap4(self.x + k * self.d), self.y, wrap4(self.z + k * self.c), self.c)

    def second(self, k):
        return device(wrap4(self.x + k * self.c), self.y, wrap4(self.z + k * self.d), self.c)

    def to_ring(self, parts):
        self.b = lax.rem(self.x, 2) * 8 + self.z * 2 + self.c
        xh = lax.div(self.x, 2)
        self.at_ring = lambda r: self.ref.at[xh, r, self.b]
        for k in range(1, 4):
            self.send(parts.at[wrap4(self.y + k)], self.at_ring(self.y), 30 + k, self.ring[k - 1])
        self.ref[xh, self.y, self.b] = parts[self.y]

    def from_ring(self):
        for k in range(1, 4):
            arrived(self.at_ring(wrap4(self.y - k)), self.rsem.at[30 + k], self.across)

    def own(self, src=None):
        src = self.piece(0, 0) if src is None else src
        for k in (2, 1, 3):
            self.send(src, self.piece(0, 0), k - 1, self.first(k))
        for k in (2, 1, 3):
            self.send(src, self.piece(0, 0), 2 + k, self.second(k))
        self.send(src, self.piece(0, 0), 15, self.across)

    def pass_on(self, j):
        here = self.piece(j, 0)
        arrived(here, self.rsem.at[j - 1], self.across)
        for k in (2, 1, 3):
            self.send(here, here, 2 + 3 * j + k, self.second(k))
        self.send(here, here, 15 + 4 * j, self.across)

    def pass_across(self, j, k):
        here = self.piece(j, k)
        arrived(here, self.rsem.at[2 + 3 * j + k], self.across)
        self.send(here, here, 15 + 4 * j + k, self.across)

    def pass_all_on(self):
        for j in (1, 3, 2):
            self.pass_on(j)

    def pass_all_across(self):
        for j in (0, 1, 3, 2):
            for k in (1, 3, 2):
                self.pass_across(j, k)

    def all_here(self):
        for j in range(4):
            for k in range(4):
                arrived(self.piece_across(j, k), self.rsem.at[15 + 4 * j + k], self.across)

    def done(self):
        for copy in self.sends:
            copy.wait_send()


def pack_wide(src, dst):
    cols = src.shape[-1]

    def rows(i, _):
        part = src[lax.div(i, 4), lax.rem(i, 4)].astype(F32).reshape(128, cols)
        dst[pl.ds(pl.multiple_of(i * 128, 128), 128)] = part.astype(BF)
        return 0

    lax.fori_loop(0, 8, rows, 0)


def pack_down(src, dst):
    def rows(i, _):
        part = src[lax.div(i, 4), pl.ds(lax.rem(i, 4) * 4, 4)].astype(F32).reshape(96, 1024)
        dst[pl.ds(pl.multiple_of(i * 96, 96), 96)] = part.astype(BF)
        return 0

    lax.fori_loop(0, 8, rows, 0)


def front_kernel(
    tok, cot, wq, wk, wv, gains, wo, low, ic, isn, oc, osn,
    att, cs, wof, wa, rows, xn, q, kvx, lse,
    sa, wal, xs, cos, sin, peak, total, acc, ssem, rsem, lsem, *sems,
):
    x, y, z, c = coords()
    ring = [device(x, wrap4(y + k), z, c) for k in range(1, 4)]
    for r in range(4):
        for g in range(2):
            h = g * 4 + r
            sa[r, :, g * 256 : g * 256 + 256] = wq[:, h * 256 : h * 256 + 256]
            sa[r, :, 512 + g * 128 : 640 + g * 128] = wk[:, h * 128 : h * 128 + 128]
            sa[r, :, 768 + g * 128 : 896 + g * 128] = wv[:, h * 128 : h * 128 + 128]
        sa[r, :, 1024:1152] = gains[...]
    a = Pieces(wal, True, *sems[:2])
    o = Pieces(wof, False, *sems[2:4])
    greet_all(True)
    sends = []

    def ring_send(n, k, src, dst):
        sends.append(send(src, dst, ssem.at[n, k - 1], rsem.at[n, k - 1], ring[k - 1]))

    a.to_ring(sa)
    for k in (2, 1, 3):
        ring_send(0, k, tok, xs.at[y])
    own_o = pltpu.make_async_copy(wo, o.piece(0, 0), lsem.at[0])
    own_o.start()
    own_c = pltpu.make_async_copy(cot, cs.at[y], lsem.at[1])
    own_c.start()
    xs[y] = tok[...]
    rope_here(ic, isn, oc, osn, cos, sin)
    a.from_ring()
    a.own()
    a.pass_all_on()
    o.own(wo)
    for k in (1, 3, 2):
        arrived(xs.at[wrap4(y - k)], rsem.at[0, k - 1], ring[0])
    for k in (2, 1, 3):
        ring_send(1, k, cot, cs.at[y])
    a.pass_all_across()
    o.pass_all_on()
    a.all_here()
    pack_wide(wal, wa)

    pick = lax.broadcasted_iota(jnp.int32, (8, 128), 0) == lax.broadcasted_iota(jnp.int32, (8, 128), 1)
    by_row = dot(pick.astype(F32).astype(BF), wa[:, 1024:1152], 1, 1)
    rows[:, :1024] = by_row
    every = lax.broadcasted_iota(jnp.int32, (1024, 128), 0) == 8 * lax.broadcasted_iota(jnp.int32, (1024, 128), 1)
    rows[:, 1024:] = dot(by_row.astype(BF), every.astype(F32).astype(BF), 1, 0)
    q_gain, k_gain = rows[2:3, 1024:], rows[3:4, 1024:]
    for r in range(4):
        block = xs[r].astype(F32)
        xn[r * 128 : r * 128 + 128] = (block * rms_scale(block) * rows[0:1, :1024]).astype(BF)

    raw = dot(xn[...], wa[:, 512:768], 1, 0)
    for g in range(2):
        k_raw = raw[:, g * 128 : g * 128 + 128]
        kvx[g, 2] = rope(k_raw * rms_scale(k_raw) * k_gain, cos[...], sin[...]).astype(BF)
    raw = dot(xn[...], wa[:, 768:1024], 1, 0)
    for g in range(2):
        kvx[2 + g, 2] = raw[:, g * 128 : g * 128 + 128].astype(BF)
    near = send(kvx.at[:, 2], kvx.at[:, 1], ssem.at[2, 0], rsem.at[2, 0], chunk_device(1))
    far = send(kvx.at[:, 2], kvx.at[:, 0], ssem.at[2, 1], rsem.at[2, 1], chunk_device(2))

    def queries(g, _):
        raw = dot(xn[...], wa[:, pl.ds(pl.multiple_of(g * 256, 256), 256)], 1, 0)
        for hd in range(2):
            q_raw = raw[:, hd * 128 : hd * 128 + 128]
            rot = rope(q_raw * rms_scale(q_raw) * q_gain, cos[...], sin[...]).astype(BF)
            for t in range(2):
                q[g, t, hd * 256 : hd * 256 + 256] = rot[t * 256 : t * 256 + 256]
        return 0

    lax.fori_loop(0, 2, queries, 0)
    attend(q, kvx, low, peak, total, acc, 2, True)
    o.pass_all_across()
    near.wait_recv()
    attend(q, kvx, low, peak, total, acc, 1, False)
    far.wait_recv()
    attend(q, kvx, low, peak, total, acc, 0, False)
    for g in range(2):
        for t in range(2):
            done = jnp.transpose(acc[g, t] / total[g, t]).astype(BF)
            lse[g, t] = peak[g, t] * EXP_SCALE + jnp.log(total[g, t]) * math.log2(math.e)
            for hd in range(2):
                cols = slice((g * 2 + hd) * 128, (g * 2 + hd) * 128 + 128)
                for half in range(2):
                    first = hd * 256 + half * 128
                    att[2 * t + half, :, cols] = done[first : first + 128]
    for k in (1, 3, 2):
        arrived(cs.at[wrap4(y - k)], rsem.at[1, k - 1], ring[0])
    o.all_here()
    own_o.wait()
    own_c.wait()
    for copy in sends + [near, far]:
        copy.wait_send()
    a.done()
    o.done()


def front(tok, cot, wq, wk, wv, gains, wo, low):
    sds = jax.ShapeDtypeStruct
    return pl.pallas_call(
        front_kernel,
        out_shape=(
            sds((4, 128, 512), BF),
            sds((4, 128, 1024), BF),
            sds((2, 16, 16, 1024), BF),
            sds((1024, 1152), BF),
            sds((8, 1152), F32),
            sds((CHUNK, 1024), BF),
            sds((2, 2, 512, 128), BF),
            sds((4, 3, CHUNK, 128), BF),
            sds((2, 2, 1, 512), F32),
        ),
        in_specs=[VMEM, HBM] + [VMEM] * 4 + [HBM] + [VMEM] * 5,
        out_specs=(VMEM, HBM, HBM) + (VMEM,) * 6,
        scratch_shapes=[
            pltpu.VMEM((4, 8, 1152), BF),
            pltpu.VMEM((2, 4, 16, 8, 1152), BF),
            pltpu.VMEM((4, 128, 1024), BF),
            pltpu.VMEM((CHUNK, 128), F32),
            pltpu.VMEM((CHUNK, 128), F32),
            pltpu.VMEM((2, 2, 1, 512), F32),
            pltpu.VMEM((2, 2, 1, 512), F32),
            pltpu.VMEM((2, 2, 128, 512), F32),
            DMA((3, 3)),
            DMA((3, 3)),
            DMA((2,)),
        ]
        + Pieces.semaphores() * 2,
        compiler_params=params(0),
        name="front",
    )(tok, cot, wq, wk, wv, gains, wo, low, *rope_tables())


class Sums:
    def __init__(self, grad, rows, cols, cut, refs):
        self.grad, self.rows, self.cols, self.cut = grad, rows, cols, cut
        (self.rc, self.sa, self.lb, self.sb, self.l2, self.sd, self.ry, self.ss, self.rs) = refs
        x, y, z, c = coords()
        self.y, self.c, self.d = y, c, 1 - c
        d = self.d
        self.across = device(x, y, z, d)
        self.ring = [device(x, wrap4(y + k), z, c) for k in range(1, 4)]
        self.to_first = [device(wrap4(x + k * d), y, wrap4(z + k * c), c) for k in range(1, 4)]
        self.to_second = [device(wrap4(x + k * c), y, wrap4(z + k * d), c) for k in range(1, 4)]
        self.p1 = x * d + z * c
        self.p2 = x * c + z * d
        self.sends = []

    @staticmethod
    def scratch(rows, cols, cut):
        buffers = [(16 * cut,), (4, 4, cut), (3, 4, cut), (4, cut), (3, cut), (cut,), (cut,)]
        return [pltpu.VMEM(lead + (rows, cols), BF) for lead in buffers] + [DMA((10,)), DMA((10,))]

    def start(self):
        self.over = send(self.grad.at[:, self.d], self.rc, self.ss.at[9], self.rs.at[9], self.across)
        self.sends.append(self.over)

    def cores(self):
        self.over.wait_recv()
        c, d, cut = self.c, self.d, self.cut

        def add(i, _):
            a2, a1, r = lax.div(i, 4 * cut), lax.rem(lax.div(i, cut), 4), lax.rem(i, cut)
            px, pz = a1 * d + a2 * c, a1 * c + a2 * d
            at = ((lax.div(px, 2) * cut + r) * 2 + lax.rem(px, 2)) * 4 + pz
            self.sa[a2, a1, r] = (self.rc[at].astype(F32) + self.grad[at, c].astype(F32)).astype(BF)
            return 0

        lax.fori_loop(0, 16 * cut, add, 0)
        self.hop = [
            send(self.sa.at[wrap4(self.p2 + k + 1)], self.lb.at[k], self.ss.at[k], self.rs.at[k], self.to_second[k])
            for k in range(3)
        ]
        self.sends += self.hop

    def second(self):
        for copy in self.hop:
            copy.wait_recv()

        def add(i, _):
            a1, r = lax.div(i, self.cut), lax.rem(i, self.cut)
            total = self.sa[self.p2, a1, r].astype(F32)
            for k in range(3):
                total = total + self.lb[k, a1, r].astype(F32)
            self.sb[a1, r] = total.astype(BF)
            return 0

        lax.fori_loop(0, 4 * self.cut, add, 0)
        self.hop = [
            send(self.sb.at[wrap4(self.p1 + k + 1)], self.l2.at[k], self.ss.at[3 + k], self.rs.at[3 + k], self.to_first[k])
            for k in range(3)
        ]
        self.sends += self.hop

    def first(self, out=None):
        for copy in self.hop:
            copy.wait_recv()
        for r in range(self.cut):
            total = self.sb[self.p1, r].astype(F32)
            for k in range(3):
                total = total + self.l2[k, r].astype(F32)
            if out is not None:
                out[...] = total
            else:
                self.sd[r] = total.astype(BF)
        if out is None:
            y = self.y
            self.hop = [
                send(self.sd.at[wrap4(y + k + 1)], self.ry.at[y], self.ss.at[6 + k], self.rs.at[6 + k], self.ring[k])
                for k in range(3)
            ]
            self.sends += self.hop
            self.ry[y] = self.sd[y]

    def owners(self):
        for copy in self.hop:
            copy.wait_recv()

    def done(self):
        for copy in self.sends:
            copy.wait_send()


def middle_kernel(
    att, tok, cot, wo, wg, wu, wdp, rows,
    out, dmid, datt, gffn, go, og, ou, od,
    part, land1, acc, unit, mid, dhid, dgu, hid, dpart, land2, dbr, opart, land3, gbs, gds,
    bparts, wbl, wdl, wb, wd, ssem, rsem, *scratch,
):
    x, y, z, c = coords()
    ring = [device(x, wrap4(y + k), z, c) for k in range(1, 4)]
    sb = Sums(gbs, 8, 1536, 4, scratch[:9])
    sd = Sums(gds, 24, 1024, 1, scratch[9:18])
    b = Pieces(wbl, True, *scratch[18:20])
    w = Pieces(wdl, False, *scratch[20:22])
    for r in range(4):
        for g in range(2):
            h = g * 4 + r
            bparts[r, :, g * 384 : g * 384 + 384] = wg[:, h * 384 : h * 384 + 384]
            bparts[r, :, 768 + g * 384 : 1152 + g * 384] = wu[:, h * 384 : h * 384 + 384]
    wdl[lax.div(x, 2), lax.rem(x, 2) * 8 + z * 2 + c] = wdp[...]
    gain = rows[1:2, :1024]
    greet_all()
    sends = []

    def ring_send(n, k, src, dst):
        sends.append(send(src, dst, ssem.at[n, k - 1], rsem.at[n, k - 1], ring[k - 1]))

    def ring_wait(n, k, dst):
        arrived(dst, rsem.at[n, k - 1], ring[0])

    b.to_ring(bparts)
    for k in (2, 1, 3, 0):
        p = dot(att[wrap4(y + k)], wo[...], 1, 0)
        if k:
            part[k - 1] = p.astype(BF)
            ring_send(0, k, part.at[k - 1], land1.at[k - 1])
        else:
            acc[...] = p + tok[...].astype(F32)
    b.from_ring()
    b.own()
    w.own()
    b.pass_all_on()
    w.pass_all_on()
    for k in (1, 3, 2):
        ring_wait(0, k, land1.at[k - 1])
    total = acc[...]
    for k in range(3):
        total = total + land1[k].astype(F32)
    acc[...] = total
    scale = rms_scale(total)
    unit[...] = total * scale
    mid[y] = (total * scale * gain).astype(BF)
    for k in (2, 1, 3):
        ring_send(1, k, mid.at[y], mid.at[y])
    b.pass_all_across()
    w.pass_all_across()
    w.all_here()
    pack_down(wdl, wd)
    for r in range(4):
        dhid[r] = dot(cot[r], wd[...], 1, 1)
    b.all_here()
    pack_wide(wbl, wb)

    for k in (0, 1, 3, 2):
        r = wrap4(y - k)
        if k:
            ring_wait(1, k, mid.at[r])
        gu = dot(mid[r], wb[...], 1, 0)
        gate, up = gu[:, :768], gu[:, 768:]
        sig = 1.0 / (1.0 + jnp.exp(-gate))
        act = gate * sig
        dh = dhid[r]
        hid[r] = (act * up).astype(BF)
        dgu[r, :, :768] = (dh * up * sig * (1.0 + gate * (1.0 - sig))).astype(BF)
        dgu[r, :, 768:] = (dh * act).astype(BF)
        p = dot(dgu[r], wb[...], 1, 1)
        if k:
            dpart[k - 1] = p.astype(BF)
            ring_send(2, 4 - k, dpart.at[k - 1], land2.at[3 - k])
        else:
            dmid[...] = p

    for k in (1, 3, 2):
        ring_wait(2, k, land2.at[k - 1])
    total = dmid[...]
    for k in range(3):
        total = total + land2[k].astype(F32)
    gffn[...] = jnp.sum(total * unit[...], axis=0, keepdims=True)
    total = total * gain
    mean = jnp.mean(total * unit[...], axis=-1, keepdims=True)
    total = cot[y].astype(F32) + rms_scale(acc[...]) * (total - unit[...] * mean)
    dmid[...] = total
    dbr[y] = total.astype(BF)
    for k in (2, 1, 3):
        ring_send(3, k, dbr.at[y], dbr.at[y])

    def gate_up_rows(f, _):
        cols = pl.ds(pl.multiple_of(f * 128, 128), 128)
        rows = mid[:, :, cols].reshape(CHUNK, 128)
        g = dot(rows, dgu[...].reshape(CHUNK, 1536), 0, 0)
        gbs[pl.ds(f * 8, 8)] = g.reshape(8, 2, 8, 1536).astype(BF)
        return 0

    lax.fori_loop(0, 8, gate_up_rows, 0)
    sb.start()

    def down_rows(f, _):
        cols = pl.ds(pl.multiple_of(f * 384, 384), 384)
        rows = hid[:, :, cols].reshape(CHUNK, 384)
        g = dot(rows, cot[...].reshape(CHUNK, 1024), 0, 0)
        gds[pl.ds(f * 8, 8)] = g.reshape(8, 2, 24, 1024).astype(BF)
        return 0

    lax.fori_loop(0, 2, down_rows, 0)
    sd.start()
    for k in (2, 1, 3, 0):
        p = dot(hid[wrap4(y + k)], wd[...], 1, 0)
        if k:
            opart[k - 1] = p.astype(BF)
            ring_send(4, k, opart.at[k - 1], land3.at[k - 1])
        else:
            acc[...] = acc[...] + p
    sb.cores()
    sd.cores()
    for k in (0, 1, 3, 2):
        r = wrap4(y - k)
        if k:
            ring_wait(3, k, dbr.at[r])
        datt[r] = dot(dbr[r], wo[...], 1, 1).astype(BF)

    def out_rows(f, _):
        cols = pl.ds(pl.multiple_of(f * 256, 256), 256)
        rows = att[:, :, cols].reshape(CHUNK, 256)
        g = dot(rows, dbr[...].reshape(CHUNK, 1024), 0, 0)
        go[pl.ds(f * 8, 8)] = g.reshape(8, 2, 16, 1024).astype(BF)
        return 0

    lax.fori_loop(0, 2, out_rows, 0)
    for k in (1, 3, 2):
        ring_wait(4, k, land3.at[k - 1])
    total = acc[...]
    for k in range(3):
        total = total + land3[k].astype(F32)
    out[...] = total.astype(BF)
    sb.second()
    sd.second()
    sb.first()
    sd.first(od)
    sb.owners()
    for r in range(4):
        for g in range(2):
            h = g * 4 + r
            og[:, h * 384 : h * 384 + 384] = sb.ry[r, :, g * 384 : g * 384 + 384].astype(F32)
            ou[:, h * 384 : h * 384 + 384] = sb.ry[r, :, 768 + g * 384 : 1152 + g * 384].astype(F32)
    for s in (sb, sd, b, w):
        s.done()
    for copy in sends:
        copy.wait_send()


def middle(att, tok, cot, wo, wg, wu, wd, rows):
    sds = jax.ShapeDtypeStruct
    block = (128, 1024)
    return pl.pallas_call(
        middle_kernel,
        out_shape=(
            sds(block, BF),
            sds(block, F32),
            sds((4, 128, 512), BF),
            sds((1, 1024), F32),
            sds((16, 2, 16, 1024), BF),
            sds((8, 3072), F32),
            sds((8, 3072), F32),
            sds((24, 1024), F32),
        ),
        in_specs=[VMEM] * 8,
        out_specs=(VMEM,) * 8,
        scratch_shapes=[
            pltpu.VMEM((3,) + block, BF),
            pltpu.VMEM((3,) + block, BF),
            pltpu.VMEM(block, F32),
            pltpu.VMEM(block, F32),
            pltpu.VMEM((4,) + block, BF),
            pltpu.VMEM((4, 128, 768), F32),
            pltpu.VMEM((4, 128, 1536), BF),
            pltpu.VMEM((4, 128, 768), BF),
            pltpu.VMEM((3,) + block, BF),
            pltpu.VMEM((3,) + block, BF),
            pltpu.VMEM((4,) + block, BF),
            pltpu.VMEM((3,) + block, BF),
            pltpu.VMEM((3,) + block, BF),
            pltpu.VMEM((64, 2, 8, 1536), BF),
            pltpu.VMEM((16, 2, 24, 1024), BF),
            pltpu.VMEM((4, 8, 1536), BF),
            pltpu.VMEM((2, 4, 16, 8, 1536), BF),
            pltpu.VMEM((2, 16, 24, 1024), BF),
            pltpu.VMEM((1024, 1536), BF),
            pltpu.VMEM((768, 1024), BF),
            DMA((5, 3)),
            DMA((5, 3)),
        ]
        + Sums.scratch(8, 1536, 4)
        + Sums.scratch(24, 1024, 1)
        + Pieces.semaphores() * 2,
        compiler_params=params(3),
        name="middle",
    )(att, tok, cot, wo, wg, wu, wd, rows)


def back_kernel(
    q, kvx, lse, att, datt, low, xn, wa, rows, go, dmid, tok, gffn, ic, isn, oc, osn,
    igrad, oq, ok, ov, oo, ogain,
    cos, sin, do, inner, dq, dkv, dkvb, land, raw, dqkv, gaq, gakv, grow, acc, dpart, landx, ssem, rsem, *scratch,
):
    x, y, z, c = coords()
    ring = [device(x, wrap4(y + k), z, c) for k in range(1, 4)]
    so = Sums(go, 16, 1024, 1, scratch[:9])
    sq = Sums(gaq, 8, 512, 4, scratch[9:18])
    sk = Sums(gakv, 8, 640, 4, scratch[18:27])
    q_gain, k_gain = rows[2:3, 1024:], rows[3:4, 1024:]
    greet_all(True)
    so.start()
    sends = []
    rope_here(ic, isn, oc, osn, cos, sin)
    ones = jnp.ones((8, 128), BF)
    for g in range(2):
        for t in range(2):
            for hd in range(2):
                cols = slice((g * 2 + hd) * 128, (g * 2 + hd) * 128 + 128)
                for half in range(2):
                    first = hd * 256 + half * 128
                    d = datt[2 * t + half, :, cols]
                    do[g, t, first : first + 128] = d
                    prod = d.astype(F32) * att[2 * t + half, :, cols].astype(F32)
                    high = prod.astype(BF)
                    rest = (prod - high.astype(F32)).astype(BF)
                    inner[g, t, :, first : first + 128] = (dot(ones, high, 1, 1) + dot(ones, rest, 1, 1))[:1]
    attend_back(q, kvx, low, lse, do, inner, dq, dkv, 0, True)
    dkvb[:, 0] = dkv[:, 0].astype(BF)
    sends.append(send(dkvb.at[:, 0], land.at[0], ssem.at[0, 0], rsem.at[0, 0], chunk_device(-2)))
    attend_back(q, kvx, low, lse, do, inner, dq, dkv, 1, False)
    dkvb[:, 1] = dkv[:, 1].astype(BF)
    sends.append(send(dkvb.at[:, 1], land.at[1], ssem.at[0, 1], rsem.at[0, 1], chunk_device(-1)))
    so.cores()
    attend_back(q, kvx, low, lse, do, inner, dq, dkv, 2, False)

    scale = HEAD_SIZE ** (-0.5)
    raw[...] = dot(xn[...], wa[:, :768], 1, 0)
    g_q = jnp.zeros((1, 128), F32)
    for g in range(2):
        for t in range(2):
            d = jnp.transpose(dq[g, t] * scale).astype(BF).astype(F32)
            span = slice(t * 256, t * 256 + 256)
            for hd in range(2):
                cols = slice((g * 2 + hd) * 128, (g * 2 + hd) * 128 + 128)
                d_raw, d_gain = prep_back(
                    d[hd * 256 : hd * 256 + 256], raw[span, cols], q_gain, cos[span], sin[span]
                )
                dqkv[span, cols] = d_raw.astype(BF)
                g_q = g_q + d_gain

    def query_rows(f, _):
        lhs = xn[:, pl.ds(pl.multiple_of(f * 128, 128), 128)]
        gaq[pl.ds(f * 8, 8)] = dot(lhs, dqkv[:, :512], 0, 0).reshape(8, 2, 8, 512).astype(BF)
        return 0

    lax.fori_loop(0, 8, query_rows, 0)
    sq.start()
    for copy in sends[:2]:
        copy.wait_recv()
    g_k = jnp.zeros((1, 128), F32)
    for g in range(2):
        d = dkv[g, 2] + land[0, g].astype(F32) + land[1, g].astype(F32)
        d = (d * scale).astype(BF).astype(F32)
        cols = slice(512 + g * 128, 640 + g * 128)
        d_raw, d_gain = prep_back(d, raw[:, cols], k_gain, cos[...], sin[...])
        dqkv[:, cols] = d_raw.astype(BF)
        g_k = g_k + d_gain
        d = dkv[2 + g, 2] + land[0, 2 + g].astype(F32) + land[1, 2 + g].astype(F32)
        dqkv[:, 768 + g * 128 : 896 + g * 128] = d.astype(BF)

    g_x = jnp.zeros((1, 1024), F32)
    for k in (2, 1, 3, 0):
        span = pl.ds(pl.multiple_of(wrap4(y + k) * 128, 128), 128)
        p = dot(dqkv[span], wa[:, :1024], 1, 1)
        g_x = g_x + jnp.sum(p * xn[span].astype(F32), axis=0, keepdims=True)
        if k:
            dpart[k - 1] = p.astype(BF)
            sends.append(send(dpart.at[k - 1], landx.at[k - 1], ssem.at[1, k - 1], rsem.at[1, k - 1], ring[k - 1]))
        else:
            acc[...] = p
    eight = lax.div(lax.broadcasted_iota(jnp.int32, (128, 1024), 1), 8) == lax.broadcasted_iota(jnp.int32, (128, 1024), 0)
    eight = eight.astype(F32).astype(BF)
    grow[...] = jnp.zeros_like(grow)
    grow[0:1] = g_x / rows[0:1, :1024]
    grow[1:2] = gffn[...]
    grow[2:3] = dot(jnp.broadcast_to(g_q, (8, 128)).astype(BF), eight, 1, 0)[:1]
    grow[3:4] = dot(jnp.broadcast_to(g_k, (8, 128)).astype(BF), eight, 1, 0)[:1]

    def key_rows(f, _):
        span = pl.ds(pl.multiple_of(f * 128, 128), 128)
        part = dot(xn[:, span], dqkv[:, 512:], 0, 0)
        gakv[pl.ds(f * 8, 8), :, :, :512] = part.reshape(8, 2, 8, 512).astype(BF)
        gakv[pl.ds(f * 8, 8), :, :, 512:] = jnp.transpose(grow[:, span]).reshape(8, 2, 8, 128).astype(BF)
        return 0

    lax.fori_loop(0, 8, key_rows, 0)
    sk.start()
    so.second()
    sq.cores()
    sk.cores()
    for k in (1, 3, 2):
        arrived(landx.at[k - 1], rsem.at[1, k - 1], ring[0])
    total = acc[...]
    for k in range(3):
        total = total + landx[k].astype(F32)
    own = tok[...].astype(F32)
    scale_own = rms_scale(own)
    unit = own * scale_own
    total = total * rows[0:1, :1024]
    mean = jnp.mean(total * unit, axis=-1, keepdims=True)
    igrad[...] = (dmid[...] + scale_own * (total - unit * mean)).astype(BF)
    sq.second()
    sk.second()
    so.first(oo)
    sq.first()
    sk.first()
    sq.owners()
    sk.owners()
    gain = jnp.zeros((8, 128), F32)
    for r in range(4):
        for g in range(2):
            h = g * 4 + r
            oq[:, h * 256 : h * 256 + 256] = sq.ry[r, :, g * 256 : g * 256 + 256].astype(F32)
            ok[:, h * 128 : h * 128 + 128] = sk.ry[r, :, g * 128 : g * 128 + 128].astype(F32)
            ov[:, h * 128 : h * 128 + 128] = sk.ry[r, :, 256 + g * 128 : 384 + g * 128].astype(F32)
        gain = gain + sk.ry[r, :, 512:640].astype(F32)
    ogain[...] = gain
    for copy in sends:
        copy.wait_send()
    for s in (so, sq, sk):
        s.done()


def back(q, kvx, lse, att, datt, low, xn, wa, rows, go, dmid, tok, gffn):
    sds = jax.ShapeDtypeStruct
    block = (128, 1024)
    return pl.pallas_call(
        back_kernel,
        out_shape=(
            sds(block, BF),
            sds((8, 2048), F32),
            sds((8, 1024), F32),
            sds((8, 1024), F32),
            sds((16, 1024), F32),
            sds((8, 128), F32),
        ),
        in_specs=[VMEM] * 17,
        out_specs=(VMEM,) * 6,
        scratch_shapes=[
            pltpu.VMEM((CHUNK, 128), F32),
            pltpu.VMEM((CHUNK, 128), F32),
            pltpu.VMEM((2, 2, 512, 128), BF),
            pltpu.VMEM((2, 2, 1, 512), F32),
            pltpu.VMEM((2, 2, 128, 512), F32),
            pltpu.VMEM((4, 3, CHUNK, 128), F32),
            pltpu.VMEM((4, 2, CHUNK, 128), BF),
            pltpu.VMEM((2, 4, CHUNK, 128), BF),
            pltpu.VMEM((CHUNK, 768), F32),
            pltpu.VMEM((CHUNK, 1024), BF),
            pltpu.VMEM((64, 2, 8, 512), BF),
            pltpu.VMEM((64, 2, 8, 640), BF),
            pltpu.VMEM((128, 1024), F32),
            pltpu.VMEM(block, F32),
            pltpu.VMEM((3,) + block, BF),
            pltpu.VMEM((3,) + block, BF),
            DMA((2, 3)),
            DMA((2, 3)),
        ]
        + Sums.scratch(16, 1024, 1)
        + Sums.scratch(8, 512, 4)
        + Sums.scratch(8, 640, 4),
        compiler_params=params(1),
        name="back",
    )(q, kvx, lse, att, datt, low, xn, wa, rows, go, dmid, tok, gffn, *rope_tables())


def first_keys(segments):
    padded = jnp.concatenate([jnp.full((2 * CHUNK,), -1, jnp.int32), segments])
    keys = lax.dynamic_slice_in_dim(padded, chunk_number() * CHUNK, 3 * CHUNK, 0)
    begins = jnp.sum((keys[:, None] < keys[None, 2 * CHUNK :]).astype(jnp.int32), axis=0)
    low = jnp.maximum(begins, jnp.arange(1, CHUNK + 1, dtype=jnp.int32)).reshape(2, 1, 256)
    return jnp.concatenate([low, low], axis=2)


def local(
    tokens, cotangent, segments, attn_gain, w_query, key_matrix, value_matrix, query_gain, key_gain,
    w_out, ffn_gain, w_gate, w_up, w_down,
):
    low = first_keys(segments)
    gains = jnp.stack(
        [attn_gain, ffn_gain, jnp.broadcast_to(query_gain, (8,)), jnp.broadcast_to(key_gain, (8,))], axis=1
    )
    gains = jnp.pad(gains, ((0, 0), (0, 124)))
    att, cs, wo, wa, rows, xn, q, kvx, lse = front(
        tokens, cotangent, w_query, key_matrix, value_matrix, gains, w_out, low
    )
    output, d_mid, d_att, g_ffn, go, g_gate, g_up, g_down = middle(
        att, tokens, cs, wo.reshape(512, 1024), w_gate, w_up, w_down, rows
    )
    input_grad, g_query, g_key, g_value, g_out, g_gains = back(
        q, kvx, lse, att, d_att, low, xn, wa, rows, go, d_mid, tokens, g_ffn
    )
    return (
        output,
        input_grad,
        g_gains[:, 0],
        g_query,
        g_key,
        g_value,
        g_gains[0, 2:3],
        g_gains[0, 3:4],
        g_out,
        g_gains[:, 1],
        g_gate,
        g_up,
        g_down,
    )


def solution(mesh):
    rows = P(("blk", "head"), None)
    cut = P(("head", "blk"), None)
    vec = P(("head", "blk"))
    return jax.shard_map(
        local,
        mesh=mesh,
        in_specs=(rows, rows, P(), vec, cut, cut, cut, vec, vec, cut, vec, cut, cut, cut),
        out_specs=(rows, rows, vec, cut, cut, cut, vec, vec, cut, vec, cut, cut, cut),
        check_vma=False,
    )
```

```python
import math

import jax
import jax.numpy as jnp
import numpy as np
from jax import lax
from jax.experimental import pallas as pl
from jax.experimental.pallas import tpu as pltpu
from jax.sharding import PartitionSpec as P

HEAD_SIZE = 128
SPAN = 1024
CHUNK = 512
EPS = 1e-06
ROPE_BASE = 1000000.0
MASKED = -1e30
MESH = pl.DeviceIdType.MESH
BF = jnp.bfloat16
F32 = jnp.float32
VMEM = pl.BlockSpec(memory_space=pltpu.VMEM)
DMA = pltpu.SemaphoreType.DMA
VMEM_LIMIT = 62 * 2**20


def coords():
    h = lax.axis_index("head")
    b = lax.axis_index("blk")
    x = 2 * lax.div(h, 4) + lax.div(b, 8)
    return x, lax.rem(h, 4), lax.rem(lax.div(b, 2), 4), lax.rem(b, 2)


def device(x, y, z, c):
    return (lax.div(x, 2) * 4 + y, lax.rem(x, 2) * 8 + z * 2 + c)


def wrap4(v):
    return lax.rem(v + 8, 4)


def send(src, dst, send_sem, recv_sem, to):
    copy = pltpu.make_async_remote_copy(
        src_ref=src, dst_ref=dst, send_sem=send_sem, recv_sem=recv_sem, device_id=to, device_id_type=MESH
    )
    copy.start()
    return copy


def arrived(dst, sem, anyone):
    pltpu.make_async_remote_copy(
        src_ref=dst, dst_ref=dst, send_sem=sem, recv_sem=sem, device_id=anyone, device_id_type=MESH
    ).wait_recv()


def meet(peers):
    barrier = pltpu.get_barrier_semaphore()
    for peer in peers:
        pl.semaphore_signal(barrier, inc=1, device_id=peer, device_id_type=MESH)
    pl.semaphore_wait(barrier, len(peers))


def params(collective_id):
    return pltpu.CompilerParams(
        collective_id=collective_id, has_side_effects=True, vmem_limit_bytes=VMEM_LIMIT
    )


def chunk_number():
    return 2 * lax.axis_index("blk") + lax.div(lax.axis_index("head"), 4)


def chunk_device(step):
    chunk = lax.rem(chunk_number() + step + 32, 32)
    return (lax.rem(chunk, 2) * 4 + lax.rem(lax.axis_index("head"), 4), lax.div(chunk, 2))


def greet_all(chunks=False):
    x, y, z, c = coords()
    peers = [device(x, wrap4(y + k), z, c) for k in range(1, 4)]
    peers += [device(wrap4(x + k), y, z, c) for k in range(1, 4)]
    peers += [device(x, y, wrap4(z + k), c) for k in range(1, 4)]
    peers += [device(x, y, z, 1 - c)]
    if chunks:
        peers += [chunk_device(s) for s in (-2, -1, 1, 2)]
    meet(peers)


def dot(a, b, ca, cb):
    return lax.dot_general(a, b, (((ca,), (cb,)), ((), ())), preferred_element_type=F32)


def rms_scale(rows):
    return lax.rsqrt(jnp.mean(rows * rows, axis=-1, keepdims=True) + EPS)


def rope_tables():
    freq = ROPE_BASE ** (-np.arange(0, HEAD_SIZE, 2, dtype=np.float64) / HEAD_SIZE)
    freq = np.concatenate([freq, freq])
    sign = np.where(np.arange(HEAD_SIZE) < 64, -1.0, 1.0)
    inner = np.arange(CHUNK)[:, None] * freq[None, :]
    outer = (np.arange(32) * CHUNK)[:, None] * freq[None, :]
    tables = [f(a) * s for a in (inner, outer) for f, s in ((np.cos, 1.0), (np.sin, sign))]
    return [jnp.asarray(t.astype(np.float32)) for t in tables]


def rope_here(ic, isn, oc, osn, cos, sin):
    n = chunk_number()
    c0, s0 = oc[pl.ds(n, 1), :], osn[pl.ds(n, 1), :]
    cos[...] = c0 * ic[...] - s0 * isn[...]
    sin[...] = s0 * ic[...] + c0 * isn[...]


def rope(rows, cos, sin):
    return rows * cos + pltpu.roll(rows, 64, 1) * sin


def rope_back(rows, cos, sin):
    return rows * cos + pltpu.roll(rows * sin, 64, 1)


def prep_back(d, raw, gain, cos, sin):
    scale = rms_scale(raw)
    unit = raw * scale
    d = rope_back(d, cos, sin)
    d_gain = jnp.sum(d * unit, axis=0, keepdims=True)
    d = d * gain
    return scale * (d - unit * jnp.mean(d * unit, axis=-1, keepdims=True)), d_gain


REACH = (((0, 512), (256, 256)), ((0, 512), (0, 512)), ((0, 256), (0, 512)))
EXP_SCALE = HEAD_SIZE ** (-0.5) * math.log2(math.e)


def allowed(low, slot, t):
    first, count = REACH[slot][t]
    place = lax.broadcasted_iota(jnp.int32, (count, 512), 0) + (slot * CHUNK + first)
    ok = place >= low[t]
    if slot == 2:
        query = lax.rem(lax.broadcasted_iota(jnp.int32, (1, 512), 1), 256) + (t * 256 + SPAN)
        ok = ok & (place <= query)
    return ok


def attend(q, kvx, low, peak, total, acc, slot, fresh):
    def group(g, _):
        for t in range(2):
            first, count = REACH[slot][t]
            keys = kvx[g, slot, first : first + count]
            values = kvx[2 + g, slot, first : first + count]
            s = dot(keys, q[g, t], 1, 1)
            s = jnp.where(allowed(low, slot, t), s, MASKED)
            top = jnp.max(s, axis=0, keepdims=True)
            if not fresh:
                before = peak[g, t]
                top = jnp.maximum(top, before)
                fade = jnp.exp2((before - top) * EXP_SCALE)
            p = jnp.exp2((s - top) * EXP_SCALE)
            add = jnp.sum(p, axis=0, keepdims=True)
            o = dot(values, p.astype(BF), 0, 0)
            if not fresh:
                add = add + total[g, t] * fade
                o = o + acc[g, t] * fade
            peak[g, t] = top
            total[g, t] = add
            acc[g, t] = o
        return 0

    lax.fori_loop(0, 2, group, 0)


def attend_back(q, kvx, low, lse, do, inner, dq, dkv, slot, fresh):
    def group(g, _):
        for t in range(2):
            first, count = REACH[slot][t]
            rows = slice(first, first + count)
            keys = kvx[g, slot, rows]
            values = kvx[2 + g, slot, rows]
            s = dot(keys, q[g, t], 1, 1)
            p = jnp.where(allowed(low, slot, t), jnp.exp2(s * EXP_SCALE - lse[g, t]), 0.0)
            dp = dot(values, do[g, t], 1, 1)
            ds = (p * (dp - inner[g, t])).astype(BF)
            dv = dot(p.astype(BF), do[g, t], 1, 0)
            dk = dot(ds, q[g, t], 1, 0)
            whole = count == CHUNK
            if whole and (t == 0 or slot == 2):
                other = slice(0, 256)
                if t == 0:
                    dkv[g, slot] = dk
                    dkv[2 + g, slot] = dv
                else:
                    dkv[g, slot, other] = dkv[g, slot, other] + dk[other]
                    dkv[2 + g, slot, other] = dkv[2 + g, slot, other] + dv[other]
                    dkv[g, slot, 256:] = dk[256:]
                    dkv[2 + g, slot, 256:] = dv[256:]
            elif t == 0:
                dkv[g, slot, rows] = dk
                dkv[2 + g, slot, rows] = dv
            else:
                dkv[g, slot, rows] = dkv[g, slot, rows] + dk
                dkv[2 + g, slot, rows] = dkv[2 + g, slot, rows] + dv
            d = dot(keys, ds, 0, 0)
            dq[g, t] = d if fresh else dq[g, t] + d
        return 0

    lax.fori_loop(0, 2, group, 0)


class Pieces:
    def __init__(self, ref, wide, ssem, rsem):
        self.ref, self.wide, self.ssem, self.rsem = ref, wide, ssem, rsem
        self.x, self.y, self.z, self.c = x, y, z, c = coords()
        self.d = 1 - c
        self.across = device(x, y, z, 1 - c)
        self.ring = [device(x, wrap4(y + k), z, c) for k in range(1, 4)]
        self.sends = []

    @staticmethod
    def semaphores():
        return [DMA((34,)), DMA((34,))]

    def slot(self, px, pz, core):
        place = lax.rem(px, 2) * 4 + pz
        if self.wide:
            return self.ref.at[lax.div(px, 2), :, place, core]
        return self.ref.at[lax.div(px, 2), 0, place, core]

    def piece(self, j, k):
        c, d = self.c, self.d
        return self.slot(wrap4(self.x - j * d - k * c), wrap4(self.z - j * c - k * d), c)

    def piece_across(self, j, k):
        c, d = self.c, self.d
        return self.slot(wrap4(self.x - j * c - k * d), wrap4(self.z - j * d - k * c), d)

    def send(self, src, dst, n, to):
        self.sends.append(send(src, dst, self.ssem.at[n], self.rsem.at[n], to))

    def first(self, k):
        return device(wrap4(self.x + k * self.d), self.y, wrap4(self.z + k * self.c), self.c)

    def second(self, k):
        return device(wrap4(self.x + k * self.c), self.y, wrap4(self.z + k * self.d), self.c)

    def to_ring(self, parts):
        place = lax.rem(self.x, 2) * 4 + self.z
        xh = lax.div(self.x, 2)
        self.at_ring = lambda r: self.ref.at[xh, r, place, self.c]
        for k in range(1, 4):
            self.send(parts.at[wrap4(self.y + k)], self.at_ring(self.y), 30 + k, self.ring[k - 1])
        self.ref[xh, self.y, place, self.c] = parts[self.y]

    def from_ring(self):
        for k in range(1, 4):
            arrived(self.at_ring(wrap4(self.y - k)), self.rsem.at[30 + k], self.across)

    def own(self, src=None):
        src = self.piece(0, 0) if src is None else src
        for k in (2, 1, 3):
            self.send(src, self.piece(0, 0), k - 1, self.first(k))
        for k in (2, 1, 3):
            self.send(src, self.piece(0, 0), 2 + k, self.second(k))
        self.send(src, self.piece(0, 0), 15, self.across)

    def pass_on(self, j):
        here = self.piece(j, 0)
        arrived(here, self.rsem.at[j - 1], self.across)
        for k in (2, 1, 3):
            self.send(here, here, 2 + 3 * j + k, self.second(k))
        self.send(here, here, 15 + 4 * j, self.across)

    def pass_across(self, j, k):
        here = self.piece(j, k)
        arrived(here, self.rsem.at[2 + 3 * j + k], self.across)
        self.send(here, here, 15 + 4 * j + k, self.across)

    def pass_all_on(self):
        for j in (1, 3, 2):
            self.pass_on(j)

    def pass_all_across(self):
        for j in (0, 1, 3, 2):
            for k in (1, 3, 2):
                self.pass_across(j, k)

    def all_here(self):
        for j in range(4):
            for k in range(4):
                arrived(self.piece_across(j, k), self.rsem.at[15 + 4 * j + k], self.across)

    def done(self):
        for copy in self.sends:
            copy.wait_send()


def pack_wide(src, dst):
    cols = src.shape[-1]

    def rows(i, _):
        part = src[lax.div(i, 4), lax.rem(i, 4)].astype(F32).reshape(128, cols)
        dst[pl.ds(pl.multiple_of(i * 128, 128), 128)] = part.astype(BF)
        return 0

    lax.fori_loop(0, 8, rows, 0)


def pack_down(src, dst):
    def rows(i, _):
        part = src[lax.div(i, 4), 0, pl.ds(lax.rem(i, 4) * 2, 2)].astype(F32).reshape(96, 1024)
        dst[pl.ds(pl.multiple_of(i * 96, 96), 96)] = part.astype(BF)
        return 0

    lax.fori_loop(0, 8, rows, 0)


class Sums:
    def __init__(self, grad, cols, refs):
        self.grad, self.cols, self.cut = grad, cols, grad.shape[1]
        (self.rc, self.sa, self.lb, self.sb, self.l2, self.sd, self.ry, self.ss, self.rs) = refs
        x, y, z, c = coords()
        self.y, self.c, self.d = y, c, 1 - c
        d = self.d
        self.across = device(x, y, z, d)
        self.ring = [device(x, wrap4(y + k), z, c) for k in range(1, 4)]
        self.to_first = [device(wrap4(x + k * d), y, wrap4(z + k * c), c) for k in range(1, 4)]
        self.to_second = [device(wrap4(x + k * c), y, wrap4(z + k * d), c) for k in range(1, 4)]
        self.p1 = x * d + z * c
        self.p2 = x * c + z * d
        self.sends = []

    @staticmethod
    def scratch(rows, cols, cut):
        buffers = [(2, cut, 8), (4, 4, cut), (3, 4, cut), (4, cut), (3, cut), (cut,), (cut,)]
        return [pltpu.VMEM(lead + (rows, cols), BF) for lead in buffers] + [DMA((10,)), DMA((10,))]

    def start(self):
        self.over = send(self.grad.at[:, :, :, self.d, :, self.cols], self.rc, self.ss.at[9], self.rs.at[9], self.across)
        self.sends.append(self.over)

    def cores(self):
        self.over.wait_recv()
        c, d, cut = self.c, self.d, self.cut

        def add(i, _):
            a2, a1, r = lax.div(i, 4 * cut), lax.rem(lax.div(i, cut), 4), lax.rem(i, cut)
            px, pz = a1 * d + a2 * c, a1 * c + a2 * d
            xh, place = lax.div(px, 2), lax.rem(px, 2) * 4 + pz
            total = self.rc[xh, r, place].astype(F32) + self.grad[xh, r, place, c, :, self.cols].astype(F32)
            self.sa[a2, a1, r] = total.astype(BF)
            return 0

        lax.fori_loop(0, 16 * cut, add, 0)
        self.hop = [
            send(self.sa.at[wrap4(self.p2 + k + 1)], self.lb.at[k], self.ss.at[k], self.rs.at[k], self.to_second[k])
            for k in range(3)
        ]
        self.sends += self.hop

    def second(self):
        for copy in self.hop:
            copy.wait_recv()

        def add(i, _):
            a1, r = lax.div(i, self.cut), lax.rem(i, self.cut)
            total = self.sa[self.p2, a1, r].astype(F32)
            for k in range(3):
                total = total + self.lb[k, a1, r].astype(F32)
            self.sb[a1, r] = total.astype(BF)
            return 0

        lax.fori_loop(0, 4 * self.cut, add, 0)
        self.hop = [
            send(self.sb.at[wrap4(self.p1 + k + 1)], self.l2.at[k], self.ss.at[3 + k], self.rs.at[3 + k], self.to_first[k])
            for k in range(3)
        ]
        self.sends += self.hop

    def first(self, out=None):
        for copy in self.hop:
            copy.wait_recv()
        for r in range(self.cut):
            total = self.sb[self.p1, r].astype(F32)
            for k in range(3):
                total = total + self.l2[k, r].astype(F32)
            if out is not None:
                out[...] = total
            else:
                self.sd[r] = total.astype(BF)
        if out is None:
            y = self.y
            self.hop = [
                send(self.sd.at[wrap4(y + k + 1)], self.ry.at[y], self.ss.at[6 + k], self.rs.at[6 + k], self.ring[k])
                for k in range(3)
            ]
            self.sends += self.hop
            self.ry[y] = self.sd[y]

    def owners(self):
        for copy in self.hop:
            copy.wait_recv()

    def done(self):
        for copy in self.sends:
            copy.wait_send()


def layer_kernel(
    tok, cot, wq, wk, wv, wg, wu, gains, wop, wdp, low, ic, isn, oc, osn,
    out, igrad, oq, ok, ov, og, ou, oo, od, ogain,
    aparts, bparts, wal, wbl, wdl, wol, wa, wb, wd, xs, cs, cos, sin, rows, xn, q, kvx, lse, peak, total, wide, att,
    part, land1, acc, unit, dhid, dgu, hid, dpart, land2, dbr, opart, land3, dmid, datt, go,
    do, inner, dkv, dkvb, land, dqkv, grow, ssem, rsem, hsem, hrem, *scratch,
):
    x, y, z, c = coords()
    ring = [device(x, wrap4(y + k), z, c) for k in range(1, 4)]
    take = lambda n: [scratch.pop(0) for _ in range(n)]
    scratch = list(scratch)
    a, b, o, w = [Pieces(ref, n < 2, *take(2)) for n, ref in enumerate((wal, wbl, wol, wdl))]
    sq = Sums(wal, slice(0, 512), take(9))
    sk = Sums(wal, slice(512, 1152), take(9))
    sb = Sums(wbl, slice(0, 1536), take(9))
    so = Sums(go, slice(0, 1024), take(9))
    sd = Sums(wdl, slice(0, 1024), take(9))
    sends = []

    def ring_send(n, k, src, dst):
        sends.append(send(src, dst, ssem.at[n, k - 1], rsem.at[n, k - 1], ring[k - 1]))
        return sends[-1]

    def ring_wait(n, k, dst):
        arrived(dst, rsem.at[n, k - 1], ring[0])

    for r in range(4):
        for g in range(2):
            h = g * 4 + r
            aparts[r, :, g * 256 : g * 256 + 256] = wq[:, h * 256 : h * 256 + 256]
            aparts[r, :, 512 + g * 128 : 640 + g * 128] = wk[:, h * 128 : h * 128 + 128]
            aparts[r, :, 768 + g * 128 : 896 + g * 128] = wv[:, h * 128 : h * 128 + 128]
            bparts[r, :, g * 384 : g * 384 + 384] = wg[:, h * 384 : h * 384 + 384]
            bparts[r, :, 768 + g * 384 : 1152 + g * 384] = wu[:, h * 384 : h * 384 + 384]
        aparts[r, :, 1024:1152] = gains[...]
    greet_all(True)
    a.to_ring(aparts)
    for k in (2, 1, 3):
        ring_send(0, k, tok, xs.at[y])
    place = lax.rem(x, 2) * 4 + z
    wol[lax.div(x, 2), 0, place, c] = wop[...]
    wdl[lax.div(x, 2), 0, place, c] = wdp[...]
    xs[y] = tok[...]
    cs[y] = cot[...]
    rope_here(ic, isn, oc, osn, cos, sin)
    a.from_ring()
    a.own()
    a.pass_all_on()
    o.own()
    for k in (1, 3, 2):
        ring_wait(0, k, xs.at[wrap4(y - k)])
    b.to_ring(bparts)
    for k in (2, 1, 3):
        ring_send(1, k, cot, cs.at[y])
    a.pass_all_across()
    o.pass_all_on()
    a.all_here()
    pack_wide(wal, wa)

    pick = lax.broadcasted_iota(jnp.int32, (8, 128), 0) == lax.broadcasted_iota(jnp.int32, (8, 128), 1)
    by_row = dot(pick.astype(F32).astype(BF), wa[:, 1024:1152], 1, 1)
    rows[:, :1024] = by_row
    every = lax.broadcasted_iota(jnp.int32, (1024, 128), 0) == 8 * lax.broadcasted_iota(jnp.int32, (1024, 128), 1)
    rows[:, 1024:] = dot(by_row.astype(BF), every.astype(F32).astype(BF), 1, 0)
    attn_gain, ffn_gain = rows[0:1, :1024], rows[1:2, :1024]
    q_gain, k_gain = rows[2:3, 1024:], rows[3:4, 1024:]

    for r in range(4):
        block = xs[r].astype(F32)
        xn[r * 128 : r * 128 + 128] = (block * rms_scale(block) * attn_gain).astype(BF)
    raw = dot(xn[...], wa[:, 512:768], 1, 0)
    for g in range(2):
        k_raw = raw[:, g * 128 : g * 128 + 128]
        kvx[g, 2] = rope(k_raw * rms_scale(k_raw) * k_gain, cos[...], sin[...]).astype(BF)
    raw = dot(xn[...], wa[:, 768:1024], 1, 0)
    for g in range(2):
        kvx[2 + g, 2] = raw[:, g * 128 : g * 128 + 128].astype(BF)
    near = send(kvx.at[:, 2], kvx.at[:, 1], hsem.at[0], hrem.at[0], chunk_device(1))
    far = send(kvx.at[:, 2], kvx.at[:, 0], hsem.at[1], hrem.at[1], chunk_device(2))
    sends += [near, far]

    def queries(g, _):
        raw = dot(xn[...], wa[:, pl.ds(pl.multiple_of(g * 256, 256), 256)], 1, 0)
        for hd in range(2):
            q_raw = raw[:, hd * 128 : hd * 128 + 128]
            rot = rope(q_raw * rms_scale(q_raw) * q_gain, cos[...], sin[...]).astype(BF)
            for t in range(2):
                q[g, t, hd * 256 : hd * 256 + 256] = rot[t * 256 : t * 256 + 256]
        return 0

    lax.fori_loop(0, 2, queries, 0)

    o.pass_all_across()
    b.from_ring()
    b.own()
    w.own()
    attend(q, kvx, low, peak, total, wide, 2, True)
    near.wait_recv()
    attend(q, kvx, low, peak, total, wide, 1, False)
    b.pass_all_on()
    w.pass_all_on()
    far.wait_recv()
    attend(q, kvx, low, peak, total, wide, 0, False)
    for g in range(2):
        for t in range(2):
            done = jnp.transpose(wide[g, t] / total[g, t]).astype(BF)
            lse[g, t] = peak[g, t] * EXP_SCALE + jnp.log(total[g, t]) * math.log2(math.e)
            for hd in range(2):
                cols = slice((g * 2 + hd) * 128, (g * 2 + hd) * 128 + 128)
                for half in range(2):
                    first = hd * 256 + half * 128
                    att[2 * t + half, :, cols] = done[first : first + 128]

    o.all_here()
    wo = lambda: wol[...].reshape(512, 1024)
    first_sends = []
    for k in (2, 1, 3, 0):
        p = dot(att[wrap4(y + k)], wo(), 1, 0)
        if k:
            part[k - 1] = p.astype(BF)
            first_sends.append(ring_send(2, k, part.at[k - 1], land1.at[k - 1]))
        else:
            acc[...] = p + tok[...].astype(F32)
    b.pass_all_across()
    w.pass_all_across()
    w.all_here()
    pack_down(wdl, wd)
    for k in (1, 3, 2):
        ring_wait(1, k, cs.at[wrap4(y - k)])
    for k in (1, 3, 2):
        ring_wait(2, k, land1.at[k - 1])
    s = acc[...]
    for k in range(3):
        s = s + land1[k].astype(F32)
    acc[...] = s
    scale = rms_scale(s)
    unit[...] = s * scale
    mid = xs
    mid[y] = (s * scale * ffn_gain).astype(BF)
    for k in (2, 1, 3):
        ring_send(3, k, mid.at[y], mid.at[y])
    for r in range(4):
        dhid[r] = dot(cs[r], wd[...], 1, 1)
    b.all_here()
    pack_wide(wbl, wb)

    for k in (0, 1, 3, 2):
        r = wrap4(y - k)
        if k:
            ring_wait(3, k, mid.at[r])
        gu = dot(mid[r], wb[...], 1, 0)
        gate, up = gu[:, :768], gu[:, 768:]
        sig = 1.0 / (1.0 + jnp.exp(-gate))
        act = gate * sig
        dh = dhid[r]
        hid[r] = (act * up).astype(BF)
        dgu[r, :, :768] = (dh * up * sig * (1.0 + gate * (1.0 - sig))).astype(BF)
        dgu[r, :, 768:] = (dh * act).astype(BF)
        p = dot(dgu[r], wb[...], 1, 1)
        if k:
            dpart[k - 1] = p.astype(BF)
            ring_send(4, 4 - k, dpart.at[k - 1], land2.at[3 - k])
        else:
            dmid[...] = p
    b.done()
    w.done()

    def gate_up_rows(f, _):
        span = pl.ds(pl.multiple_of(f * 128, 128), 128)
        lhs = mid[:, :, span].reshape(CHUNK, 128)
        g = dot(lhs, dgu[...].reshape(CHUNK, 1536), 0, 0)
        wbl[lax.div(f, 4), lax.rem(f, 4)] = g.reshape(8, 2, 8, 1536).astype(BF)
        return 0

    lax.fori_loop(0, 8, gate_up_rows, 0)
    sb.start()

    for k in (1, 3, 2):
        ring_wait(4, k, land2.at[k - 1])
    s = dmid[...]
    for k in range(3):
        s = s + land2[k].astype(F32)
    grow[...] = jnp.zeros_like(grow)
    grow[1:2] = jnp.sum(s * unit[...], axis=0, keepdims=True)
    s = s * ffn_gain
    mean = jnp.mean(s * unit[...], axis=-1, keepdims=True)
    s = cs[y].astype(F32) + rms_scale(acc[...]) * (s - unit[...] * mean)
    dmid[...] = s
    dbr[y] = s.astype(BF)
    for k in (2, 1, 3):
        ring_send(5, k, dbr.at[y], dbr.at[y])

    def down_rows(f, _):
        span = pl.ds(pl.multiple_of(f * 384, 384), 384)
        lhs = hid[:, :, span].reshape(CHUNK, 384)
        g = dot(lhs, cs[...].reshape(CHUNK, 1024), 0, 0)
        wdl[f, 0] = g.reshape(8, 2, 24, 1024).astype(BF)
        return 0

    lax.fori_loop(0, 2, down_rows, 0)
    sd.start()
    sb.cores()
    for k in (2, 1, 3, 0):
        p = dot(hid[wrap4(y + k)], wd[...], 1, 0)
        if k:
            opart[k - 1] = p.astype(BF)
        else:
            acc[...] = acc[...] + p
    sd.cores()
    for k in (0, 1, 3, 2):
        r = wrap4(y - k)
        if k:
            ring_wait(5, k, dbr.at[r])
        datt[r] = dot(dbr[r], wo(), 1, 1).astype(BF)
    for k in (2, 1, 3):
        ring_send(6, k, opart.at[k - 1], land3.at[k - 1])

    ones = jnp.ones((8, 128), BF)
    for g in range(2):
        for t in range(2):
            for hd in range(2):
                cols = slice((g * 2 + hd) * 128, (g * 2 + hd) * 128 + 128)
                for half in range(2):
                    first = hd * 256 + half * 128
                    d = datt[2 * t + half, :, cols]
                    do[g, t, first : first + 128] = d
                    prod = d.astype(F32) * att[2 * t + half, :, cols].astype(F32)
                    high = prod.astype(BF)
                    rest = (prod - high.astype(F32)).astype(BF)
                    inner[g, t, :, first : first + 128] = (dot(ones, high, 1, 1) + dot(ones, rest, 1, 1))[:1]
    dq = wide
    attend_back(q, kvx, low, lse, do, inner, dq, dkv, 0, True)
    dkvb[:, 0] = dkv[:, 0].astype(BF)
    back_far = send(dkvb.at[:, 0], land.at[0], hsem.at[2], hrem.at[2], chunk_device(-2))
    attend_back(q, kvx, low, lse, do, inner, dq, dkv, 1, False)
    dkvb[:, 1] = dkv[:, 1].astype(BF)
    back_near = send(dkvb.at[:, 1], land.at[1], hsem.at[3], hrem.at[3], chunk_device(-1))
    sends += [back_far, back_near]

    def out_rows(f, _):
        span = pl.ds(pl.multiple_of(f * 256, 256), 256)
        lhs = att[:, :, span].reshape(CHUNK, 256)
        g = dot(lhs, dbr[...].reshape(CHUNK, 1024), 0, 0)
        go[f, 0] = g.reshape(8, 2, 16, 1024).astype(BF)
        return 0

    lax.fori_loop(0, 2, out_rows, 0)
    so.start()
    sb.second()
    sd.second()
    attend_back(q, kvx, low, lse, do, inner, dq, dkv, 2, False)

    scale = HEAD_SIZE ** (-0.5)
    raw = dhid
    raw[...] = dot(xn[...], wa[:, :768], 1, 0).reshape(4, 128, 768)
    a.done()
    g_q = jnp.zeros((1, 128), F32)
    for g in range(2):
        for t in range(2):
            d = jnp.transpose(dq[g, t] * scale).astype(BF).astype(F32)
            span = slice(t * 256, t * 256 + 256)
            for hd in range(2):
                cols = slice((g * 2 + hd) * 128, (g * 2 + hd) * 128 + 128)
                q_raw = raw[2 * t : 2 * t + 2, :, cols].reshape(256, 128)
                d_raw, d_gain = prep_back(d[hd * 256 : hd * 256 + 256], q_raw, q_gain, cos[span], sin[span])
                dqkv[span, cols] = d_raw.astype(BF)
                g_q = g_q + d_gain

    def query_rows(f, _):
        lhs = xn[:, pl.ds(pl.multiple_of(f * 128, 128), 128)]
        g = dot(lhs, dqkv[:, :512], 0, 0)
        wal[lax.div(f, 4), lax.rem(f, 4), :, :, :, :512] = g.reshape(8, 2, 8, 512).astype(BF)
        return 0

    lax.fori_loop(0, 8, query_rows, 0)
    sq.start()
    so.cores()
    sb.first()
    sd.first(od)
    for k in (1, 3, 2):
        ring_wait(6, k, land3.at[k - 1])
    s = acc[...]
    for k in range(3):
        s = s + land3[k].astype(F32)
    out[...] = s.astype(BF)
    back_far.wait_recv()
    back_near.wait_recv()
    g_k = jnp.zeros((1, 128), F32)
    for g in range(2):
        d = dkv[g, 2] + land[0, g].astype(F32) + land[1, g].astype(F32)
        d = (d * scale).astype(BF).astype(F32)
        cols = slice(512 + g * 128, 640 + g * 128)
        k_raw = raw[:, :, cols].reshape(CHUNK, 128)
        d_raw, d_gain = prep_back(d, k_raw, k_gain, cos[...], sin[...])
        dqkv[:, cols] = d_raw.astype(BF)
        g_k = g_k + d_gain
        d = dkv[2 + g, 2] + land[0, 2 + g].astype(F32) + land[1, 2 + g].astype(F32)
        dqkv[:, 768 + g * 128 : 896 + g * 128] = d.astype(BF)

    for copy in first_sends:
        copy.wait_send()
    sends[:] = [copy for copy in sends if all(copy is not s for s in first_sends)]
    g_x = jnp.zeros((1, 1024), F32)
    for k in (2, 1, 3, 0):
        span = pl.ds(pl.multiple_of(wrap4(y + k) * 128, 128), 128)
        p = dot(dqkv[span], wa[:, :1024], 1, 1)
        g_x = g_x + jnp.sum(p * xn[span].astype(F32), axis=0, keepdims=True)
        if k:
            part[k - 1] = p.astype(BF)
            ring_send(7, k, part.at[k - 1], land1.at[k - 1])
        else:
            acc[...] = p
    eight = lax.div(lax.broadcasted_iota(jnp.int32, (128, 1024), 1), 8) == lax.broadcasted_iota(jnp.int32, (128, 1024), 0)
    eight = eight.astype(F32).astype(BF)
    grow[0:1] = g_x / attn_gain
    grow[2:3] = dot(jnp.broadcast_to(g_q, (8, 128)).astype(BF), eight, 1, 0)[:1]
    grow[3:4] = dot(jnp.broadcast_to(g_k, (8, 128)).astype(BF), eight, 1, 0)[:1]

    def key_rows(f, _):
        span = pl.ds(pl.multiple_of(f * 128, 128), 128)
        g = dot(xn[:, span], dqkv[:, 512:], 0, 0)
        at = (lax.div(f, 4), lax.rem(f, 4))
        wal[at[0], at[1], :, :, :, 512:1024] = g.reshape(8, 2, 8, 512).astype(BF)
        wal[at[0], at[1], :, :, :, 1024:] = jnp.transpose(grow[:, span]).reshape(8, 2, 8, 128).astype(BF)
        return 0

    lax.fori_loop(0, 8, key_rows, 0)
    sk.start()
    sq.cores()
    sk.cores()
    so.second()
    sb.owners()
    for r in range(4):
        for g in range(2):
            h = g * 4 + r
            og[:, h * 384 : h * 384 + 384] = sb.ry[r, :, g * 384 : g * 384 + 384].astype(F32)
            ou[:, h * 384 : h * 384 + 384] = sb.ry[r, :, 768 + g * 384 : 1152 + g * 384].astype(F32)
    sq.second()
    sk.second()
    so.first(oo)
    for k in (1, 3, 2):
        ring_wait(7, k, land1.at[k - 1])
    s = acc[...]
    for k in range(3):
        s = s + land1[k].astype(F32)
    own = tok[...].astype(F32)
    scale_own = rms_scale(own)
    own = own * scale_own
    s = s * attn_gain
    mean = jnp.mean(s * own, axis=-1, keepdims=True)
    igrad[...] = (dmid[...] + scale_own * (s - own * mean)).astype(BF)
    sq.first()
    sk.first()
    sq.owners()
    sk.owners()
    gain = jnp.zeros((8, 128), F32)
    for r in range(4):
        for g in range(2):
            h = g * 4 + r
            oq[:, h * 256 : h * 256 + 256] = sq.ry[r, :, g * 256 : g * 256 + 256].astype(F32)
            ok[:, h * 128 : h * 128 + 128] = sk.ry[r, :, g * 128 : g * 128 + 128].astype(F32)
            ov[:, h * 128 : h * 128 + 128] = sk.ry[r, :, 256 + g * 128 : 384 + g * 128].astype(F32)
        gain = gain + sk.ry[r, :, 512:640].astype(F32)
    ogain[...] = gain
    for copy in sends:
        copy.wait_send()
    for s in (o, sq, sk, sb, so, sd):
        s.done()


def whole_layer(tok, cot, wq, wk, wv, wg, wu, gains, wo, wd, low):
    sds = jax.ShapeDtypeStruct
    block = (128, 1024)
    mem = lambda *shape: pltpu.VMEM(shape, BF)
    mem32 = lambda *shape: pltpu.VMEM(shape, F32)
    return pl.pallas_call(
        layer_kernel,
        out_shape=(
            sds(block, BF),
            sds(block, BF),
            sds((8, 2048), F32),
            sds((8, 1024), F32),
            sds((8, 1024), F32),
            sds((8, 3072), F32),
            sds((8, 3072), F32),
            sds((16, 1024), F32),
            sds((24, 1024), F32),
            sds((8, 128), F32),
        ),
        in_specs=[VMEM] * 15,
        out_specs=(VMEM,) * 10,
        scratch_shapes=[
            mem(4, 8, 1152),
            mem(4, 8, 1536),
            mem(2, 4, 8, 2, 8, 1152),
            mem(2, 4, 8, 2, 8, 1536),
            mem(2, 1, 8, 2, 24, 1024),
            mem(2, 1, 8, 2, 16, 1024),
            mem(1024, 1152),
            mem(1024, 1536),
            mem(768, 1024),
            mem(4, *block),
            mem(4, *block),
            mem32(CHUNK, 128),
            mem32(CHUNK, 128),
            mem32(8, 1152),
            mem(CHUNK, 1024),
            mem(2, 2, 512, 128),
            mem(4, 3, CHUNK, 128),
            mem32(2, 2, 1, 512),
            mem32(2, 2, 1, 512),
            mem32(2, 2, 1, 512),
            mem32(2, 2, 128, 512),
            mem(4, 128, 512),
            mem(3, *block),
            mem(3, *block),
            mem32(*block),
            mem32(*block),
            mem32(4, 128, 768),
            mem(4, 128, 1536),
            mem(4, 128, 768),
            mem(3, *block),
            mem(3, *block),
            mem(4, *block),
            mem(3, *block),
            mem(3, *block),
            mem32(*block),
            mem(4, 128, 512),
            mem(2, 1, 8, 2, 16, 1024),
            mem(2, 2, 512, 128),
            mem32(2, 2, 1, 512),
            mem32(4, 3, CHUNK, 128),
            mem(4, 2, CHUNK, 128),
            mem(2, 4, CHUNK, 128),
            mem(CHUNK, 1024),
            mem32(128, 1024),
            DMA((8, 3)),
            DMA((8, 3)),
            DMA((4,)),
            DMA((4,)),
        ]
        + Pieces.semaphores() * 4
        + Sums.scratch(8, 512, 4)
        + Sums.scratch(8, 640, 4)
        + Sums.scratch(8, 1536, 4)
        + Sums.scratch(16, 1024, 1)
        + Sums.scratch(24, 1024, 1),
        compiler_params=params(0),
        name="whole_layer",
    )(tok, cot, wq, wk, wv, wg, wu, gains, wo, wd, low, *rope_tables())


def results_kernel(*refs):
    half = len(refs) // 2
    for src, dst in zip(refs[:half], refs[half:]):
        dst[...] = src[...]


def results(*arrays):
    return pl.pallas_call(
        results_kernel,
        out_shape=tuple(jax.ShapeDtypeStruct(r.shape, r.dtype) for r in arrays),
        in_specs=[VMEM] * len(arrays),
        out_specs=(VMEM,) * len(arrays),
        name="results",
    )(*arrays)


def first_keys(segments):
    padded = jnp.concatenate([jnp.full((2 * CHUNK,), -1, jnp.int32), segments])
    keys = lax.dynamic_slice_in_dim(padded, chunk_number() * CHUNK, 3 * CHUNK, 0)
    begins = jnp.sum((keys[:, None] < keys[None, 2 * CHUNK :]).astype(jnp.int32), axis=0)
    low = jnp.maximum(begins, jnp.arange(1, CHUNK + 1, dtype=jnp.int32)).reshape(2, 1, 256)
    return jnp.concatenate([low, low], axis=2)


def local(
    tokens, cotangent, segments, attn_gain, w_query, key_matrix, value_matrix, query_gain, key_gain,
    w_out, ffn_gain, w_gate, w_up, w_down,
):
    low = first_keys(segments)
    gains = jnp.stack(
        [attn_gain, ffn_gain, jnp.broadcast_to(query_gain, (8,)), jnp.broadcast_to(key_gain, (8,))], axis=1
    )
    gains = jnp.pad(gains, ((0, 0), (0, 124)))
    output, input_grad, g_query, g_key, g_value, g_gate, g_up, g_out, g_down, g_gains = results(
        *whole_layer(
            tokens, cotangent, w_query, key_matrix, value_matrix, w_gate, w_up, gains, w_out, w_down, low
        )
    )
    return (
        output,
        input_grad,
        g_gains[:, 0],
        g_query,
        g_key,
        g_value,
        g_gains[0, 2:3],
        g_gains[0, 3:4],
        g_out,
        g_gains[:, 1],
        g_gate,
        g_up,
        g_down,
    )


def solution(mesh):
    rows = P(("blk", "head"), None)
    cut = P(("head", "blk"), None)
    vec = P(("head", "blk"))
    return jax.shard_map(
        local,
        mesh=mesh,
        in_specs=(rows, rows, P(), vec, cut, cut, cut, vec, vec, cut, vec, cut, cut, cut),
        out_specs=(rows, rows, vec, cut, cut, cut, vec, vec, cut, vec, cut, cut, cut),
        check_vma=False,
    )
```

```python
import math

import jax
import jax.numpy as jnp
import numpy as np
from jax import lax
from jax.experimental import pallas as pl
from jax.experimental.pallas import tpu as pltpu
from jax.sharding import PartitionSpec as P

HEAD_SIZE = 128
SPAN = 1024
CHUNK = 512
EPS = 1e-06
ROPE_BASE = 1000000.0
MASKED = -1e30
MESH = pl.DeviceIdType.MESH
BF = jnp.bfloat16
F32 = jnp.float32
VMEM = pl.BlockSpec(memory_space=pltpu.VMEM)
SMEM = pl.BlockSpec(memory_space=pltpu.SMEM)
DMA = pltpu.SemaphoreType.DMA
VMEM_LIMIT = 62 * 2**20


def coords():
    h = lax.axis_index("head")
    b = lax.axis_index("blk")
    x = 2 * lax.div(h, 4) + lax.div(b, 8)
    return x, lax.rem(h, 4), lax.rem(lax.div(b, 2), 4), lax.rem(b, 2)


def device(x, y, z, c):
    return (lax.div(x, 2) * 4 + y, lax.rem(x, 2) * 8 + z * 2 + c)


def wrap4(v):
    return lax.rem(v + 8, 4)


def send(src, dst, send_sem, recv_sem, to):
    copy = pltpu.make_async_remote_copy(
        src_ref=src, dst_ref=dst, send_sem=send_sem, recv_sem=recv_sem, device_id=to, device_id_type=MESH
    )
    copy.start()
    return copy


def arrived(dst, sem, anyone):
    pltpu.make_async_remote_copy(
        src_ref=dst, dst_ref=dst, send_sem=sem, recv_sem=sem, device_id=anyone, device_id_type=MESH
    ).wait_recv()


def greet(peers):
    barrier = pltpu.get_barrier_semaphore()
    for peer in peers:
        pl.semaphore_signal(barrier, inc=1, device_id=peer, device_id_type=MESH)
    return lambda: pl.semaphore_wait(barrier, len(peers))


def params(collective_id):
    return pltpu.CompilerParams(
        collective_id=collective_id, has_side_effects=True, vmem_limit_bytes=VMEM_LIMIT
    )


def chunk_number():
    return 2 * lax.axis_index("blk") + lax.div(lax.axis_index("head"), 4)


def chunk_device(step):
    chunk = lax.rem(chunk_number() + step + 32, 32)
    return (lax.rem(chunk, 2) * 4 + lax.rem(lax.axis_index("head"), 4), lax.div(chunk, 2))


def greet_all():
    x, y, z, c = coords()
    peers = [device(x, y, z, 1 - c)]
    for j in range(4):
        for r in range(4):
            if j or r:
                peers.append(device(wrap4(x + j * (1 - c)), wrap4(y + r), wrap4(z + j * c), c))
    peers += [device(wrap4(x + k * c), y, wrap4(z + k * (1 - c)), c) for k in range(1, 4)]
    return greet(peers + [chunk_device(s) for s in (-2, -1, 1, 2)])


def dot(a, b, ca, cb):
    return lax.dot_general(a, b, (((ca,), (cb,)), ((), ())), preferred_element_type=F32)


def rms_scale(rows):
    return lax.rsqrt(jnp.mean(rows * rows, axis=-1, keepdims=True) + EPS)


def rope_tables():
    freq = ROPE_BASE ** (-np.arange(0, HEAD_SIZE, 2, dtype=np.float64) / HEAD_SIZE)
    freq = np.concatenate([freq, freq])
    sign = np.where(np.arange(HEAD_SIZE) < 64, -1.0, 1.0)
    inner = np.arange(CHUNK)[:, None] * freq[None, :]
    outer = (np.arange(32) * CHUNK)[:, None] * freq[None, :]
    tables = [f(a) * s for a in (inner, outer) for f, s in ((np.cos, 1.0), (np.sin, sign))]
    return [jnp.asarray(t.astype(np.float32)) for t in tables]


def rope_here(ic, isn, oc, osn, cos, sin):
    n = chunk_number()
    c0, s0 = oc[pl.ds(n, 1), :], osn[pl.ds(n, 1), :]
    cos[...] = c0 * ic[...] - s0 * isn[...]
    sin[...] = s0 * ic[...] + c0 * isn[...]


def rope(rows, cos, sin):
    return rows * cos + pltpu.roll(rows, 64, 1) * sin


def rope_back(rows, cos, sin):
    return rows * cos + pltpu.roll(rows * sin, 64, 1)


def prep_back(d, raw, gain, cos, sin):
    scale = rms_scale(raw)
    unit = raw * scale
    d = rope_back(d, cos, sin)
    d_gain = jnp.sum(d * unit, axis=0, keepdims=True)
    d = d * gain
    return scale * (d - unit * jnp.mean(d * unit, axis=-1, keepdims=True)), d_gain


def first_keys(seg, low):
    start = chunk_number() * 4 - 8
    rows = []
    for i in range(12):
        row = seg[pl.ds(jnp.maximum(start + i, 0), 1), :].astype(F32)
        rows.append(jnp.where(start + i < 0, -1.0, row))
    keys = jnp.transpose(jnp.concatenate(rows + [jnp.zeros((116, 128), F32)], axis=0))
    for t in range(2):
        for half in range(2):
            query = rows[8 + 2 * t + half]
            begins = jnp.zeros((1, 128), F32)
            for i in range(12):
                before = jnp.where(keys[:, i : i + 1] < query, 1.0, 0.0)
                begins = begins + jnp.sum(before, axis=0, keepdims=True)
            row = lax.broadcasted_iota(jnp.int32, (1, 128), 1) + (t * 256 + half * 128 + 1)
            for hd in range(2):
                at = hd * 256 + half * 128
                low[t, :, at : at + 128] = jnp.maximum(begins.astype(jnp.int32), row)


def gain_tile(gains):
    row = lax.broadcasted_iota(jnp.int32, (8, 128), 0)
    col = lax.broadcasted_iota(jnp.int32, (8, 128), 1)
    tile = jnp.where(col == 2, gains[16], jnp.where(col == 3, gains[17], 0.0))
    for i in range(8):
        tile = jnp.where((row == i) & (col == 0), gains[i], tile)
        tile = jnp.where((row == i) & (col == 1), gains[8 + i], tile)
    return tile.astype(BF)


REACH = (((0, 512), (256, 256)), ((0, 512), (0, 512)), ((0, 256), (0, 512)))
EXP_SCALE = HEAD_SIZE ** (-0.5) * math.log2(math.e)


def allowed(low, slot, t):
    first, count = REACH[slot][t]
    place = lax.broadcasted_iota(jnp.int32, (count, 512), 0) + (slot * CHUNK + first)
    ok = place >= low[t]
    if slot == 2:
        query = lax.rem(lax.broadcasted_iota(jnp.int32, (1, 512), 1), 256) + (t * 256 + SPAN)
        ok = ok & (place <= query)
    return ok


def attend(q, kvx, low, peak, total, acc, slot, fresh):
    def group(g, _):
        for t in range(2):
            first, count = REACH[slot][t]
            keys = kvx[2 * g, slot, first : first + count]
            values = kvx[2 * g + 1, slot, first : first + count]
            s = dot(keys, q[g, t], 1, 1)
            s = jnp.where(allowed(low, slot, t), s, MASKED)
            top = jnp.max(s, axis=0, keepdims=True)
            if not fresh:
                before = peak[g, t]
                top = jnp.maximum(top, before)
                fade = jnp.exp2((before - top) * EXP_SCALE)
            p = jnp.exp2((s - top) * EXP_SCALE)
            add = jnp.sum(p, axis=0, keepdims=True)
            o = dot(values, p.astype(BF), 0, 0)
            if not fresh:
                add = add + total[g, t] * fade
                o = o + acc[g, t] * fade
            peak[g, t] = top
            total[g, t] = add
            acc[g, t] = o
        return 0

    lax.fori_loop(0, 2, group, 0)


def attend_back(q, kvx, low, lse, do, inner, dq, dkv, slot, fresh, after=None):
    def group(g, _):
        for t in range(2):
            first, count = REACH[slot][t]
            rows = slice(first, first + count)
            keys = kvx[2 * g, slot, rows]
            values = kvx[2 * g + 1, slot, rows]
            s = dot(keys, q[g, t], 1, 1)
            p = jnp.where(allowed(low, slot, t), jnp.exp2(s * EXP_SCALE - lse[g, t]), 0.0)
            dp = dot(values, do[g, t], 1, 1)
            ds = (p * (dp - inner[g, t])).astype(BF)
            dv = dot(p.astype(BF), do[g, t], 1, 0)
            dk = dot(ds, q[g, t], 1, 0)
            for n, d in ((2 * g, dk), (2 * g + 1, dv)):
                if t == 0:
                    dkv[n, slot, rows] = d
                elif slot == 2:
                    dkv[n, slot, :256] = dkv[n, slot, :256] + d[:256]
                    dkv[n, slot, 256:] = d[256:]
                else:
                    dkv[n, slot, rows] = dkv[n, slot, rows] + d
            d = dot(keys, ds, 0, 0)
            dq[g, t] = d if fresh else dq[g, t] + d
        return 0

    if after is None:
        lax.fori_loop(0, 2, group, 0)
    else:
        for g in range(2):
            group(g, 0)
            after(g)


LOW, HIGH = pl.ds(0, 64), pl.ds(64, 64)


class Ring:
    def __init__(self, ssem, rsem):
        x, self.y, z, c = coords()
        self.next = device(x, wrap4(self.y + 1), z, c)
        self.last = device(x, wrap4(self.y + 3), z, c)
        self.ssem, self.rsem = ssem, rsem
        self.sends = []

    def send(self, n, src, dst, to):
        self.sends.append(send(src, dst, self.ssem.at[n], self.rsem.at[n], to))

    def wait(self, n, dst):
        arrived(dst, self.rsem.at[n], self.next)

    def done(self):
        for copy in self.sends:
            copy.wait_send()
        self.sends = []


class RingGather(Ring):
    def __init__(self, ref, ssem, rsem):
        super().__init__(ssem, rsem)
        self.ref = ref

    def half(self, back, rows):
        return self.ref.at[wrap4(self.y - back), rows]

    def start(self):
        low, high = self.half(0, LOW), self.half(0, HIGH)
        self.send(0, low, low, self.next)
        self.send(1, high, high, self.last)
        self.send(2, high, high, self.next)
        self.send(3, low, low, self.last)

    def pass_on(self):
        low, high = self.half(1, LOW), self.half(3, HIGH)
        self.wait(0, low)
        self.send(4, low, low, self.next)
        self.wait(1, high)
        self.send(5, high, high, self.last)

    def block(self, back):
        if back == 1:
            self.wait(2, self.half(1, HIGH))
        elif back == 3:
            self.wait(3, self.half(3, LOW))
        elif back == 2:
            self.wait(4, self.half(2, LOW))
            self.wait(5, self.half(2, HIGH))


class RingSum(Ring):
    def __init__(self, part, relayed, landed, ssem, rsem):
        super().__init__(ssem, rsem)
        self.part, self.relayed, self.landed = part, relayed, landed

    def give(self, k):
        part = self.part.at[k - 1]
        if k == 2:
            self.send(0, part.at[LOW], self.relayed.at[0], self.next)
            self.send(1, part.at[HIGH], self.relayed.at[1], self.last)
        elif k == 1:
            self.send(2, part.at[HIGH], self.landed.at[0, HIGH], self.next)
        else:
            self.send(3, part.at[LOW], self.landed.at[1, LOW], self.last)

    def relay(self):
        part, relayed, landed = self.part, self.relayed, self.landed
        self.wait(0, relayed.at[0])
        part[0, :64] = (part[0, :64].astype(F32) + relayed[0].astype(F32)).astype(BF)
        self.send(4, part.at[0, LOW], landed.at[0, LOW], self.next)
        self.wait(1, relayed.at[1])
        part[2, 64:] = (part[2, 64:].astype(F32) + relayed[1].astype(F32)).astype(BF)
        self.send(5, part.at[2, HIGH], landed.at[1, HIGH], self.last)

    def total(self, own):
        landed = self.landed
        self.wait(2, landed.at[0, HIGH])
        self.wait(3, landed.at[1, LOW])
        self.wait(4, landed.at[0, LOW])
        self.wait(5, landed.at[1, HIGH])
        return own + landed[0].astype(F32) + landed[1].astype(F32)


class Pieces:
    def __init__(self, ref, ssem, rsem):
        self.ref, self.wide, self.ssem, self.rsem = ref, ref.shape[1] == 4, ssem, rsem
        self.x, self.y, self.z, self.c = x, y, z, c = coords()
        self.d = 1 - c
        self.across = device(x, y, z, 1 - c)
        self.sends = []

    @staticmethod
    def semaphores():
        return [DMA((44,)), DMA((44,))]

    def slot(self, px, pz, core):
        place = lax.rem(px, 2) * 4 + pz
        if self.wide:
            return self.ref.at[lax.div(px, 2), :, place, core]
        return self.ref.at[lax.div(px, 2), 0, place, core]

    def back(self, j, k):
        c, d = self.c, self.d
        return wrap4(self.x - j * d - k * c), wrap4(self.z - j * c - k * d)

    def piece(self, j, k):
        return self.slot(*self.back(j, k), self.c)

    def piece_across(self, j, k):
        c, d = self.c, self.d
        return self.slot(wrap4(self.x - j * c - k * d), wrap4(self.z - j * d - k * c), d)

    def send(self, src, dst, n, to):
        self.sends.append(send(src, dst, self.ssem.at[n], self.rsem.at[n], to))

    def ahead(self, j, k, r=0):
        px, pz = self.back(-j, -k)
        return device(px, wrap4(self.y + r), pz, self.c)

    def from_source(self, j, r):
        px, pz = self.back(j, 0)
        return self.ref.at[lax.div(px, 2), wrap4(self.y - r) if self.wide else 0, lax.rem(px, 2) * 4 + pz, self.c]

    def start(self, parts):
        here = self.from_source(0, 0)
        for j in (2, 1, 3, 0):
            for r in (2, 1, 3, 0) if self.wide else (0,):
                if j or r:
                    src = parts.at[wrap4(self.y + r)] if self.wide else parts
                    self.send(src, here, 4 * j + r, self.ahead(j, 0, r))
        px, pz = self.back(0, 0)
        if self.wide:
            self.ref[lax.div(px, 2), self.y, lax.rem(px, 2) * 4 + pz, self.c] = parts[self.y]
        else:
            self.ref[lax.div(px, 2), 0, lax.rem(px, 2) * 4 + pz, self.c] = parts[...]

    def pass_on(self, j):
        for r in range(4) if self.wide else (0,):
            if j or r:
                arrived(self.from_source(j, r), self.rsem.at[4 * j + r], self.across)
        here = self.piece(j, 0)
        for k in (2, 1, 3):
            self.send(here, here, 15 + 3 * j + k, self.ahead(0, k))
        self.send(here, here, 28 + 4 * j, self.across)

    def pass_across(self, j, k):
        here = self.piece(j, k)
        arrived(here, self.rsem.at[15 + 3 * j + k], self.across)
        self.send(here, here, 28 + 4 * j + k, self.across)

    def pass_all_on(self):
        for j in (0, 1, 3, 2):
            self.pass_on(j)

    def pass_all_across(self):
        for j in (0, 1, 3, 2):
            for k in (1, 3, 2):
                self.pass_across(j, k)

    def all_here(self):
        for j in range(4):
            for k in range(4):
                arrived(self.piece_across(j, k), self.rsem.at[28 + 4 * j + k], self.across)

    def done(self):
        for copy in self.sends:
            copy.wait_send()


def pack_wide(src, dst):
    cols = src.shape[-1]

    def rows(i, _):
        part = src[lax.div(i, 4), lax.rem(i, 4)].astype(F32).reshape(128, cols)
        dst[pl.ds(pl.multiple_of(i * 128, 128), 128)] = part.astype(BF)
        return 0

    lax.fori_loop(0, 8, rows, 0)


def pack_down(src, dst):
    def rows(i, _):
        part = src[lax.div(i, 4), 0, pl.ds(lax.rem(i, 4) * 2, 2)].astype(F32).reshape(96, 1024)
        dst[pl.ds(pl.multiple_of(i * 96, 96), 96)] = part.astype(BF)
        return 0

    lax.fori_loop(0, 8, rows, 0)


class Sums:
    def __init__(self, grad, refs):
        self.grad, self.cut = grad, grad.shape[1]
        (self.rc, self.sa, self.lb, self.sb, self.lg, self.ss, self.rs) = refs
        x, y, z, c = coords()
        self.y, self.c, self.d = y, c, 1 - c
        d = self.d
        self.across = device(x, y, z, d)
        self.ahead = lambda j, k, r: device(wrap4(x + j * d + k * c), wrap4(y + r), wrap4(z + j * c + k * d), c)
        self.p1 = x * d + z * c
        self.p2 = x * c + z * d
        self.sends = []

    @staticmethod
    def scratch(rows, cols, cut):
        buffers = [(2, cut, 8), (4, 4, cut), (3, 4, cut), (4, cut), (4, cut)]
        return [pltpu.VMEM(lead + (rows, cols), BF) for lead in buffers] + [DMA((20,)), DMA((20,))]

    def send(self, src, dst, n, to):
        self.sends.append(send(src, dst, self.ss.at[n], self.rs.at[n], to))

    def start(self):
        self.send(self.grad.at[:, :, :, self.d], self.rc, 0, self.across)

    def cores(self):
        arrived(self.rc, self.rs.at[0], self.across)
        c, d, cut = self.c, self.d, self.cut

        def add(i, _):
            a2, a1, r = lax.div(i, 4 * cut), lax.rem(lax.div(i, cut), 4), lax.rem(i, cut)
            px, pz = a1 * d + a2 * c, a1 * c + a2 * d
            xh, place = lax.div(px, 2), lax.rem(px, 2) * 4 + pz
            total = self.rc[xh, r, place].astype(F32) + self.grad[xh, r, place, c].astype(F32)
            self.sa[a2, a1, r] = total.astype(BF)
            return 0

        lax.fori_loop(0, 16 * cut, add, 0)
        for k in (2, 1, 3):
            self.send(self.sa.at[wrap4(self.p2 + k)], self.lb.at[k - 1], k, self.ahead(0, k, 0))

    def second(self):
        for k in (1, 3, 2):
            arrived(self.lb.at[k - 1], self.rs.at[k], self.across)

        def add(i, _):
            a1, r = lax.div(i, self.cut), lax.rem(i, self.cut)
            total = self.sa[self.p2, a1, r].astype(F32)
            for k in range(3):
                total = total + self.lb[k, a1, r].astype(F32)
            self.sb[a1, r] = total.astype(BF)
            return 0

        lax.fori_loop(0, 4 * self.cut, add, 0)
        for j in (2, 1, 3, 0):
            for r in (2, 1, 3, 0) if self.cut > 1 else (0,):
                if j or r:
                    src = self.sb.at[wrap4(self.p1 + j), wrap4(self.y + r) if self.cut > 1 else 0]
                    self.send(src, self.lg.at[j, r], 4 + 4 * j + r, self.ahead(j, 0, r))
        if self.cut > 1:
            self.lg[0, 0] = self.sb[self.p1, self.y]
        else:
            self.lg[0, 0] = self.sb[self.p1, 0]

    def last(self, r=0):
        total = 0.0
        for j in range(4):
            if j or r:
                arrived(self.lg.at[j, r], self.rs.at[4 + 4 * j + r], self.across)
            total = total + self.lg[j, r].astype(F32)
        return total

    def done(self):
        for copy in self.sends:
            copy.wait_send()


def layer_kernel(
    tok, cot, wq, wk, wv, wg, wu, gains, wop, wdp, seg, ic, isn, oc, osn,
    out, igrad, oq, ok, ov, og, ou, oo, od, ogain,
    kparts, qparts, bparts, wkl, wql, wbl, wdl, wol, wkv, wqs, wb, wd, low, xs, cs, cos, sin, rows, xn, q, kvx, lse,
    peak, total, wide, att, part, relay1, land1, acc, unit, dhid, dgu, hid, dpart, relay2, land2, dbr, opart, scale_two, land3,
    dmid, datt, go, do, inner, dkv, dkvb, land, dqkv, grow, dxq, rsend, rrecv, ssem, rsem, hsem, hrem, *scratch,
):
    x, y, z, c = coords()
    ring = [device(x, wrap4(y + k), z, c) for k in range(1, 4)]
    take = lambda n: [scratch.pop(0) for _ in range(n)]
    scratch = list(scratch)
    kv, qw, b, o, w = [Pieces(ref, *take(2)) for ref in (wkl, wql, wbl, wol, wdl)]
    sq, sk, sb, so, sd = [Sums(ref, take(7)) for ref in (wql, wkl, wbl, go, wdl)]
    sends = []

    def ring_send(n, k, src, dst):
        sends.append(send(src, dst, ssem.at[n, k - 1], rsem.at[n, k - 1], ring[k - 1]))
        return sends[-1]

    def ring_wait(n, k, dst):
        arrived(dst, rsem.at[n, k - 1], ring[0])

    mid = xs
    tokens_in = RingGather(xs, rsend.at[0], rrecv.at[0])
    sum_out = RingSum(part, relay1, land1, rsend.at[1], rrecv.at[1])
    mid_in = RingGather(mid, rsend.at[2], rrecv.at[2])
    sum_mid = RingSum(dpart, relay2, land2, rsend.at[3], rrecv.at[3])
    branch_in = RingGather(dbr, rsend.at[4], rrecv.at[4])
    sum_x = RingSum(part, relay1, land1, rsend.at[5], rrecv.at[5])

    everyone = greet_all()
    for r in range(4):
        for g in range(2):
            h = g * 4 + r
            kparts[r, :, g * 256 : 128 + g * 256] = wk[:, h * 128 : h * 128 + 128]
            kparts[r, :, 128 + g * 256 : 256 + g * 256] = wv[:, h * 128 : h * 128 + 128]
            qparts[r, :, g * 256 : g * 256 + 256] = wq[:, h * 256 : h * 256 + 256]
        kparts[r, :, 512:] = gain_tile(gains)
    xs[y] = tok[...]
    everyone()
    kv.start(kparts)
    tokens_in.start()
    qw.start(qparts)
    for r in range(4):
        for g in range(2):
            h = g * 4 + r
            bparts[r, :, g * 384 : g * 384 + 384] = wg[:, h * 384 : h * 384 + 384]
            bparts[r, :, 768 + g * 384 : 1152 + g * 384] = wu[:, h * 384 : h * 384 + 384]
    o.start(wop)
    cs[y] = cot[...]
    first_keys(seg, low)
    rope_here(ic, isn, oc, osn, cos, sin)
    kv.pass_all_on()
    tokens_in.pass_on()
    qw.pass_all_on()
    kv.pass_all_across()
    kv.all_here()
    o.pass_all_on()
    b.start(bparts)
    w.start(wdp)
    pack_wide(wkl, wkv)
    for back in (1, 3, 2):
        tokens_in.block(back)

    pick = lax.broadcasted_iota(jnp.int32, (8, 128), 0) == lax.broadcasted_iota(jnp.int32, (8, 128), 1)
    by_row = dot(pick.astype(F32).astype(BF), wkv[:, 512:], 1, 1)
    rows[:, :1024] = by_row
    every = lax.broadcasted_iota(jnp.int32, (1024, 128), 0) == 8 * lax.broadcasted_iota(jnp.int32, (1024, 128), 1)
    rows[:, 1024:] = dot(by_row.astype(BF), every.astype(F32).astype(BF), 1, 0)
    attn_gain, ffn_gain = rows[0:1, :1024], rows[1:2, :1024]
    q_gain, k_gain = rows[2:3, 1024:], rows[3:4, 1024:]

    for r in range(4):
        block = xs[r].astype(F32)
        xn[r * 128 : r * 128 + 128] = (block * rms_scale(block) * attn_gain).astype(BF)
    near, far = [], []
    for g in range(2):
        raw = dot(xn[...], wkv[:, g * 256 : g * 256 + 256], 1, 0)
        k_raw = raw[:, :128]
        kvx[2 * g, 2] = rope(k_raw * rms_scale(k_raw) * k_gain, cos[...], sin[...]).astype(BF)
        kvx[2 * g + 1, 2] = raw[:, 128:].astype(BF)
        pair = pl.ds(2 * g, 2)
        near.append(send(kvx.at[pair, 2], kvx.at[pair, 1], hsem.at[g], hrem.at[g], chunk_device(1)))
        far.append(send(kvx.at[pair, 2], kvx.at[pair, 0], hsem.at[2 + g], hrem.at[2 + g], chunk_device(2)))
    sends += near + far
    for n in (2, 1, 3):
        ring_send(1, n, cot, cs.at[y])
    qw.pass_all_across()
    qw.all_here()
    pack_wide(wql, wqs)

    def queries(g, _):
        raw = dot(xn[...], wqs[:, pl.ds(pl.multiple_of(g * 256, 256), 256)], 1, 0)
        for hd in range(2):
            q_raw = raw[:, hd * 128 : hd * 128 + 128]
            rot = rope(q_raw * rms_scale(q_raw) * q_gain, cos[...], sin[...]).astype(BF)
            for t in range(2):
                q[g, t, hd * 256 : hd * 256 + 256] = rot[t * 256 : t * 256 + 256]
        return 0

    lax.fori_loop(0, 2, queries, 0)

    attend(q, kvx, low, peak, total, wide, 2, True)
    o.pass_all_across()
    for copy in far:
        copy.wait_recv()
    attend(q, kvx, low, peak, total, wide, 0, False)
    for copy in near:
        copy.wait_recv()
    b.pass_all_on()
    w.pass_all_on()
    attend(q, kvx, low, peak, total, wide, 1, False)
    for g in range(2):
        for t in range(2):
            done = jnp.transpose(wide[g, t] / total[g, t]).astype(BF)
            lse[g, t] = peak[g, t] * EXP_SCALE + jnp.log(total[g, t]) * math.log2(math.e)
            for hd in range(2):
                cols = slice((g * 2 + hd) * 128, (g * 2 + hd) * 128 + 128)
                for half in range(2):
                    first = hd * 256 + half * 128
                    att[2 * t + half, :, cols] = done[first : first + 128]

    o.all_here()
    wo = lambda: wol[...].reshape(512, 1024)
    tokens_in.done()
    for n in (2, 1, 3, 0):
        p = dot(att[wrap4(y + n)], wo(), 1, 0)
        if n:
            part[n - 1] = p.astype(BF)
            sum_out.give(n)
        else:
            acc[...] = p + tok[...].astype(F32)
    sum_out.relay()
    b.pass_all_across()
    s = sum_out.total(acc[...])
    acc[...] = s
    scale = rms_scale(s)
    scale_two[...] = scale
    unit[...] = s * scale
    mid[y] = (s * scale * ffn_gain).astype(BF)
    mid_in.start()
    b.all_here()
    pack_wide(wbl, wb)
    mid_in.pass_on()
    w.pass_all_across()
    w.all_here()
    pack_down(wdl, wd)
    for n in (1, 3, 2):
        ring_wait(1, n, cs.at[wrap4(y - n)])
    for r in range(4):
        dhid[r] = dot(cs[r], wd[...], 1, 1)

    for k in (0, 1, 3, 2):
        r = wrap4(y - k)
        if k:
            mid_in.block(k)
        gu = dot(mid[r], wb[...], 1, 0)
        gate, up = gu[:, :768], gu[:, 768:]
        sig = 1.0 / (1.0 + jnp.exp(-gate))
        act = gate * sig
        dh = dhid[r]
        hid[r] = (act * up).astype(BF)
        dgu[r, :, :768] = (dh * up * sig * (1.0 + gate * (1.0 - sig))).astype(BF)
        dgu[r, :, 768:] = (dh * act).astype(BF)
        p = dot(dgu[r], wb[...], 1, 1)
        if k:
            dpart[3 - k] = p.astype(BF)
            sum_mid.give(4 - k)
        else:
            dmid[...] = p
    b.done()
    w.done()

    def gate_up_rows(f, _):
        span = pl.ds(pl.multiple_of(f * 128, 128), 128)
        lhs = mid[:, :, span].reshape(CHUNK, 128)
        g = dot(lhs, dgu[...].reshape(CHUNK, 1536), 0, 0)
        wbl[lax.div(f, 4), lax.rem(f, 4)] = g.reshape(8, 2, 8, 1536).astype(BF)
        return 0

    lax.fori_loop(0, 8, gate_up_rows, 0)
    sb.start()

    def down_rows(f, _):
        span = pl.ds(pl.multiple_of(f * 384, 384), 384)
        lhs = hid[:, :, span].reshape(CHUNK, 384)
        g = dot(lhs, cs[...].reshape(CHUNK, 1024), 0, 0)
        wdl[f, 0] = g.reshape(8, 2, 24, 1024).astype(BF)
        return 0

    lax.fori_loop(0, 2, down_rows, 0)
    sd.start()
    sum_mid.relay()
    sb.cores()
    for n in (2, 1, 3, 0):
        p = dot(hid[wrap4(y + n)], wd[...], 1, 0)
        if n:
            opart[n - 1] = p.astype(BF)
        else:
            acc[...] = acc[...] + p
    sd.cores()

    s = sum_mid.total(dmid[...])
    grow[...] = jnp.zeros_like(grow)
    grow[1:2] = jnp.sum(s * unit[...], axis=0, keepdims=True)
    s = s * ffn_gain
    mean = jnp.mean(s * unit[...], axis=-1, keepdims=True)
    s = cs[y].astype(F32) + scale_two[...] * (s - unit[...] * mean)
    dmid[...] = s
    dbr[y] = s.astype(BF)
    branch_in.start()

    branch_in.pass_on()
    sb.second()
    sd.second()
    for k in (0, 1, 3, 2):
        r = wrap4(y - k)
        if k:
            branch_in.block(k)
        datt[r] = dot(dbr[r], wo(), 1, 1).astype(BF)
    for k in (2, 1, 3):
        ring_send(0, k, opart.at[k - 1], land3.at[k - 1])

    ones = jnp.ones((8, 128), BF)
    for g in range(2):
        for t in range(2):
            for hd in range(2):
                cols = slice((g * 2 + hd) * 128, (g * 2 + hd) * 128 + 128)
                for half in range(2):
                    first = hd * 256 + half * 128
                    d = datt[2 * t + half, :, cols]
                    do[g, t, first : first + 128] = d
                    prod = d.astype(F32) * att[2 * t + half, :, cols].astype(F32)
                    high = prod.astype(BF)
                    rest = (prod - high.astype(F32)).astype(BF)
                    inner[g, t, :, first : first + 128] = (dot(ones, high, 1, 1) + dot(ones, rest, 1, 1))[:1]
    dq = wide
    back_near, back_far = [], []

    def give_back(g, slot, step, copies):
        pair = pl.ds(2 * g, 2)
        dkvb[2 * g : 2 * g + 2, slot] = dkv[2 * g : 2 * g + 2, slot].astype(BF)
        n = 4 + 2 * slot + g
        copies.append(send(dkvb.at[pair, slot], land.at[slot, pair], hsem.at[n], hrem.at[n], chunk_device(step)))

    attend_back(q, kvx, low, lse, do, inner, dq, dkv, 1, True, lambda g: give_back(g, 1, -1, back_near))
    attend_back(q, kvx, low, lse, do, inner, dq, dkv, 0, False, lambda g: give_back(g, 0, -2, back_far))
    sends += back_near + back_far

    def out_rows(f, _):
        span = pl.ds(pl.multiple_of(f * 256, 256), 256)
        lhs = att[:, :, span].reshape(CHUNK, 256)
        g = dot(lhs, dbr[...].reshape(CHUNK, 1024), 0, 0)
        go[f, 0] = g.reshape(8, 2, 16, 1024).astype(BF)
        return 0

    lax.fori_loop(0, 2, out_rows, 0)
    so.start()
    attend_back(q, kvx, low, lse, do, inner, dq, dkv, 2, False)

    scale = HEAD_SIZE ** (-0.5)
    raw = dhid
    raw[:, :, :512] = dot(xn[...], wqs[...], 1, 0).reshape(4, 128, 512)
    for g in range(2):
        raw[:, :, 512 + g * 128 : 640 + g * 128] = dot(xn[...], wkv[:, g * 256 : g * 256 + 128], 1, 0).reshape(4, 128, 128)
    kv.done()
    qw.done()
    g_q = jnp.zeros((1, 128), F32)
    for g in range(2):
        for t in range(2):
            d = jnp.transpose(dq[g, t] * scale).astype(BF).astype(F32)
            span = slice(t * 256, t * 256 + 256)
            for hd in range(2):
                cols = slice((g * 2 + hd) * 128, (g * 2 + hd) * 128 + 128)
                q_raw = raw[2 * t : 2 * t + 2, :, cols].reshape(256, 128)
                d_raw, d_gain = prep_back(d[hd * 256 : hd * 256 + 256], q_raw, q_gain, cos[span], sin[span])
                dqkv[span, cols] = d_raw.astype(BF)
                g_q = g_q + d_gain

    def query_rows(f, _):
        span = pl.ds(pl.multiple_of(f * 128, 128), 128)
        g = dot(xn[:, span], dqkv[:, :512], 0, 0)
        wql[lax.div(f, 4), lax.rem(f, 4)] = g.reshape(8, 2, 8, 512).astype(BF)
        of_gain = jnp.sum(g * wqs[span].astype(F32), axis=1, keepdims=True)
        grow[4:5, span] = jnp.transpose(jnp.broadcast_to(of_gain, (128, 128)))[:1]
        return 0

    lax.fori_loop(0, 8, query_rows, 0)
    sq.start()
    for r in range(4):
        dxq[r] = dot(dqkv[r * 128 : r * 128 + 128, :512], wqs[...], 1, 1)
    so.cores()
    sq.cores()
    for n in (1, 3, 2):
        ring_wait(0, n, land3.at[n - 1])
    s = acc[...]
    for n in range(3):
        s = s + land3[n].astype(F32)
    out[...] = s.astype(BF)
    for r in range(4):
        gate_up = sb.last(r)
        h = wrap4(y - r)
        for g in range(2):
            span = pl.ds(pl.multiple_of((g * 4 + h) * 384, 128), 384)
            og[:, span] = gate_up[:, g * 384 : g * 384 + 384]
            ou[:, span] = gate_up[:, 768 + g * 384 : 1152 + g * 384]
    od[...] = sd.last()
    sum_out.done()
    for copy in back_near + back_far:
        copy.wait_recv()
    g_k = jnp.zeros((1, 128), F32)
    for g in range(2):
        d = dkv[2 * g, 2] + land[0, 2 * g].astype(F32) + land[1, 2 * g].astype(F32)
        d = (d * scale).astype(BF).astype(F32)
        cols = slice(512 + g * 256, 640 + g * 256)
        k_raw = raw[:, :, 512 + g * 128 : 640 + g * 128].reshape(CHUNK, 128)
        d_raw, d_gain = prep_back(d, k_raw, k_gain, cos[...], sin[...])
        dqkv[:, cols] = d_raw.astype(BF)
        g_k = g_k + d_gain
        d = dkv[2 * g + 1, 2] + land[0, 2 * g + 1].astype(F32) + land[1, 2 * g + 1].astype(F32)
        dqkv[:, 640 + g * 256 : 768 + g * 256] = d.astype(BF)

    eight = lax.div(lax.broadcasted_iota(jnp.int32, (128, 1024), 1), 8) == lax.broadcasted_iota(jnp.int32, (128, 1024), 0)
    eight = eight.astype(F32).astype(BF)
    grow[2:3] = dot(jnp.broadcast_to(g_q, (8, 128)).astype(BF), eight, 1, 0)[:1]
    grow[3:4] = dot(jnp.broadcast_to(g_k, (8, 128)).astype(BF), eight, 1, 0)[:1]

    def key_rows(f, _):
        span = pl.ds(pl.multiple_of(f * 128, 128), 128)
        g = dot(xn[:, span], dqkv[:, 512:], 0, 0)
        at = (lax.div(f, 4), lax.rem(f, 4))
        wkl[at[0], at[1], :, :, :, :512] = g.reshape(8, 2, 8, 512).astype(BF)
        w_rows = wkv[span].astype(F32)
        tile = jnp.transpose(jnp.concatenate([grow[:, span], jnp.zeros((120, 128), F32)], axis=0))
        d_gain = (tile[:, 4:5] + jnp.sum(g * w_rows[:, :512], axis=1, keepdims=True)) / w_rows[:, 512:513]
        lane = lax.broadcasted_iota(jnp.int32, (128, 128), 1)
        tile = jnp.where(lane == 0, d_gain, tile)
        wkl[at[0], at[1], :, :, :, 512:] = tile.reshape(8, 2, 8, 128).astype(BF)
        return 0

    lax.fori_loop(0, 8, key_rows, 0)
    sk.start()

    for n in (2, 1, 3, 0):
        r = wrap4(y + n)
        span = pl.ds(pl.multiple_of(r * 128, 128), 128)
        if n == 0:
            sk.cores()
            sum_x.relay()
        p = dxq[r] + dot(dqkv[span, 512:], wkv[:, :512], 1, 1)
        if n:
            part[n - 1] = p.astype(BF)
            sum_x.give(n)
        else:
            acc[...] = p
    so.second()
    sq.second()
    sk.second()
    s = sum_x.total(acc[...])
    own = tok[...].astype(F32)
    scale_own = rms_scale(own)
    own = own * scale_own
    s = s * attn_gain
    mean = jnp.mean(s * own, axis=-1, keepdims=True)
    igrad[...] = (dmid[...] + scale_own * (s - own * mean)).astype(BF)
    oo[...] = so.last()
    gain = jnp.zeros((8, 128), F32)
    for r in range(4):
        h = wrap4(y - r)
        queries_ = sq.last(r)
        keys_ = sk.last(r)
        for g in range(2):
            span = pl.ds(pl.multiple_of((g * 4 + h) * 128, 128), 128)
            oq[:, pl.ds(pl.multiple_of((g * 4 + h) * 256, 128), 256)] = queries_[:, g * 256 : g * 256 + 256]
            ok[:, span] = keys_[:, g * 256 : g * 256 + 128]
            ov[:, span] = keys_[:, g * 256 + 128 : g * 256 + 256]
        gain = gain + keys_[:, 512:640]
    ogain[...] = gain
    for copy in sends:
        copy.wait_send()
    for s in (o, sq, sk, sb, so, sd, tokens_in, mid_in, sum_mid, branch_in, sum_x):
        s.done()


def whole_layer(tok, cot, wq, wk, wv, wg, wu, gains, wo, wd, segments):
    sds = jax.ShapeDtypeStruct
    block = (128, 1024)
    mem = lambda *shape: pltpu.VMEM(shape, BF)
    mem32 = lambda *shape: pltpu.VMEM(shape, F32)
    return pl.pallas_call(
        layer_kernel,
        out_shape=(
            sds(block, BF),
            sds(block, BF),
            sds((8, 2048), F32),
            sds((8, 1024), F32),
            sds((8, 1024), F32),
            sds((8, 3072), F32),
            sds((8, 3072), F32),
            sds((16, 1024), F32),
            sds((24, 1024), F32),
            sds((8, 128), F32),
        ),
        in_specs=[VMEM] * 7 + [SMEM] + [VMEM] * 7,
        out_specs=(VMEM,) * 10,
        scratch_shapes=[
            mem(4, 8, 640),
            mem(4, 8, 512),
            mem(4, 8, 1536),
            mem(2, 4, 8, 2, 8, 640),
            mem(2, 4, 8, 2, 8, 512),
            mem(2, 4, 8, 2, 8, 1536),
            mem(2, 1, 8, 2, 24, 1024),
            mem(2, 1, 8, 2, 16, 1024),
            mem(1024, 640),
            mem(1024, 512),
            mem(1024, 1536),
            mem(768, 1024),
            pltpu.VMEM((2, 1, 512), jnp.int32),
            mem(4, *block),
            mem(4, *block),
            mem32(CHUNK, 128),
            mem32(CHUNK, 128),
            mem32(8, 1152),
            mem(CHUNK, 1024),
            mem(2, 2, 512, 128),
            mem(4, 3, CHUNK, 128),
            mem32(2, 2, 1, 512),
            mem32(2, 2, 1, 512),
            mem32(2, 2, 1, 512),
            mem32(2, 2, 128, 512),
            mem(4, 128, 512),
            mem(3, *block),
            mem(2, 64, 1024),
            mem(2, *block),
            mem32(*block),
            mem32(*block),
            mem32(4, 128, 768),
            mem(4, 128, 1536),
            mem(4, 128, 768),
            mem(3, *block),
            mem(2, 64, 1024),
            mem(2, *block),
            mem(4, *block),
            mem(3, *block),
            mem32(128, 1),
            mem(3, *block),
            mem32(*block),
            mem(4, 128, 512),
            mem(2, 1, 8, 2, 16, 1024),
            mem(2, 2, 512, 128),
            mem32(2, 2, 1, 512),
            mem32(4, 3, CHUNK, 128),
            mem(4, 2, CHUNK, 128),
            mem(2, 4, CHUNK, 128),
            mem(CHUNK, 1024),
            mem32(8, 1024),
            mem32(4, *block),
            DMA((6, 6)),
            DMA((6, 6)),
            DMA((2, 3)),
            DMA((2, 3)),
            DMA((8,)),
            DMA((8,)),
        ]
        + Pieces.semaphores() * 5
        + Sums.scratch(8, 512, 4)
        + Sums.scratch(8, 640, 4)
        + Sums.scratch(8, 1536, 4)
        + Sums.scratch(16, 1024, 1)
        + Sums.scratch(24, 1024, 1),
        compiler_params=params(0),
        name="whole_layer",
    )(tok, cot, wq, wk, wv, wg, wu, gains, wo, wd, segments.reshape(128, 128), *rope_tables())


def results_kernel(*refs):
    ins, outs = refs[:10], refs[10:]
    for src, dst in zip(ins[:9], outs):
        dst[...] = src[...]
    gains = ins[9][...]
    row = lax.broadcasted_iota(jnp.int32, (8, 128), 0)
    col = lax.broadcasted_iota(jnp.int32, (8, 128), 1)
    for kind, dst in enumerate(outs[9:]):
        for i in range(dst.shape[0]):
            dst[i] = jnp.sum(jnp.where((row == i) & (col == kind), gains, 0.0))


def results(*arrays):
    vectors = [jax.ShapeDtypeStruct((n,), F32) for n in (8, 8, 1, 1)]
    return pl.pallas_call(
        results_kernel,
        out_shape=tuple(jax.ShapeDtypeStruct(r.shape, r.dtype) for r in arrays[:9]) + tuple(vectors),
        in_specs=[VMEM] * 10,
        out_specs=(VMEM,) * 9 + (SMEM,) * 4,
        name="results",
    )(*arrays)


def local(
    tokens, cotangent, segments, attn_gain, w_query, key_matrix, value_matrix, query_gain, key_gain,
    w_out, ffn_gain, w_gate, w_up, w_down,
):
    gains = jnp.concatenate([attn_gain, ffn_gain, query_gain, key_gain]).astype(F32)
    output, input_grad, g_query, g_key, g_value, g_gate, g_up, g_out, g_down, g_attn, g_ffn, g_qg, g_kg = results(
        *whole_layer(
            tokens, cotangent, w_query, key_matrix, value_matrix, w_gate, w_up, gains, w_out, w_down, segments
        )
    )
    return (
        output, input_grad, g_attn, g_query, g_key, g_value, g_qg, g_kg, g_out, g_ffn, g_gate, g_up, g_down,
    )


def solution(mesh):
    rows = P(("blk", "head"), None)
    cut = P(("head", "blk"), None)
    vec = P(("head", "blk"))
    return jax.shard_map(
        local,
        mesh=mesh,
        in_specs=(rows, rows, P(), vec, cut, cut, cut, vec, vec, cut, vec, cut, cut, cut),
        out_specs=(rows, rows, vec, cut, cut, cut, vec, vec, cut, vec, cut, cut, cut),
        check_vma=False,
    )
```

```python
import math

import jax
import jax.numpy as jnp
import numpy as np
from jax import lax
from jax.experimental import pallas as pl
from jax.experimental.pallas import tpu as pltpu
from jax.sharding import PartitionSpec as P

HEAD_SIZE = 128
SPAN = 1024
CHUNK = 512
EPS = 1e-06
ROPE_BASE = 1000000.0
MASKED = -1e30
MESH = pl.DeviceIdType.MESH
BF = jnp.bfloat16
F32 = jnp.float32
VMEM = pl.BlockSpec(memory_space=pltpu.VMEM)
SMEM = pl.BlockSpec(memory_space=pltpu.SMEM)
DMA = pltpu.SemaphoreType.DMA
VMEM_LIMIT = 62 * 2**20


def coords():
    h = lax.axis_index("head")
    b = lax.axis_index("blk")
    x = 2 * lax.div(h, 4) + lax.div(b, 8)
    return x, lax.rem(h, 4), lax.rem(lax.div(b, 2), 4), lax.rem(b, 2)


def device(x, y, z, c):
    return (lax.div(x, 2) * 4 + y, lax.rem(x, 2) * 8 + z * 2 + c)


def wrap4(v):
    return lax.rem(v + 8, 4)


def send(src, dst, send_sem, recv_sem, to):
    copy = pltpu.make_async_remote_copy(
        src_ref=src, dst_ref=dst, send_sem=send_sem, recv_sem=recv_sem, device_id=to, device_id_type=MESH
    )
    copy.start()
    return copy


def arrived(dst, sem, anyone):
    pltpu.make_async_remote_copy(
        src_ref=dst, dst_ref=dst, send_sem=sem, recv_sem=sem, device_id=anyone, device_id_type=MESH
    ).wait_recv()


def greet(peers):
    barrier = pltpu.get_barrier_semaphore()
    for peer in peers:
        pl.semaphore_signal(barrier, inc=1, device_id=peer, device_id_type=MESH)
    return lambda: pl.semaphore_wait(barrier, len(peers))


def params(collective_id):
    return pltpu.CompilerParams(
        collective_id=collective_id, has_side_effects=True, vmem_limit_bytes=VMEM_LIMIT
    )


def chunk_number():
    return 2 * lax.axis_index("blk") + lax.div(lax.axis_index("head"), 4)


def chunk_device(step):
    chunk = lax.rem(chunk_number() + step + 32, 32)
    return (lax.rem(chunk, 2) * 4 + lax.rem(lax.axis_index("head"), 4), lax.div(chunk, 2))


def greet_all():
    x, y, z, c = coords()
    peers = [device(x, y, z, 1 - c)]
    for j in range(4):
        for r in range(4):
            if j or r:
                peers.append(device(wrap4(x + j * (1 - c)), wrap4(y + r), wrap4(z + j * c), c))
    peers += [device(wrap4(x + k * c), y, wrap4(z + k * (1 - c)), c) for k in range(1, 4)]
    return greet(peers + [chunk_device(s) for s in (-2, -1, 1, 2)])


def dot(a, b, ca, cb):
    return lax.dot_general(a, b, (((ca,), (cb,)), ((), ())), preferred_element_type=F32)


def rms_scale(rows):
    return lax.rsqrt(jnp.mean(rows * rows, axis=-1, keepdims=True) + EPS)


def rope_tables():
    freq = ROPE_BASE ** (-np.arange(0, HEAD_SIZE, 2, dtype=np.float64) / HEAD_SIZE)
    freq = np.concatenate([freq, freq])
    sign = np.where(np.arange(HEAD_SIZE) < 64, -1.0, 1.0)
    inner = np.arange(CHUNK)[:, None] * freq[None, :]
    outer = (np.arange(32) * CHUNK)[:, None] * freq[None, :]
    tables = [f(a) * s for a in (inner, outer) for f, s in ((np.cos, 1.0), (np.sin, sign))]
    return [jnp.asarray(t.astype(np.float32)) for t in tables]


def rope_of(step, ic, isn, oc, osn, cos, sin):
    n = lax.rem(chunk_number() + step + 32, 32)
    c0, s0 = oc[pl.ds(n, 1), :], osn[pl.ds(n, 1), :]
    cos[...] = c0 * ic[...] - s0 * isn[...]
    sin[...] = s0 * ic[...] + c0 * isn[...]


def rope(rows, cos, sin):
    return rows * cos + pltpu.roll(rows, 64, 1) * sin


def rope_back(rows, cos, sin):
    return rows * cos + pltpu.roll(rows * sin, 64, 1)


def prep_back(d, raw, gain, cos, sin):
    scale = rms_scale(raw)
    unit = raw * scale
    d = rope_back(d, cos, sin)
    d_gain = jnp.sum(d * unit, axis=0, keepdims=True)
    d = d * gain
    return scale * (d - unit * jnp.mean(d * unit, axis=-1, keepdims=True)), d_gain


def first_keys(seg, low):
    start = chunk_number() * 4 - 8
    rows = []
    for i in range(12):
        row = seg[pl.ds(jnp.maximum(start + i, 0), 1), :].astype(F32)
        rows.append(jnp.where(start + i < 0, -1.0, row))
    keys = jnp.transpose(jnp.concatenate(rows + [jnp.zeros((116, 128), F32)], axis=0))
    for t in range(2):
        for half in range(2):
            query = rows[8 + 2 * t + half]
            begins = jnp.zeros((1, 128), F32)
            for i in range(12):
                before = jnp.where(keys[:, i : i + 1] < query, 1.0, 0.0)
                begins = begins + jnp.sum(before, axis=0, keepdims=True)
            row = lax.broadcasted_iota(jnp.int32, (1, 128), 1) + (t * 256 + half * 128 + 1)
            for hd in range(2):
                at = hd * 256 + half * 128
                low[t, :, at : at + 128] = jnp.maximum(begins.astype(jnp.int32), row)


def gain_tile(gains):
    row = lax.broadcasted_iota(jnp.int32, (8, 128), 0)
    col = lax.broadcasted_iota(jnp.int32, (8, 128), 1)
    tile = jnp.where(col == 2, gains[16], jnp.where(col == 3, gains[17], 0.0))
    for i in range(8):
        tile = jnp.where((row == i) & (col == 0), gains[i], tile)
        tile = jnp.where((row == i) & (col == 1), gains[8 + i], tile)
    return tile.astype(BF)


REACH = (((0, 512), (256, 256)), ((0, 512), (0, 512)), ((0, 256), (0, 512)))
EXP_SCALE = HEAD_SIZE ** (-0.5) * math.log2(math.e)


def allowed(low, slot, t):
    first, count = REACH[slot][t]
    place = lax.broadcasted_iota(jnp.int32, (count, 512), 0) + (slot * CHUNK + first)
    ok = place >= low[t]
    if slot == 2:
        query = lax.rem(lax.broadcasted_iota(jnp.int32, (1, 512), 1), 256) + (t * 256 + SPAN)
        ok = ok & (place <= query)
    return ok


def attend(q, kvx, low, peak, total, acc, slot, fresh):
    def group(g, _):
        for t in range(2):
            first, count = REACH[slot][t]
            keys = kvx[2 * g, slot, first : first + count]
            values = kvx[2 * g + 1, slot, first : first + count]
            s = dot(keys, q[g, t], 1, 1)
            s = jnp.where(allowed(low, slot, t), s, MASKED)
            top = jnp.max(s, axis=0, keepdims=True)
            if not fresh:
                before = peak[g, t]
                top = jnp.maximum(top, before)
                fade = jnp.exp2((before - top) * EXP_SCALE)
            p = jnp.exp2((s - top) * EXP_SCALE)
            add = jnp.sum(p, axis=0, keepdims=True)
            o = dot(values, p.astype(BF), 0, 0)
            if not fresh:
                add = add + total[g, t] * fade
                o = o + acc[g, t] * fade
            peak[g, t] = top
            total[g, t] = add
            acc[g, t] = o
        return 0

    lax.fori_loop(0, 2, group, 0)


def attend_back(q, kvx, low, lse, do, inner, dq, dkv, slot, fresh, after=None):
    def group(g, _):
        for t in range(2):
            first, count = REACH[slot][t]
            rows = slice(first, first + count)
            keys = kvx[2 * g, slot, rows]
            values = kvx[2 * g + 1, slot, rows]
            s = dot(keys, q[g, t], 1, 1)
            p = jnp.where(allowed(low, slot, t), jnp.exp2(s * EXP_SCALE - lse[g, t]), 0.0)
            dp = dot(values, do[g, t], 1, 1)
            ds = (p * (dp - inner[g, t])).astype(BF)
            dv = dot(p.astype(BF), do[g, t], 1, 0)
            dk = dot(ds, q[g, t], 1, 0)
            for n, d in ((2 * g, dk), (2 * g + 1, dv)):
                if t == 0:
                    dkv[n, slot, rows] = d
                elif slot == 2:
                    dkv[n, slot, :256] = dkv[n, slot, :256] + d[:256]
                    dkv[n, slot, 256:] = d[256:]
                else:
                    dkv[n, slot, rows] = dkv[n, slot, rows] + d
            d = dot(keys, ds, 0, 0)
            dq[g, t] = d if fresh else dq[g, t] + d
        return 0

    if after is None:
        lax.fori_loop(0, 2, group, 0)
    else:
        for g in range(2):
            group(g, 0)
            after(g)


LOW, HIGH = pl.ds(0, 64), pl.ds(64, 64)


class Ring:
    def __init__(self, ssem, rsem):
        x, self.y, z, c = coords()
        self.next = device(x, wrap4(self.y + 1), z, c)
        self.last = device(x, wrap4(self.y + 3), z, c)
        self.ssem, self.rsem = ssem, rsem
        self.sends = []

    def send(self, n, src, dst, to):
        self.sends.append(send(src, dst, self.ssem.at[n], self.rsem.at[n], to))

    def wait(self, n, dst):
        arrived(dst, self.rsem.at[n], self.next)

    def done(self):
        for copy in self.sends:
            copy.wait_send()
        self.sends = []


class RingGather(Ring):
    def __init__(self, ref, ssem, rsem):
        super().__init__(ssem, rsem)
        self.ref = ref

    def half(self, back, rows):
        return self.ref.at[wrap4(self.y - back), rows]

    def start(self):
        low, high = self.half(0, LOW), self.half(0, HIGH)
        self.send(0, low, low, self.next)
        self.send(1, high, high, self.last)
        self.send(2, high, high, self.next)
        self.send(3, low, low, self.last)

    def pass_on(self):
        low, high = self.half(1, LOW), self.half(3, HIGH)
        self.wait(0, low)
        self.send(4, low, low, self.next)
        self.wait(1, high)
        self.send(5, high, high, self.last)

    def block(self, back):
        if back == 1:
            self.wait(2, self.half(1, HIGH))
        elif back == 3:
            self.wait(3, self.half(3, LOW))
        elif back == 2:
            self.wait(4, self.half(2, LOW))
            self.wait(5, self.half(2, HIGH))


class RingSum(Ring):
    def __init__(self, part, relayed, landed, ssem, rsem):
        super().__init__(ssem, rsem)
        self.part, self.relayed, self.landed = part, relayed, landed

    def give(self, k):
        part = self.part.at[k - 1]
        if k == 2:
            self.send(0, part.at[LOW], self.relayed.at[0], self.next)
            self.send(1, part.at[HIGH], self.relayed.at[1], self.last)
        elif k == 1:
            self.send(2, part.at[HIGH], self.landed.at[0, HIGH], self.next)
        else:
            self.send(3, part.at[LOW], self.landed.at[1, LOW], self.last)

    def relay(self):
        part, relayed, landed = self.part, self.relayed, self.landed
        self.wait(0, relayed.at[0])
        part[0, :64] = (part[0, :64].astype(F32) + relayed[0].astype(F32)).astype(BF)
        self.send(4, part.at[0, LOW], landed.at[0, LOW], self.next)
        self.wait(1, relayed.at[1])
        part[2, 64:] = (part[2, 64:].astype(F32) + relayed[1].astype(F32)).astype(BF)
        self.send(5, part.at[2, HIGH], landed.at[1, HIGH], self.last)

    def total(self, own):
        landed = self.landed
        self.wait(2, landed.at[0, HIGH])
        self.wait(3, landed.at[1, LOW])
        self.wait(4, landed.at[0, LOW])
        self.wait(5, landed.at[1, HIGH])
        return own + landed[0].astype(F32) + landed[1].astype(F32)


class Pieces:
    def __init__(self, ref, ssem, rsem):
        self.ref, self.wide, self.ssem, self.rsem = ref, ref.shape[3] == 4, ssem, rsem
        self.x, self.y, self.z, self.c = x, y, z, c = coords()
        self.d = 1 - c
        self.p1 = x * self.d + z * c
        self.p2 = x * c + z * self.d
        self.across = device(x, y, z, 1 - c)
        self.sends = []
        self.whole = False

    @staticmethod
    def semaphores():
        return [DMA((32,)), DMA((32,))]

    def piece(self, j, k):
        return self.ref.at[self.c, wrap4(self.p2 - k), wrap4(self.p1 - j)]

    def send(self, src, dst, n, to):
        self.sends.append(send(src, dst, self.ssem.at[n], self.rsem.at[n], to))

    def ahead(self, j, k, r=0):
        c, d = self.c, self.d
        return device(wrap4(self.x + j * d + k * c), wrap4(self.y + r), wrap4(self.z + j * c + k * d), c)

    def from_source(self, j, r):
        return self.ref.at[self.c, self.p2, wrap4(self.p1 - j), wrap4(self.y - r) if self.wide else 0]

    def start(self, parts):
        here = self.from_source(0, 0)
        for j in (2, 1, 3, 0):
            for r in (2, 1, 3, 0) if self.wide else (0,):
                if j or r:
                    src = parts.at[wrap4(self.y + r)] if self.wide else parts
                    self.send(src, here, 4 * j + r, self.ahead(j, 0, r))
        if self.wide:
            self.ref[self.c, self.p2, self.p1, self.y] = parts[self.y]
        else:
            self.ref[self.c, self.p2, self.p1, 0] = parts[...]

    def start_ring(self, parts):
        here = self.from_source(0, 0)
        for r in (2, 1, 3):
            self.send(parts.at[wrap4(self.y + r)], here, r, self.ahead(0, 0, r))
        self.ref[self.c, self.p2, self.p1, self.y] = parts[self.y]

    def pass_first(self):
        for r in (1, 3, 2):
            arrived(self.from_source(0, r), self.rsem.at[r], self.across)
        here = self.piece(0, 0)
        for j in (2, 1, 3):
            self.send(here, here, 4 * j, self.ahead(j, 0))
        self.whole = True

    def pass_all_on(self):
        for j in (0, 1, 3, 2):
            if self.whole:
                if j:
                    arrived(self.piece(j, 0), self.rsem.at[4 * j], self.across)
            else:
                for r in range(4) if self.wide else (0,):
                    if j or r:
                        arrived(self.from_source(j, r), self.rsem.at[4 * j + r], self.across)
            here = self.piece(j, 0)
            for k in (2, 1, 3):
                self.send(here, here, 15 + 3 * j + k, self.ahead(0, k))

    def pass_all_across(self):
        for j in (0, 1, 3, 2):
            for k in (1, 3, 2):
                arrived(self.piece(j, k), self.rsem.at[15 + 3 * j + k], self.across)
            here = self.ref.at[self.c, :, wrap4(self.p1 - j)]
            self.send(here, here, 28 + j, self.across)

    def all_here(self):
        for j in range(4):
            arrived(self.ref.at[self.d, :, wrap4(self.p2 - j)], self.rsem.at[28 + j], self.across)

    def done(self):
        for copy in self.sends:
            copy.wait_send()


def pack(src, dst):
    _, _, _, cut, rows, cols = src.shape

    def block(i, _):
        px, r = lax.div(i, cut), lax.rem(i, cut)
        both = jnp.stack([src[0, :, px, r].astype(F32), src[1, px, :, r].astype(F32)], axis=1)
        first = lax.div(px, 2) * (16 * cut * rows) + r * (16 * rows) + lax.rem(px, 2) * (8 * rows)
        dst[pl.ds(pl.multiple_of(first, 8 * rows), 8 * rows)] = both.reshape(8 * rows, cols).astype(BF)
        return 0

    lax.fori_loop(0, 4 * cut, block, 0)


def unpack(part, dst, xh, r):
    _, _, _, _, rows, cols = dst.shape
    part = part.reshape(2, 4, 2, rows, cols).astype(BF)
    for xl in range(2):
        px = 2 * xh + xl
        dst[0, :, px, r] = part[xl, :, 0]
        dst[1, px, :, r] = part[xl, :, 1]


class Sums:
    def __init__(self, grad, refs):
        self.grad, self.cut = grad, grad.shape[3]
        (self.rc, self.lb, self.lg, self.ss, self.rs) = refs
        x, y, z, c = coords()
        self.y, self.c, self.d = y, c, 1 - c
        d = self.d
        self.across = device(x, y, z, d)
        self.ahead = lambda j, k, r: device(wrap4(x + j * d + k * c), wrap4(y + r), wrap4(z + j * c + k * d), c)
        self.p1 = x * d + z * c
        self.p2 = x * c + z * d
        self.sends = []

    @staticmethod
    def scratch(rows, cols, cut):
        buffers = [(4, 4, cut), (3, 4, cut), (4, cut)]
        return [pltpu.VMEM(lead + (rows, cols), BF) for lead in buffers] + [DMA((20,)), DMA((20,))]

    def send(self, src, dst, n, to):
        self.sends.append(send(src, dst, self.ss.at[n], self.rs.at[n], to))

    def start(self):
        self.send(self.grad.at[self.d], self.rc, 0, self.across)

    def cores(self):
        arrived(self.rc, self.rs.at[0], self.across)
        for k in (2, 1, 3, 0):
            a2 = wrap4(self.p2 + k)
            self.rc[a2] = (self.rc[a2].astype(F32) + self.grad[self.c, a2].astype(F32)).astype(BF)
            if k:
                self.send(self.rc.at[a2], self.lb.at[k - 1], k, self.ahead(0, k, 0))

    def second(self):
        for k in (1, 3, 2):
            arrived(self.lb.at[k - 1], self.rs.at[k], self.across)
        total = self.rc[self.p2].astype(F32)
        for k in range(3):
            total = total + self.lb[k].astype(F32)
        self.rc[self.p2] = total.astype(BF)
        for j in (2, 1, 3, 0):
            for r in (2, 1, 3, 0) if self.cut > 1 else (0,):
                if j or r:
                    src = self.rc.at[self.p2, wrap4(self.p1 + j), wrap4(self.y + r) if self.cut > 1 else 0]
                    self.send(src, self.lg.at[j, r], 4 + 4 * j + r, self.ahead(j, 0, r))
        self.lg[0, 0] = self.rc[self.p2, self.p1, self.y if self.cut > 1 else 0]

    def last(self, r=0):
        total = 0.0
        for j in range(4):
            if j or r:
                arrived(self.lg.at[j, r], self.rs.at[4 + 4 * j + r], self.across)
            total = total + self.lg[j, r].astype(F32)
        return total

    def done(self):
        for copy in self.sends:
            copy.wait_send()


def layer_kernel(
    tok, cot, wq, wk, wv, wg, wu, gains, wop, wdp, seg, ic, isn, oc, osn,
    out, igrad, oq, ok, ov, og, ou, oo, od, ogain,
    kparts, qparts, bparts, wkl, wql, wbl, wdl, wol, wkv, wqs, wb, wd, wo, low, xs, xs_near, cs, cos, sin, cos_near, sin_near, rows, xn, xnt, q, kvx, lse,
    peak, total, wide, att, part, relay1, land1, acc, unit, dhid, dgu, hid, dpart, relay2, land2, dbr, opart, scale_two, land3,
    dmid, datt, do, inner, dkv, dkvb, land, dqkv, grow, dxq, rsend, rrecv, ssem, rsem, hsem, hrem, *scratch,
):
    x, y, z, c = coords()
    ring = [device(x, wrap4(y + k), z, c) for k in range(1, 4)]
    take = lambda n: [scratch.pop(0) for _ in range(n)]
    scratch = list(scratch)
    kv, qw, b, o, w = [Pieces(ref, *take(2)) for ref in (wkl, wql, wbl, wol, wdl)]
    sq, sk, sb, so, sd = [Sums(ref, take(5)) for ref in (wql, wkl, wbl, wol, wdl)]
    sends = []

    def ring_send(n, k, src, dst):
        sends.append(send(src, dst, ssem.at[n, k - 1], rsem.at[n, k - 1], ring[k - 1]))
        return sends[-1]

    def ring_wait(n, k, dst):
        arrived(dst, rsem.at[n, k - 1], ring[0])

    mid = xs
    tokens_in = RingGather(xs, rsend.at[0], rrecv.at[0])
    sum_out = RingSum(part, relay1, land1, rsend.at[1], rrecv.at[1])
    mid_in = RingGather(mid, rsend.at[2], rrecv.at[2])
    sum_mid = RingSum(dpart, relay2, land2, rsend.at[3], rrecv.at[3])
    branch_in = RingGather(dbr, rsend.at[4], rrecv.at[4])
    sum_x = RingSum(part, relay1, land1, rsend.at[5], rrecv.at[5])
    near_in = RingGather(xs_near, rsend.at[6], rrecv.at[6])
    cot_in = RingGather(cs, rsend.at[7], rrecv.at[7])

    everyone = greet_all()
    for r in range(4):
        for g in range(2):
            h = g * 4 + r
            kparts[r, :, g * 256 : 128 + g * 256] = wk[:, h * 128 : h * 128 + 128]
            kparts[r, :, 128 + g * 256 : 256 + g * 256] = wv[:, h * 128 : h * 128 + 128]
            qparts[r, :, g * 256 : g * 256 + 256] = wq[:, h * 256 : h * 256 + 256]
        kparts[r, :, 512:] = gain_tile(gains)
    xs[y] = tok[...]
    everyone()
    kv.start(kparts)
    near_tok = send(tok, xs_near.at[y], hsem.at[0], hrem.at[0], chunk_device(1))
    sends.append(near_tok)
    tokens_in.start()
    qw.start(qparts)
    for r in range(4):
        for g in range(2):
            h = g * 4 + r
            bparts[r, :, g * 384 : g * 384 + 384] = wg[:, h * 384 : h * 384 + 384]
            bparts[r, :, 768 + g * 384 : 1152 + g * 384] = wu[:, h * 384 : h * 384 + 384]
    b.start_ring(bparts)
    o.start(wop)
    w.start(wdp)
    cs[y] = cot[...]
    first_keys(seg, low)
    rope_of(0, ic, isn, oc, osn, cos, sin)
    kv.pass_all_on()
    tokens_in.pass_on()
    near_tok.wait_recv()
    near_in.start()
    kv.pass_all_across()
    qw.pass_all_on()
    o.pass_all_on()
    b.pass_first()
    kv.all_here()
    pack(wkl, wkv)
    for back in (1, 3, 2):
        tokens_in.block(back)

    pick = lax.broadcasted_iota(jnp.int32, (8, 128), 0) == lax.broadcasted_iota(jnp.int32, (8, 128), 1)
    by_row = dot(pick.astype(F32).astype(BF), wkv[:, 512:], 1, 1)
    rows[:, :1024] = by_row
    every = lax.broadcasted_iota(jnp.int32, (1024, 128), 0) == 8 * lax.broadcasted_iota(jnp.int32, (1024, 128), 1)
    rows[:, 1024:] = dot(by_row.astype(BF), every.astype(F32).astype(BF), 1, 0)
    attn_gain, ffn_gain = rows[0:1, :1024], rows[1:2, :1024]
    q_gain, k_gain = rows[2:3, 1024:], rows[3:4, 1024:]

    for r in range(4):
        block = xs[r].astype(F32)
        xn[r * 128 : r * 128 + 128] = (block * rms_scale(block) * attn_gain).astype(BF)

    def keys_values(rows_in, slot, cos_, sin_, g):
        raw = dot(rows_in, wkv[:, g * 256 : g * 256 + 256], 1, 0)
        k_raw = raw[:, :128]
        kvx[2 * g, slot] = rope(k_raw * rms_scale(k_raw) * k_gain, cos_[...], sin_[...]).astype(BF)
        kvx[2 * g + 1, slot] = raw[:, 128:].astype(BF)

    far = []
    for g in range(2):
        keys_values(xn[...], 2, cos, sin, g)
        pair = pl.ds(2 * g, 2)
        far.append(send(kvx.at[pair, 2], kvx.at[pair, 0], hsem.at[2 + g], hrem.at[2 + g], chunk_device(2)))
    sends += far
    near_in.pass_on()
    w.pass_all_on()
    qw.pass_all_across()
    rope_of(-1, ic, isn, oc, osn, cos_near, sin_near)
    qw.all_here()
    pack(wql, wqs)

    for f in range(8):
        xnt[f * 128 : f * 128 + 128] = jnp.transpose(xn[:, f * 128 : f * 128 + 128])

    def queries(g, _):
        raw = dot(xn[...], wqs[:, pl.ds(pl.multiple_of(g * 256, 256), 256)], 1, 0)
        for hd in range(2):
            q_raw = raw[:, hd * 128 : hd * 128 + 128]
            rot = rope(q_raw * rms_scale(q_raw) * q_gain, cos[...], sin[...]).astype(BF)
            for t in range(2):
                q[g, t, hd * 256 : hd * 256 + 256] = rot[t * 256 : t * 256 + 256]
        return 0

    lax.fori_loop(0, 2, queries, 0)

    attend(q, kvx, low, peak, total, wide, 2, True)
    o.pass_all_across()
    for back in (1, 3, 2):
        near_in.block(back)
    cot_in.start()
    near_in.done()
    for r in range(4):
        block = xs_near[r].astype(F32)
        xs_near[r] = (block * rms_scale(block) * attn_gain).astype(BF)
    for g in range(2):
        keys_values(xs_near[...].reshape(CHUNK, 1024), 1, cos_near, sin_near, g)
    attend(q, kvx, low, peak, total, wide, 1, False)
    b.pass_all_on()
    cot_in.pass_on()
    for copy in far:
        copy.wait_recv()
    attend(q, kvx, low, peak, total, wide, 0, False)
    for g in range(2):
        for t in range(2):
            done = jnp.transpose(wide[g, t] / total[g, t]).astype(BF)
            lse[g, t] = peak[g, t] * EXP_SCALE + jnp.log(total[g, t]) * math.log2(math.e)
            for hd in range(2):
                cols = slice((g * 2 + hd) * 128, (g * 2 + hd) * 128 + 128)
                for half in range(2):
                    first = hd * 256 + half * 128
                    att[2 * t + half, :, cols] = done[first : first + 128]

    o.all_here()
    pack(wol, wo)
    tokens_in.done()
    for n in (2, 1, 3, 0):
        p = dot(att[wrap4(y + n)], wo[...], 1, 0)
        if n:
            part[n - 1] = p.astype(BF)
            sum_out.give(n)
        else:
            acc[...] = p + tok[...].astype(F32)
    sum_out.relay()
    b.pass_all_across()
    w.pass_all_across()
    s = sum_out.total(acc[...])
    acc[...] = s
    scale = rms_scale(s)
    scale_two[...] = scale
    unit[...] = s * scale
    mid[y] = (s * scale * ffn_gain).astype(BF)
    mid_in.start()
    b.all_here()
    pack(wbl, wb)
    mid_in.pass_on()
    w.all_here()
    pack(wdl, wd)
    for back in (1, 3, 2):
        cot_in.block(back)
    for r in range(4):
        dhid[r] = dot(cs[r], wd[...], 1, 1)

    for k in (0, 1, 3, 2):
        r = wrap4(y - k)
        if k:
            mid_in.block(k)
        gu = dot(mid[r], wb[...], 1, 0)
        gate, up = gu[:, :768], gu[:, 768:]
        sig = 1.0 / (1.0 + jnp.exp(-gate))
        act = gate * sig
        dh = dhid[r]
        hid[r] = (act * up).astype(BF)
        dgu[r, :, :768] = (dh * up * sig * (1.0 + gate * (1.0 - sig))).astype(BF)
        dgu[r, :, 768:] = (dh * act).astype(BF)
        p = dot(dgu[r], wb[...], 1, 1)
        if k:
            dpart[3 - k] = p.astype(BF)
            sum_mid.give(4 - k)
        else:
            dmid[...] = p
    b.done()
    w.done()
    o.done()

    def gate_up_rows(f, _):
        span = pl.ds(pl.multiple_of(f * 128, 128), 128)
        lhs = mid[:, :, span].reshape(CHUNK, 128)
        g = dot(lhs, dgu[...].reshape(CHUNK, 1536), 0, 0)
        unpack(g, wbl, lax.div(f, 4), lax.rem(f, 4))
        return 0

    lax.fori_loop(0, 8, gate_up_rows, 0)
    sb.start()

    def down_rows(f, _):
        span = pl.ds(pl.multiple_of(f * 384, 384), 384)
        lhs = hid[:, :, span].reshape(CHUNK, 384)
        g = dot(lhs, cs[...].reshape(CHUNK, 1024), 0, 0)
        unpack(g, wdl, f, 0)
        return 0

    lax.fori_loop(0, 2, down_rows, 0)
    sd.start()
    sum_mid.relay()
    sb.cores()
    for n in (2, 1, 3, 0):
        p = dot(hid[wrap4(y + n)], wd[...], 1, 0)
        if n:
            opart[n - 1] = p.astype(BF)
        else:
            acc[...] = acc[...] + p
    sd.cores()

    s = sum_mid.total(dmid[...])
    grow[...] = jnp.zeros_like(grow)
    grow[1:2] = jnp.sum(s * unit[...], axis=0, keepdims=True)
    s = s * ffn_gain
    mean = jnp.mean(s * unit[...], axis=-1, keepdims=True)
    s = cs[y].astype(F32) + scale_two[...] * (s - unit[...] * mean)
    dmid[...] = s
    dbr[y] = s.astype(BF)
    branch_in.start()

    branch_in.pass_on()
    sb.second()
    sd.second()
    for k in (0, 1, 3, 2):
        r = wrap4(y - k)
        if k:
            branch_in.block(k)
        datt[r] = dot(dbr[r], wo[...], 1, 1).astype(BF)
    for k in (2, 1, 3):
        ring_send(0, k, opart.at[k - 1], land3.at[k - 1])

    ones = jnp.ones((8, 128), BF)
    for g in range(2):
        for t in range(2):
            for hd in range(2):
                cols = slice((g * 2 + hd) * 128, (g * 2 + hd) * 128 + 128)
                for half in range(2):
                    first = hd * 256 + half * 128
                    d = datt[2 * t + half, :, cols]
                    do[g, t, first : first + 128] = d
                    prod = d.astype(F32) * att[2 * t + half, :, cols].astype(F32)
                    high = prod.astype(BF)
                    rest = (prod - high.astype(F32)).astype(BF)
                    inner[g, t, :, first : first + 128] = (dot(ones, high, 1, 1) + dot(ones, rest, 1, 1))[:1]
    dq = wide
    back_near, back_far = [], []

    def give_back(g, slot, step, copies):
        pair = pl.ds(2 * g, 2)
        dkvb[2 * g : 2 * g + 2, slot] = dkv[2 * g : 2 * g + 2, slot].astype(BF)
        n = 4 + 2 * slot + g
        copies.append(send(dkvb.at[pair, slot], land.at[slot, pair], hsem.at[n], hrem.at[n], chunk_device(step)))

    attend_back(q, kvx, low, lse, do, inner, dq, dkv, 1, True, lambda g: give_back(g, 1, -1, back_near))
    attend_back(q, kvx, low, lse, do, inner, dq, dkv, 0, False, lambda g: give_back(g, 0, -2, back_far))
    sends += back_near + back_far

    def out_rows(f, _):
        span = pl.ds(pl.multiple_of(f * 256, 256), 256)
        lhs = att[:, :, span].reshape(CHUNK, 256)
        g = dot(lhs, dbr[...].reshape(CHUNK, 1024), 0, 0)
        unpack(g, wol, f, 0)
        return 0

    lax.fori_loop(0, 2, out_rows, 0)
    so.start()
    attend_back(q, kvx, low, lse, do, inner, dq, dkv, 2, False)

    scale = HEAD_SIZE ** (-0.5)
    raw = dhid
    raw[:, :, :512] = dot(xn[...], wqs[...], 1, 0).reshape(4, 128, 512)
    for g in range(2):
        raw[:, :, 512 + g * 128 : 640 + g * 128] = dot(xn[...], wkv[:, g * 256 : g * 256 + 128], 1, 0).reshape(4, 128, 128)
    kv.done()
    qw.done()
    g_q = jnp.zeros((1, 128), F32)
    for g in range(2):
        for t in range(2):
            d = jnp.transpose(dq[g, t] * scale).astype(BF).astype(F32)
            span = slice(t * 256, t * 256 + 256)
            for hd in range(2):
                cols = slice((g * 2 + hd) * 128, (g * 2 + hd) * 128 + 128)
                q_raw = raw[2 * t : 2 * t + 2, :, cols].reshape(256, 128)
                d_raw, d_gain = prep_back(d[hd * 256 : hd * 256 + 256], q_raw, q_gain, cos[span], sin[span])
                dqkv[span, cols] = d_raw.astype(BF)
                g_q = g_q + d_gain

    def query_rows(f, _):
        span = pl.ds(pl.multiple_of(f * 128, 128), 128)
        g = dot(xnt[span], dqkv[:, :512], 1, 0)
        unpack(g, wql, lax.div(f, 4), lax.rem(f, 4))
        of_gain = jnp.sum(g * wqs[span].astype(F32), axis=1, keepdims=True)
        grow[4:5, span] = jnp.transpose(jnp.broadcast_to(of_gain, (128, 128)))[:1]
        return 0

    lax.fori_loop(0, 8, query_rows, 0)
    sq.start()
    for r in range(4):
        dxq[r] = dot(dqkv[r * 128 : r * 128 + 128, :512], wqs[...], 1, 1)
    so.cores()
    sq.cores()
    for n in (1, 3, 2):
        ring_wait(0, n, land3.at[n - 1])
    s = acc[...]
    for n in range(3):
        s = s + land3[n].astype(F32)
    out[...] = s.astype(BF)
    for r in range(4):
        gate_up = sb.last(r)
        h = wrap4(y - r)
        for g in range(2):
            span = pl.ds(pl.multiple_of((g * 4 + h) * 384, 128), 384)
            og[:, span] = gate_up[:, g * 384 : g * 384 + 384]
            ou[:, span] = gate_up[:, 768 + g * 384 : 1152 + g * 384]
    od[...] = sd.last()
    sum_out.done()
    for copy in back_near + back_far:
        copy.wait_recv()
    g_k = jnp.zeros((1, 128), F32)
    for g in range(2):
        d = dkv[2 * g, 2] + land[0, 2 * g].astype(F32) + land[1, 2 * g].astype(F32)
        d = (d * scale).astype(BF).astype(F32)
        cols = slice(512 + g * 256, 640 + g * 256)
        k_raw = raw[:, :, 512 + g * 128 : 640 + g * 128].reshape(CHUNK, 128)
        d_raw, d_gain = prep_back(d, k_raw, k_gain, cos[...], sin[...])
        dqkv[:, cols] = d_raw.astype(BF)
        g_k = g_k + d_gain
        d = dkv[2 * g + 1, 2] + land[0, 2 * g + 1].astype(F32) + land[1, 2 * g + 1].astype(F32)
        dqkv[:, 640 + g * 256 : 768 + g * 256] = d.astype(BF)

    eight = lax.div(lax.broadcasted_iota(jnp.int32, (128, 1024), 1), 8) == lax.broadcasted_iota(jnp.int32, (128, 1024), 0)
    eight = eight.astype(F32).astype(BF)
    grow[2:3] = dot(jnp.broadcast_to(g_q, (8, 128)).astype(BF), eight, 1, 0)[:1]
    grow[3:4] = dot(jnp.broadcast_to(g_k, (8, 128)).astype(BF), eight, 1, 0)[:1]

    def key_rows(f, _):
        span = pl.ds(pl.multiple_of(f * 128, 128), 128)
        g = dot(xnt[span], dqkv[:, 512:], 1, 0)
        w_rows = wkv[span].astype(F32)
        tile = jnp.transpose(jnp.concatenate([grow[:, span], jnp.zeros((120, 128), F32)], axis=0))
        d_gain = (tile[:, 4:5] + jnp.sum(g * w_rows[:, :512], axis=1, keepdims=True)) / w_rows[:, 512:513]
        lane = lax.broadcasted_iota(jnp.int32, (128, 128), 1)
        tile = jnp.where(lane == 0, d_gain, tile)
        unpack(jnp.concatenate([g, tile], axis=1), wkl, lax.div(f, 4), lax.rem(f, 4))
        return 0

    lax.fori_loop(0, 8, key_rows, 0)
    sk.start()

    for n in (2, 1, 3, 0):
        r = wrap4(y + n)
        span = pl.ds(pl.multiple_of(r * 128, 128), 128)
        if n == 0:
            sk.cores()
            sum_x.relay()
        p = dxq[r] + dot(dqkv[span, 512:], wkv[:, :512], 1, 1)
        if n:
            part[n - 1] = p.astype(BF)
            sum_x.give(n)
        else:
            acc[...] = p
    so.second()
    sq.second()
    sk.second()
    s = sum_x.total(acc[...])
    own = tok[...].astype(F32)
    scale_own = rms_scale(own)
    own = own * scale_own
    s = s * attn_gain
    mean = jnp.mean(s * own, axis=-1, keepdims=True)
    igrad[...] = (dmid[...] + scale_own * (s - own * mean)).astype(BF)
    oo[...] = so.last()
    gain = jnp.zeros((8, 128), F32)
    for r in range(4):
        h = wrap4(y - r)
        queries_ = sq.last(r)
        keys_ = sk.last(r)
        for g in range(2):
            span = pl.ds(pl.multiple_of((g * 4 + h) * 128, 128), 128)
            oq[:, pl.ds(pl.multiple_of((g * 4 + h) * 256, 128), 256)] = queries_[:, g * 256 : g * 256 + 256]
            ok[:, span] = keys_[:, g * 256 : g * 256 + 128]
            ov[:, span] = keys_[:, g * 256 + 128 : g * 256 + 256]
        gain = gain + keys_[:, 512:640]
    ogain[...] = gain
    for copy in sends:
        copy.wait_send()
    for s in (sq, sk, sb, so, sd, tokens_in, mid_in, sum_mid, branch_in, sum_x, cot_in):
        s.done()


def whole_layer(tok, cot, wq, wk, wv, wg, wu, gains, wo, wd, segments):
    sds = jax.ShapeDtypeStruct
    block = (128, 1024)
    mem = lambda *shape: pltpu.VMEM(shape, BF)
    mem32 = lambda *shape: pltpu.VMEM(shape, F32)
    return pl.pallas_call(
        layer_kernel,
        out_shape=(
            sds(block, BF),
            sds(block, BF),
            sds((8, 2048), F32),
            sds((8, 1024), F32),
            sds((8, 1024), F32),
            sds((8, 3072), F32),
            sds((8, 3072), F32),
            sds((16, 1024), F32),
            sds((24, 1024), F32),
            sds((8, 128), F32),
        ),
        in_specs=[VMEM] * 7 + [SMEM] + [VMEM] * 7,
        out_specs=(VMEM,) * 10,
        scratch_shapes=[
            mem(4, 8, 640),
            mem(4, 8, 512),
            mem(4, 8, 1536),
            mem(2, 4, 4, 4, 8, 640),
            mem(2, 4, 4, 4, 8, 512),
            mem(2, 4, 4, 4, 8, 1536),
            mem(2, 4, 4, 1, 24, 1024),
            mem(2, 4, 4, 1, 16, 1024),
            mem(1024, 640),
            mem(1024, 512),
            mem(1024, 1536),
            mem(768, 1024),
            mem(512, 1024),
            pltpu.VMEM((2, 1, 512), jnp.int32),
            mem(4, *block),
            mem(4, *block),
            mem(4, *block),
            mem32(CHUNK, 128),
            mem32(CHUNK, 128),
            mem32(CHUNK, 128),
            mem32(CHUNK, 128),
            mem32(8, 1152),
            mem(CHUNK, 1024),
            mem(1024, CHUNK),
            mem(2, 2, 512, 128),
            mem(4, 3, CHUNK, 128),
            mem32(2, 2, 1, 512),
            mem32(2, 2, 1, 512),
            mem32(2, 2, 1, 512),
            mem32(2, 2, 128, 512),
            mem(4, 128, 512),
            mem(3, *block),
            mem(2, 64, 1024),
            mem(2, *block),
            mem32(*block),
            mem32(*block),
            mem32(4, 128, 768),
            mem(4, 128, 1536),
            mem(4, 128, 768),
            mem(3, *block),
            mem(2, 64, 1024),
            mem(2, *block),
            mem(4, *block),
            mem(3, *block),
            mem32(128, 1),
            mem(3, *block),
            mem32(*block),
            mem(4, 128, 512),
            mem(2, 2, 512, 128),
            mem32(2, 2, 1, 512),
            mem32(4, 3, CHUNK, 128),
            mem(4, 2, CHUNK, 128),
            mem(2, 4, CHUNK, 128),
            mem(CHUNK, 1024),
            mem32(8, 1024),
            mem32(4, *block),
            DMA((8, 6)),
            DMA((8, 6)),
            DMA((2, 3)),
            DMA((2, 3)),
            DMA((8,)),
            DMA((8,)),
        ]
        + Pieces.semaphores() * 5
        + Sums.scratch(8, 512, 4)
        + Sums.scratch(8, 640, 4)
        + Sums.scratch(8, 1536, 4)
        + Sums.scratch(16, 1024, 1)
        + Sums.scratch(24, 1024, 1),
        compiler_params=params(0),
        name="whole_layer",
    )(tok, cot, wq, wk, wv, wg, wu, gains, wo, wd, segments.reshape(128, 128), *rope_tables())


def results_kernel(*refs):
    ins, outs = refs[:10], refs[10:]
    for src, dst in zip(ins[:9], outs):
        dst[...] = src[...]
    gains = ins[9][...]
    row = lax.broadcasted_iota(jnp.int32, (8, 128), 0)
    col = lax.broadcasted_iota(jnp.int32, (8, 128), 1)
    for kind, dst in enumerate(outs[9:]):
        for i in range(dst.shape[0]):
            dst[i] = jnp.sum(jnp.where((row == i) & (col == kind), gains, 0.0))


def results(*arrays):
    vectors = [jax.ShapeDtypeStruct((n,), F32) for n in (8, 8, 1, 1)]
    return pl.pallas_call(
        results_kernel,
        out_shape=tuple(jax.ShapeDtypeStruct(r.shape, r.dtype) for r in arrays[:9]) + tuple(vectors),
        in_specs=[VMEM] * 10,
        out_specs=(VMEM,) * 9 + (SMEM,) * 4,
        name="results",
    )(*arrays)


def local(
    tokens, cotangent, segments, attn_gain, w_query, key_matrix, value_matrix, query_gain, key_gain,
    w_out, ffn_gain, w_gate, w_up, w_down,
):
    gains = jnp.concatenate([attn_gain, ffn_gain, query_gain, key_gain]).astype(F32)
    output, input_grad, g_query, g_key, g_value, g_gate, g_up, g_out, g_down, g_attn, g_ffn, g_qg, g_kg = results(
        *whole_layer(
            tokens, cotangent, w_query, key_matrix, value_matrix, w_gate, w_up, gains, w_out, w_down, segments
        )
    )
    return (
        output, input_grad, g_attn, g_query, g_key, g_value, g_qg, g_kg, g_out, g_ffn, g_gate, g_up, g_down,
    )


def solution(mesh):
    rows = P(("blk", "head"), None)
    cut = P(("head", "blk"), None)
    vec = P(("head", "blk"))
    return jax.shard_map(
        local,
        mesh=mesh,
        in_specs=(rows, rows, P(), vec, cut, cut, cut, vec, vec, cut, vec, cut, cut, cut),
        out_specs=(rows, rows, vec, cut, cut, cut, vec, vec, cut, vec, cut, cut, cut),
        check_vma=False,
    )
```

```python
import math

import jax
import jax.numpy as jnp
import numpy as np
from jax import lax
from jax.experimental import pallas as pl
from jax.experimental.pallas import tpu as pltpu
from jax.sharding import PartitionSpec as P

HEAD_SIZE = 128
SPAN = 1024
CHUNK = 512
EPS = 1e-06
ROPE_BASE = 1000000.0
MASKED = -1e30
MESH = pl.DeviceIdType.MESH
BF = jnp.bfloat16
F32 = jnp.float32
VMEM = pl.BlockSpec(memory_space=pltpu.VMEM)
SMEM = pl.BlockSpec(memory_space=pltpu.SMEM)
DMA = pltpu.SemaphoreType.DMA
VMEM_LIMIT = 62 * 2**20


def coords():
    h = lax.axis_index("head")
    b = lax.axis_index("blk")
    x = 2 * lax.div(h, 4) + lax.div(b, 8)
    return x, lax.rem(h, 4), lax.rem(lax.div(b, 2), 4), lax.rem(b, 2)


def device(x, y, z, c):
    return (lax.div(x, 2) * 4 + y, lax.rem(x, 2) * 8 + z * 2 + c)


def wrap4(v):
    return lax.rem(v + 8, 4)


def send(src, dst, send_sem, recv_sem, to):
    copy = pltpu.make_async_remote_copy(
        src_ref=src, dst_ref=dst, send_sem=send_sem, recv_sem=recv_sem, device_id=to, device_id_type=MESH
    )
    copy.start()
    return copy


def arrived(dst, sem, anyone):
    pltpu.make_async_remote_copy(
        src_ref=dst, dst_ref=dst, send_sem=sem, recv_sem=sem, device_id=anyone, device_id_type=MESH
    ).wait_recv()


def greet(peers):
    barrier = pltpu.get_barrier_semaphore()
    for peer in peers:
        pl.semaphore_signal(barrier, inc=1, device_id=peer, device_id_type=MESH)
    return lambda: pl.semaphore_wait(barrier, len(peers))


def params(collective_id):
    return pltpu.CompilerParams(
        collective_id=collective_id, has_side_effects=True, vmem_limit_bytes=VMEM_LIMIT
    )


def chunk_number():
    return 2 * lax.axis_index("blk") + lax.div(lax.axis_index("head"), 4)


def chunk_device(step):
    chunk = lax.rem(chunk_number() + step + 32, 32)
    return (lax.rem(chunk, 2) * 4 + lax.rem(lax.axis_index("head"), 4), lax.div(chunk, 2))


def greet_all():
    x, y, z, c = coords()
    peers = [device(x, y, z, 1 - c)]
    for j in range(4):
        for r in range(4):
            if j or r:
                peers.append(device(wrap4(x + j * (1 - c)), wrap4(y + r), wrap4(z + j * c), c))
    peers += [device(wrap4(x + k * c), y, wrap4(z + k * (1 - c)), c) for k in range(1, 4)]
    return greet(peers + [chunk_device(s) for s in (-2, -1, 1, 2)])


def dot(a, b, ca, cb):
    return lax.dot_general(a, b, (((ca,), (cb,)), ((), ())), preferred_element_type=F32)


def rms_scale(rows):
    return lax.rsqrt(jnp.mean(rows * rows, axis=-1, keepdims=True) + EPS)


def rope_tables():
    freq = ROPE_BASE ** (-np.arange(0, HEAD_SIZE, 2, dtype=np.float64) / HEAD_SIZE)
    freq = np.concatenate([freq, freq])
    sign = np.where(np.arange(HEAD_SIZE) < 64, -1.0, 1.0)
    inner = np.arange(CHUNK)[:, None] * freq[None, :]
    outer = (np.arange(32) * CHUNK)[:, None] * freq[None, :]
    tables = [f(a) * s for a in (inner, outer) for f, s in ((np.cos, 1.0), (np.sin, sign))]
    return [jnp.asarray(t.astype(np.float32)) for t in tables]


def rope_of(step, ic, isn, oc, osn, cos, sin):
    n = lax.rem(chunk_number() + step + 32, 32)
    c0, s0 = oc[pl.ds(n, 1), :], osn[pl.ds(n, 1), :]
    cos[...] = c0 * ic[...] - s0 * isn[...]
    sin[...] = s0 * ic[...] + c0 * isn[...]


def rope(rows, cos, sin):
    return rows * cos + pltpu.roll(rows, 64, 1) * sin


def rope_back(rows, cos, sin):
    return rows * cos + pltpu.roll(rows * sin, 64, 1)


def prep_back(d, raw, gain, cos, sin):
    scale = rms_scale(raw)
    unit = raw * scale
    d = rope_back(d, cos, sin)
    d_gain = jnp.sum(d * unit, axis=0, keepdims=True)
    d = d * gain
    return scale * (d - unit * jnp.mean(d * unit, axis=-1, keepdims=True)), d_gain


def first_keys(seg, low):
    start = chunk_number() * 4 - 8
    rows = []
    for i in range(12):
        row = seg[pl.ds(jnp.maximum(start + i, 0), 1), :].astype(F32)
        rows.append(jnp.where(start + i < 0, -1.0, row))
    keys = jnp.transpose(jnp.concatenate(rows + [jnp.zeros((116, 128), F32)], axis=0))
    for t in range(2):
        for half in range(2):
            query = rows[8 + 2 * t + half]
            begins = jnp.zeros((1, 128), F32)
            for i in range(12):
                before = jnp.where(keys[:, i : i + 1] < query, 1.0, 0.0)
                begins = begins + jnp.sum(before, axis=0, keepdims=True)
            row = lax.broadcasted_iota(jnp.int32, (1, 128), 1) + (t * 256 + half * 128 + 1)
            for hd in range(2):
                at = hd * 256 + half * 128
                low[t, :, at : at + 128] = jnp.maximum(begins.astype(jnp.int32), row)


def gain_tile(gains):
    row = lax.broadcasted_iota(jnp.int32, (8, 128), 0)
    col = lax.broadcasted_iota(jnp.int32, (8, 128), 1)
    tile = jnp.where(col == 2, gains[16], jnp.where(col == 3, gains[17], 0.0))
    for i in range(8):
        tile = jnp.where((row == i) & (col == 0), gains[i], tile)
        tile = jnp.where((row == i) & (col == 1), gains[8 + i], tile)
    return tile.astype(BF)


REACH = (((0, 512), (256, 256)), ((0, 512), (0, 512)), ((0, 256), (0, 512)))
EXP_SCALE = HEAD_SIZE ** (-0.5) * math.log2(math.e)


def allowed(low, slot, t):
    first, count = REACH[slot][t]
    place = lax.broadcasted_iota(jnp.int32, (count, 512), 0) + (slot * CHUNK + first)
    ok = place >= low[t]
    if slot == 2:
        query = lax.rem(lax.broadcasted_iota(jnp.int32, (1, 512), 1), 256) + (t * 256 + SPAN)
        ok = ok & (place <= query)
    return ok


def attend(q, kvx, low, peak, total, acc, slot, fresh):
    def group(g, _):
        for t in range(2):
            first, count = REACH[slot][t]
            keys = kvx[2 * g, slot, first : first + count]
            values = kvx[2 * g + 1, slot, first : first + count]
            s = dot(keys, q[g, t], 1, 1)
            s = jnp.where(allowed(low, slot, t), s, MASKED)
            top = jnp.max(s, axis=0, keepdims=True)
            if not fresh:
                before = peak[g, t]
                top = jnp.maximum(top, before)
                fade = jnp.exp2((before - top) * EXP_SCALE)
            p = jnp.exp2((s - top) * EXP_SCALE)
            add = jnp.sum(p, axis=0, keepdims=True)
            o = dot(values, p.astype(BF), 0, 0)
            if not fresh:
                add = add + total[g, t] * fade
                o = o + acc[g, t] * fade
            peak[g, t] = top
            total[g, t] = add
            acc[g, t] = o
        return 0

    lax.fori_loop(0, 2, group, 0)


def attend_back(q, kvx, low, lse, do, inner, dq, dkv, slot, fresh, after=None):
    def group(g, _):
        for t in range(2):
            first, count = REACH[slot][t]
            rows = slice(first, first + count)
            keys = kvx[2 * g, slot, rows]
            values = kvx[2 * g + 1, slot, rows]
            s = dot(keys, q[g, t], 1, 1)
            p = jnp.where(allowed(low, slot, t), jnp.exp2(s * EXP_SCALE - lse[g, t]), 0.0)
            dp = dot(values, do[g, t], 1, 1)
            ds = (p * (dp - inner[g, t])).astype(BF)
            dv = dot(p.astype(BF), do[g, t], 1, 0)
            dk = dot(ds, q[g, t], 1, 0)
            for n, d in ((2 * g, dk), (2 * g + 1, dv)):
                if t == 0:
                    dkv[n, slot, rows] = d
                elif slot == 2:
                    dkv[n, slot, :256] = dkv[n, slot, :256] + d[:256]
                    dkv[n, slot, 256:] = d[256:]
                else:
                    dkv[n, slot, rows] = dkv[n, slot, rows] + d
            d = dot(keys, ds, 0, 0)
            dq[g, t] = d if fresh else dq[g, t] + d
        return 0

    if after is None:
        lax.fori_loop(0, 2, group, 0)
    else:
        for g in range(2):
            group(g, 0)
            after(g)


LOW, HIGH = pl.ds(0, 64), pl.ds(64, 64)


class Ring:
    def __init__(self, ssem, rsem):
        x, self.y, z, c = coords()
        self.next = device(x, wrap4(self.y + 1), z, c)
        self.last = device(x, wrap4(self.y + 3), z, c)
        self.ssem, self.rsem = ssem, rsem
        self.sends = []

    def send(self, n, src, dst, to):
        self.sends.append(send(src, dst, self.ssem.at[n], self.rsem.at[n], to))

    def wait(self, n, dst):
        arrived(dst, self.rsem.at[n], self.next)

    def done(self):
        for copy in self.sends:
            copy.wait_send()
        self.sends = []


class RingGather(Ring):
    def __init__(self, ref, ssem, rsem):
        super().__init__(ssem, rsem)
        self.ref = ref

    def half(self, back, rows):
        return self.ref.at[wrap4(self.y - back), rows]

    def start(self):
        low, high = self.half(0, LOW), self.half(0, HIGH)
        self.send(0, low, low, self.next)
        self.send(1, high, high, self.last)
        self.send(2, high, high, self.next)
        self.send(3, low, low, self.last)

    def pass_on(self):
        low, high = self.half(1, LOW), self.half(3, HIGH)
        self.wait(0, low)
        self.send(4, low, low, self.next)
        self.wait(1, high)
        self.send(5, high, high, self.last)

    def block(self, back):
        if back == 1:
            self.wait(2, self.half(1, HIGH))
        elif back == 3:
            self.wait(3, self.half(3, LOW))
        elif back == 2:
            self.wait(4, self.half(2, LOW))
            self.wait(5, self.half(2, HIGH))


class RingSum(Ring):
    def __init__(self, part, relayed, landed, ssem, rsem):
        super().__init__(ssem, rsem)
        self.part, self.relayed, self.landed = part, relayed, landed

    def give(self, k):
        part = self.part.at[k - 1]
        if k == 2:
            self.send(0, part.at[LOW], self.relayed.at[0], self.next)
            self.send(1, part.at[HIGH], self.relayed.at[1], self.last)
        elif k == 1:
            self.send(2, part.at[HIGH], self.landed.at[0, HIGH], self.next)
        else:
            self.send(3, part.at[LOW], self.landed.at[1, LOW], self.last)

    def relay(self):
        part, relayed, landed = self.part, self.relayed, self.landed
        self.wait(0, relayed.at[0])
        part[0, :64] = (part[0, :64].astype(F32) + relayed[0].astype(F32)).astype(BF)
        self.send(4, part.at[0, LOW], landed.at[0, LOW], self.next)
        self.wait(1, relayed.at[1])
        part[2, 64:] = (part[2, 64:].astype(F32) + relayed[1].astype(F32)).astype(BF)
        self.send(5, part.at[2, HIGH], landed.at[1, HIGH], self.last)

    def total(self, own):
        landed = self.landed
        self.wait(2, landed.at[0, HIGH])
        self.wait(3, landed.at[1, LOW])
        self.wait(4, landed.at[0, LOW])
        self.wait(5, landed.at[1, HIGH])
        return own + landed[0].astype(F32) + landed[1].astype(F32)


class Pieces:
    def __init__(self, ref, ssem, rsem):
        self.ref, self.wide, self.ssem, self.rsem = ref, ref.shape[3] == 4, ssem, rsem
        self.x, self.y, self.z, self.c = x, y, z, c = coords()
        self.d = 1 - c
        self.p1 = x * self.d + z * c
        self.p2 = x * c + z * self.d
        self.across = device(x, y, z, 1 - c)
        self.sends = []
        self.whole = False

    @staticmethod
    def semaphores():
        return [DMA((32,)), DMA((32,))]

    def piece(self, j, k):
        return self.ref.at[self.c, wrap4(self.p2 - k), wrap4(self.p1 - j)]

    def send(self, src, dst, n, to):
        self.sends.append(send(src, dst, self.ssem.at[n], self.rsem.at[n], to))

    def ahead(self, j, k, r=0):
        c, d = self.c, self.d
        return device(wrap4(self.x + j * d + k * c), wrap4(self.y + r), wrap4(self.z + j * c + k * d), c)

    def from_source(self, j, r):
        return self.ref.at[self.c, self.p2, wrap4(self.p1 - j), wrap4(self.y - r) if self.wide else 0]

    def start(self, parts):
        here = self.from_source(0, 0)
        for j in (2, 1, 3, 0):
            for r in (2, 1, 3, 0) if self.wide else (0,):
                if j or r:
                    src = parts.at[wrap4(self.y + r)] if self.wide else parts
                    self.send(src, here, 4 * j + r, self.ahead(j, 0, r))
        if self.wide:
            self.ref[self.c, self.p2, self.p1, self.y] = parts[self.y]
        else:
            self.ref[self.c, self.p2, self.p1, 0] = parts[...]

    def start_ring(self, parts):
        here = self.from_source(0, 0)
        for r in (2, 1, 3):
            self.send(parts.at[wrap4(self.y + r)], here, r, self.ahead(0, 0, r))
        self.ref[self.c, self.p2, self.p1, self.y] = parts[self.y]

    def pass_first(self):
        for r in (1, 3, 2):
            arrived(self.from_source(0, r), self.rsem.at[r], self.across)
        here = self.piece(0, 0)
        for j in (2, 1, 3):
            self.send(here, here, 4 * j, self.ahead(j, 0))
        self.whole = True

    def pass_all_on(self):
        for j in (0, 1, 3, 2):
            if self.whole:
                if j:
                    arrived(self.piece(j, 0), self.rsem.at[4 * j], self.across)
            else:
                for r in range(4) if self.wide else (0,):
                    if j or r:
                        arrived(self.from_source(j, r), self.rsem.at[4 * j + r], self.across)
            here = self.piece(j, 0)
            for k in (2, 1, 3):
                self.send(here, here, 15 + 3 * j + k, self.ahead(0, k))

    def pass_all_across(self):
        for j in (0, 1, 3, 2):
            for k in (1, 3, 2):
                arrived(self.piece(j, k), self.rsem.at[15 + 3 * j + k], self.across)
            here = self.ref.at[self.c, :, wrap4(self.p1 - j)]
            self.send(here, here, 28 + j, self.across)

    def all_here(self):
        for j in range(4):
            arrived(self.ref.at[self.d, :, wrap4(self.p2 - j)], self.rsem.at[28 + j], self.across)

    def done(self):
        for copy in self.sends:
            copy.wait_send()


def pack(src, dst):
    _, _, _, cut, rows, cols = src.shape

    def block(i, _):
        px, r = lax.div(i, cut), lax.rem(i, cut)
        both = jnp.stack([src[0, :, px, r].astype(F32), src[1, px, :, r].astype(F32)], axis=1)
        first = lax.div(px, 2) * (16 * cut * rows) + r * (16 * rows) + lax.rem(px, 2) * (8 * rows)
        dst[pl.ds(pl.multiple_of(first, 8 * rows), 8 * rows)] = both.reshape(8 * rows, cols).astype(BF)
        return 0

    lax.fori_loop(0, 4 * cut, block, 0)


def unpack(part, dst, xh, r):
    _, _, _, _, rows, cols = dst.shape
    part = part.reshape(2, 4, 2, rows, cols).astype(BF)
    for xl in range(2):
        px = 2 * xh + xl
        dst[0, :, px, r] = part[xl, :, 0]
        dst[1, px, :, r] = part[xl, :, 1]


class Sums:
    def __init__(self, grad, refs):
        self.grad, self.cut = grad, grad.shape[3]
        (self.rc, self.lb, self.lg, self.ss, self.rs) = refs
        x, y, z, c = coords()
        self.y, self.c, self.d = y, c, 1 - c
        d = self.d
        self.across = device(x, y, z, d)
        self.ahead = lambda j, k, r: device(wrap4(x + j * d + k * c), wrap4(y + r), wrap4(z + j * c + k * d), c)
        self.p1 = x * d + z * c
        self.p2 = x * c + z * d
        self.sends = []

    @staticmethod
    def scratch(rows, cols, cut):
        buffers = [(4, 4, cut), (3, 4, cut), (4, cut)]
        return [pltpu.VMEM(lead + (rows, cols), BF) for lead in buffers] + [DMA((20,)), DMA((20,))]

    def send(self, src, dst, n, to):
        self.sends.append(send(src, dst, self.ss.at[n], self.rs.at[n], to))

    def start(self):
        self.send(self.grad.at[self.d], self.rc, 0, self.across)

    def cores(self):
        arrived(self.rc, self.rs.at[0], self.across)
        for k in (2, 1, 3, 0):
            a2 = wrap4(self.p2 + k)
            self.rc[a2] = (self.rc[a2].astype(F32) + self.grad[self.c, a2].astype(F32)).astype(BF)
            if k:
                self.send(self.rc.at[a2], self.lb.at[k - 1], k, self.ahead(0, k, 0))

    def second(self):
        for k in (1, 3, 2):
            arrived(self.lb.at[k - 1], self.rs.at[k], self.across)
        total = self.rc[self.p2].astype(F32)
        for k in range(3):
            total = total + self.lb[k].astype(F32)
        self.rc[self.p2] = total.astype(BF)
        for j in (2, 1, 3, 0):
            for r in (2, 1, 3, 0) if self.cut > 1 else (0,):
                if j or r:
                    src = self.rc.at[self.p2, wrap4(self.p1 + j), wrap4(self.y + r) if self.cut > 1 else 0]
                    self.send(src, self.lg.at[j, r], 4 + 4 * j + r, self.ahead(j, 0, r))
        self.lg[0, 0] = self.rc[self.p2, self.p1, self.y if self.cut > 1 else 0]

    def last(self, r=0):
        total = 0.0
        for j in range(4):
            if j or r:
                arrived(self.lg.at[j, r], self.rs.at[4 + 4 * j + r], self.across)
            total = total + self.lg[j, r].astype(F32)
        return total

    def done(self):
        for copy in self.sends:
            copy.wait_send()


def layer_kernel(
    tok, cot, wq, wk, wv, wg, wu, gains, wop, wdp, seg, ic, isn, oc, osn,
    out, igrad, oq, ok, ov, og, ou, oo, od, ogain,
    kparts, qparts, bparts, wkl, wql, wbl, wdl, wol, wkv, wqs, wb, wd, wo, low, xs, xs_near, scales, cs, cos, sin, cos_near, sin_near, rows, xn, xnt, q, kvx, lse,
    peak, total, wide, att, part, relay1, land1, acc, unit, dhid, dgu, hid, dpart, relay2, land2, dbr, opart, scale_two, land3,
    dmid, datt, do, inner, dkv, dkvb, land, dqkv, grow, dxq, rsend, rrecv, ssem, rsem, hsem, hrem, *scratch,
):
    x, y, z, c = coords()
    ring = [device(x, wrap4(y + k), z, c) for k in range(1, 4)]
    take = lambda n: [scratch.pop(0) for _ in range(n)]
    scratch = list(scratch)
    kv, qw, b, o, w = [Pieces(ref, *take(2)) for ref in (wkl, wql, wbl, wol, wdl)]
    sq, sk, sb, so, sd = [Sums(ref, take(5)) for ref in (wql, wkl, wbl, wol, wdl)]
    sends = []

    def ring_send(n, k, src, dst):
        sends.append(send(src, dst, ssem.at[n, k - 1], rsem.at[n, k - 1], ring[k - 1]))
        return sends[-1]

    def ring_wait(n, k, dst):
        arrived(dst, rsem.at[n, k - 1], ring[0])

    mid = xs
    tokens_in = RingGather(xs, rsend.at[0], rrecv.at[0])
    sum_out = RingSum(part, relay1, land1, rsend.at[1], rrecv.at[1])
    mid_in = RingGather(mid, rsend.at[2], rrecv.at[2])
    sum_mid = RingSum(dpart, relay2, land2, rsend.at[3], rrecv.at[3])
    branch_in = RingGather(dbr, rsend.at[4], rrecv.at[4])
    sum_x = RingSum(part, relay1, land1, rsend.at[5], rrecv.at[5])
    near_in = RingGather(xs_near, rsend.at[6], rrecv.at[6])
    cot_in = RingGather(cs, rsend.at[7], rrecv.at[7])

    everyone = greet_all()
    for r in range(4):
        for g in range(2):
            h = g * 4 + r
            kparts[r, :, g * 256 : 128 + g * 256] = wk[:, h * 128 : h * 128 + 128]
            kparts[r, :, 128 + g * 256 : 256 + g * 256] = wv[:, h * 128 : h * 128 + 128]
            qparts[r, :, g * 256 : g * 256 + 256] = wq[:, h * 256 : h * 256 + 256]
        kparts[r, :, 512:] = gain_tile(gains)
    xs[y] = tok[...]
    everyone()
    kv.start(kparts)
    near_tok = send(tok, xs_near.at[y], hsem.at[0], hrem.at[0], chunk_device(1))
    sends.append(near_tok)
    tokens_in.start()
    qw.start(qparts)
    for r in range(4):
        for g in range(2):
            h = g * 4 + r
            bparts[r, :, g * 384 : g * 384 + 384] = wg[:, h * 384 : h * 384 + 384]
            bparts[r, :, 768 + g * 384 : 1152 + g * 384] = wu[:, h * 384 : h * 384 + 384]
    b.start_ring(bparts)
    o.start(wop)
    w.start(wdp)
    cs[y] = cot[...]
    first_keys(seg, low)
    rope_of(0, ic, isn, oc, osn, cos, sin)
    kv.pass_all_on()
    tokens_in.pass_on()
    near_tok.wait_recv()
    near_in.start()
    kv.pass_all_across()
    qw.pass_all_on()
    o.pass_all_on()
    b.pass_first()
    for back in (0, 1, 3, 2):
        tokens_in.block(back)
        r = wrap4(y - back)
        block = xs[r].astype(F32)
        scales[r] = rms_scale(block)
    kv.all_here()
    pack(wkl, wkv)

    pick = lax.broadcasted_iota(jnp.int32, (8, 128), 0) == lax.broadcasted_iota(jnp.int32, (8, 128), 1)
    by_row = dot(pick.astype(F32).astype(BF), wkv[:, 512:], 1, 1)
    rows[:, :1024] = by_row
    every = lax.broadcasted_iota(jnp.int32, (1024, 128), 0) == 8 * lax.broadcasted_iota(jnp.int32, (1024, 128), 1)
    rows[:, 1024:] = dot(by_row.astype(BF), every.astype(F32).astype(BF), 1, 0)
    attn_gain, ffn_gain = rows[0:1, :1024], rows[1:2, :1024]
    q_gain, k_gain = rows[2:3, 1024:], rows[3:4, 1024:]

    for r in range(4):
        xn[r * 128 : r * 128 + 128] = (xs[r].astype(F32) * scales[r] * attn_gain).astype(BF)

    def keys_values(rows_in, slot, cos_, sin_, g):
        raw = dot(rows_in, wkv[:, g * 256 : g * 256 + 256], 1, 0)
        k_raw = raw[:, :128]
        kvx[2 * g, slot] = rope(k_raw * rms_scale(k_raw) * k_gain, cos_[...], sin_[...]).astype(BF)
        kvx[2 * g + 1, slot] = raw[:, 128:].astype(BF)

    far = []
    for g in range(2):
        keys_values(xn[...], 2, cos, sin, g)
        pair = pl.ds(2 * g, 2)
        far.append(send(kvx.at[pair, 2], kvx.at[pair, 0], hsem.at[2 + g], hrem.at[2 + g], chunk_device(2)))
    sends += far
    near_in.pass_on()
    w.pass_all_on()
    qw.pass_all_across()
    rope_of(-1, ic, isn, oc, osn, cos_near, sin_near)
    qw.all_here()
    pack(wql, wqs)

    def queries(g, _):
        raw = dot(xn[...], wqs[:, pl.ds(pl.multiple_of(g * 256, 256), 256)], 1, 0)
        for hd in range(2):
            q_raw = raw[:, hd * 128 : hd * 128 + 128]
            rot = rope(q_raw * rms_scale(q_raw) * q_gain, cos[...], sin[...]).astype(BF)
            for t in range(2):
                q[g, t, hd * 256 : hd * 256 + 256] = rot[t * 256 : t * 256 + 256]
        return 0

    lax.fori_loop(0, 2, queries, 0)

    attend(q, kvx, low, peak, total, wide, 2, True)
    o.pass_all_across()
    for back in (1, 3, 2):
        near_in.block(back)
    cot_in.start()
    near_in.done()
    for r in range(4):
        block = xs_near[r].astype(F32)
        xs_near[r] = (block * rms_scale(block) * attn_gain).astype(BF)
    for g in range(2):
        keys_values(xs_near[...].reshape(CHUNK, 1024), 1, cos_near, sin_near, g)
    attend(q, kvx, low, peak, total, wide, 1, False)
    b.pass_all_on()
    cot_in.pass_on()
    for copy in far:
        copy.wait_recv()
    attend(q, kvx, low, peak, total, wide, 0, False)
    for g in range(2):
        for t in range(2):
            done = jnp.transpose(wide[g, t] / total[g, t]).astype(BF)
            lse[g, t] = peak[g, t] * EXP_SCALE + jnp.log(total[g, t]) * math.log2(math.e)
            for hd in range(2):
                cols = slice((g * 2 + hd) * 128, (g * 2 + hd) * 128 + 128)
                for half in range(2):
                    first = hd * 256 + half * 128
                    att[2 * t + half, :, cols] = done[first : first + 128]

    o.all_here()
    pack(wol, wo)
    tokens_in.done()
    for n in (2, 1, 3, 0):
        p = dot(att[wrap4(y + n)], wo[...], 1, 0)
        if n:
            part[n - 1] = p.astype(BF)
            sum_out.give(n)
        else:
            acc[...] = p + tok[...].astype(F32)
    for f in range(8):
        xnt[f * 128 : f * 128 + 128] = jnp.transpose(xn[:, f * 128 : f * 128 + 128])
    sum_out.relay()
    b.pass_all_across()
    w.pass_all_across()
    s = sum_out.total(acc[...])
    acc[...] = s
    scale = rms_scale(s)
    scale_two[...] = scale
    unit[...] = s * scale
    mid[y] = (s * scale * ffn_gain).astype(BF)
    mid_in.start()
    b.all_here()
    pack(wbl, wb)
    mid_in.pass_on()
    w.all_here()
    pack(wdl, wd)
    for back in (1, 3, 2):
        cot_in.block(back)
    for r in range(4):
        dhid[r] = dot(cs[r], wd[...], 1, 1)

    for k in (0, 1, 3, 2):
        r = wrap4(y - k)
        if k:
            mid_in.block(k)
        gu = dot(mid[r], wb[...], 1, 0)
        gate, up = gu[:, :768], gu[:, 768:]
        sig = 1.0 / (1.0 + jnp.exp(-gate))
        act = gate * sig
        dh = dhid[r]
        hid[r] = (act * up).astype(BF)
        dgu[r, :, :768] = (dh * up * sig * (1.0 + gate * (1.0 - sig))).astype(BF)
        dgu[r, :, 768:] = (dh * act).astype(BF)
        p = dot(dgu[r], wb[...], 1, 1)
        if k:
            dpart[3 - k] = p.astype(BF)
            sum_mid.give(4 - k)
        else:
            dmid[...] = p
    b.done()
    w.done()
    o.done()

    def gate_up_rows(f, _):
        span = pl.ds(pl.multiple_of(f * 128, 128), 128)
        lhs = mid[:, :, span].reshape(CHUNK, 128)
        g = dot(lhs, dgu[...].reshape(CHUNK, 1536), 0, 0)
        unpack(g, wbl, lax.div(f, 4), lax.rem(f, 4))
        return 0

    lax.fori_loop(0, 8, gate_up_rows, 0)
    sb.start()

    def down_rows(f, _):
        span = pl.ds(pl.multiple_of(f * 384, 384), 384)
        lhs = hid[:, :, span].reshape(CHUNK, 384)
        g = dot(lhs, cs[...].reshape(CHUNK, 1024), 0, 0)
        unpack(g, wdl, f, 0)
        return 0

    lax.fori_loop(0, 2, down_rows, 0)
    sd.start()
    sum_mid.relay()
    sb.cores()

    s = sum_mid.total(dmid[...])
    grow[...] = jnp.zeros_like(grow)
    grow[1:2] = jnp.sum(s * unit[...], axis=0, keepdims=True)
    s = s * ffn_gain
    mean = jnp.mean(s * unit[...], axis=-1, keepdims=True)
    s = cs[y].astype(F32) + scale_two[...] * (s - unit[...] * mean)
    dmid[...] = s
    dbr[y] = s.astype(BF)
    branch_in.start()
    for n in (2, 1, 3, 0):
        p = dot(hid[wrap4(y + n)], wd[...], 1, 0)
        if n:
            opart[n - 1] = p.astype(BF)
        else:
            acc[...] = acc[...] + p
    sd.cores()

    branch_in.pass_on()
    sb.second()
    for k in (0, 1, 3, 2):
        r = wrap4(y - k)
        if k:
            branch_in.block(k)
        datt[r] = dot(dbr[r], wo[...], 1, 1).astype(BF)
    for k in (2, 1, 3):
        ring_send(0, k, opart.at[k - 1], land3.at[k - 1])

    ones = jnp.ones((8, 128), BF)
    for g in range(2):
        for t in range(2):
            for hd in range(2):
                cols = slice((g * 2 + hd) * 128, (g * 2 + hd) * 128 + 128)
                for half in range(2):
                    first = hd * 256 + half * 128
                    d = datt[2 * t + half, :, cols]
                    do[g, t, first : first + 128] = d
                    prod = d.astype(F32) * att[2 * t + half, :, cols].astype(F32)
                    high = prod.astype(BF)
                    rest = (prod - high.astype(F32)).astype(BF)
                    inner[g, t, :, first : first + 128] = (dot(ones, high, 1, 1) + dot(ones, rest, 1, 1))[:1]
    dq = wide
    back_near, back_far = [], []

    def give_back(g, slot, step, copies):
        pair = pl.ds(2 * g, 2)
        dkvb[2 * g : 2 * g + 2, slot] = dkv[2 * g : 2 * g + 2, slot].astype(BF)
        n = 4 + 2 * slot + g
        copies.append(send(dkvb.at[pair, slot], land.at[slot, pair], hsem.at[n], hrem.at[n], chunk_device(step)))

    attend_back(q, kvx, low, lse, do, inner, dq, dkv, 1, True, lambda g: give_back(g, 1, -1, back_near))
    attend_back(q, kvx, low, lse, do, inner, dq, dkv, 0, False, lambda g: give_back(g, 0, -2, back_far))
    sd.second()
    sends += back_near + back_far

    def out_rows(f, _):
        span = pl.ds(pl.multiple_of(f * 256, 256), 256)
        lhs = att[:, :, span].reshape(CHUNK, 256)
        g = dot(lhs, dbr[...].reshape(CHUNK, 1024), 0, 0)
        unpack(g, wol, f, 0)
        return 0

    lax.fori_loop(0, 2, out_rows, 0)
    so.start()
    attend_back(q, kvx, low, lse, do, inner, dq, dkv, 2, False)

    scale = HEAD_SIZE ** (-0.5)
    raw = dhid
    raw[:, :, :512] = dot(xn[...], wqs[...], 1, 0).reshape(4, 128, 512)
    for g in range(2):
        raw[:, :, 512 + g * 128 : 640 + g * 128] = dot(xn[...], wkv[:, g * 256 : g * 256 + 128], 1, 0).reshape(4, 128, 128)
    kv.done()
    qw.done()
    g_q = jnp.zeros((1, 128), F32)
    for g in range(2):
        for t in range(2):
            d = jnp.transpose(dq[g, t] * scale).astype(BF).astype(F32)
            span = slice(t * 256, t * 256 + 256)
            for hd in range(2):
                cols = slice((g * 2 + hd) * 128, (g * 2 + hd) * 128 + 128)
                q_raw = raw[2 * t : 2 * t + 2, :, cols].reshape(256, 128)
                d_raw, d_gain = prep_back(d[hd * 256 : hd * 256 + 256], q_raw, q_gain, cos[span], sin[span])
                dqkv[span, cols] = d_raw.astype(BF)
                g_q = g_q + d_gain

    def query_rows(f, _):
        span = pl.ds(pl.multiple_of(f * 128, 128), 128)
        g = dot(xnt[span], dqkv[:, :512], 1, 0)
        unpack(g, wql, lax.div(f, 4), lax.rem(f, 4))
        of_gain = jnp.sum(g * wqs[span].astype(F32), axis=1, keepdims=True)
        grow[4:5, span] = jnp.transpose(jnp.broadcast_to(of_gain, (128, 128)))[:1]
        return 0

    lax.fori_loop(0, 8, query_rows, 0)
    sq.start()
    for r in range(4):
        dxq[r] = dot(dqkv[r * 128 : r * 128 + 128, :512], wqs[...], 1, 1)
    for n in (1, 3, 2):
        ring_wait(0, n, land3.at[n - 1])
    s = acc[...]
    for n in range(3):
        s = s + land3[n].astype(F32)
    out[...] = s.astype(BF)
    for r in range(4):
        gate_up = sb.last(r)
        h = wrap4(y - r)
        for g in range(2):
            span = pl.ds(pl.multiple_of((g * 4 + h) * 384, 128), 384)
            og[:, span] = gate_up[:, g * 384 : g * 384 + 384]
            ou[:, span] = gate_up[:, 768 + g * 384 : 1152 + g * 384]
    od[...] = sd.last()
    sum_out.done()
    for copy in back_near + back_far:
        copy.wait_recv()
    sq.cores()
    so.cores()
    g_k = jnp.zeros((1, 128), F32)
    for g in range(2):
        d = dkv[2 * g, 2] + land[0, 2 * g].astype(F32) + land[1, 2 * g].astype(F32)
        d = (d * scale).astype(BF).astype(F32)
        cols = slice(512 + g * 256, 640 + g * 256)
        k_raw = raw[:, :, 512 + g * 128 : 640 + g * 128].reshape(CHUNK, 128)
        d_raw, d_gain = prep_back(d, k_raw, k_gain, cos[...], sin[...])
        dqkv[:, cols] = d_raw.astype(BF)
        g_k = g_k + d_gain
        d = dkv[2 * g + 1, 2] + land[0, 2 * g + 1].astype(F32) + land[1, 2 * g + 1].astype(F32)
        dqkv[:, 640 + g * 256 : 768 + g * 256] = d.astype(BF)

    eight = lax.div(lax.broadcasted_iota(jnp.int32, (128, 1024), 1), 8) == lax.broadcasted_iota(jnp.int32, (128, 1024), 0)
    eight = eight.astype(F32).astype(BF)
    grow[2:3] = dot(jnp.broadcast_to(g_q, (8, 128)).astype(BF), eight, 1, 0)[:1]
    grow[3:4] = dot(jnp.broadcast_to(g_k, (8, 128)).astype(BF), eight, 1, 0)[:1]

    def key_rows(f, _):
        span = pl.ds(pl.multiple_of(f * 128, 128), 128)
        g = dot(xnt[span], dqkv[:, 512:], 1, 0)
        w_rows = wkv[span].astype(F32)
        tile = jnp.transpose(jnp.concatenate([grow[:, span], jnp.zeros((120, 128), F32)], axis=0))
        d_gain = (tile[:, 4:5] + jnp.sum(g * w_rows[:, :512], axis=1, keepdims=True)) / w_rows[:, 512:513]
        lane = lax.broadcasted_iota(jnp.int32, (128, 128), 1)
        tile = jnp.where(lane == 0, d_gain, tile)
        unpack(jnp.concatenate([g, tile], axis=1), wkl, lax.div(f, 4), lax.rem(f, 4))
        return 0

    lax.fori_loop(0, 8, key_rows, 0)
    sk.start()

    for n in (2, 1, 3, 0):
        r = wrap4(y + n)
        span = pl.ds(pl.multiple_of(r * 128, 128), 128)
        if n == 0:
            sk.cores()
            sum_x.relay()
        p = dxq[r] + dot(dqkv[span, 512:], wkv[:, :512], 1, 1)
        if n:
            part[n - 1] = p.astype(BF)
            sum_x.give(n)
        else:
            acc[...] = p
    sk.second()
    sq.second()
    so.second()
    s = sum_x.total(acc[...])
    own = tok[...].astype(F32)
    scale_own = rms_scale(own)
    own = own * scale_own
    s = s * attn_gain
    mean = jnp.mean(s * own, axis=-1, keepdims=True)
    igrad[...] = (dmid[...] + scale_own * (s - own * mean)).astype(BF)
    oo[...] = so.last()
    gain = jnp.zeros((8, 128), F32)
    for r in range(4):
        h = wrap4(y - r)
        queries_ = sq.last(r)
        keys_ = sk.last(r)
        for g in range(2):
            span = pl.ds(pl.multiple_of((g * 4 + h) * 128, 128), 128)
            oq[:, pl.ds(pl.multiple_of((g * 4 + h) * 256, 128), 256)] = queries_[:, g * 256 : g * 256 + 256]
            ok[:, span] = keys_[:, g * 256 : g * 256 + 128]
            ov[:, span] = keys_[:, g * 256 + 128 : g * 256 + 256]
        gain = gain + keys_[:, 512:640]
    ogain[...] = gain
    for copy in sends:
        copy.wait_send()
    for s in (sq, sk, sb, so, sd, tokens_in, mid_in, sum_mid, branch_in, sum_x, cot_in):
        s.done()


def whole_layer(tok, cot, wq, wk, wv, wg, wu, gains, wo, wd, segments):
    sds = jax.ShapeDtypeStruct
    block = (128, 1024)
    mem = lambda *shape: pltpu.VMEM(shape, BF)
    mem32 = lambda *shape: pltpu.VMEM(shape, F32)
    return pl.pallas_call(
        layer_kernel,
        out_shape=(
            sds(block, BF),
            sds(block, BF),
            sds((8, 2048), F32),
            sds((8, 1024), F32),
            sds((8, 1024), F32),
            sds((8, 3072), F32),
            sds((8, 3072), F32),
            sds((16, 1024), F32),
            sds((24, 1024), F32),
            sds((8, 128), F32),
        ),
        in_specs=[VMEM] * 7 + [SMEM] + [VMEM] * 7,
        out_specs=(VMEM,) * 10,
        scratch_shapes=[
            mem(4, 8, 640),
            mem(4, 8, 512),
            mem(4, 8, 1536),
            mem(2, 4, 4, 4, 8, 640),
            mem(2, 4, 4, 4, 8, 512),
            mem(2, 4, 4, 4, 8, 1536),
            mem(2, 4, 4, 1, 24, 1024),
            mem(2, 4, 4, 1, 16, 1024),
            mem(1024, 640),
            mem(1024, 512),
            mem(1024, 1536),
            mem(768, 1024),
            mem(512, 1024),
            pltpu.VMEM((2, 1, 512), jnp.int32),
            mem(4, *block),
            mem(4, *block),
            mem32(4, 128, 1),
            mem(4, *block),
            mem32(CHUNK, 128),
            mem32(CHUNK, 128),
            mem32(CHUNK, 128),
            mem32(CHUNK, 128),
            mem32(8, 1152),
            mem(CHUNK, 1024),
            mem(1024, CHUNK),
            mem(2, 2, 512, 128),
            mem(4, 3, CHUNK, 128),
            mem32(2, 2, 1, 512),
            mem32(2, 2, 1, 512),
            mem32(2, 2, 1, 512),
            mem32(2, 2, 128, 512),
            mem(4, 128, 512),
            mem(3, *block),
            mem(2, 64, 1024),
            mem(2, *block),
            mem32(*block),
            mem32(*block),
            mem32(4, 128, 768),
            mem(4, 128, 1536),
            mem(4, 128, 768),
            mem(3, *block),
            mem(2, 64, 1024),
            mem(2, *block),
            mem(4, *block),
            mem(3, *block),
            mem32(128, 1),
            mem(3, *block),
            mem32(*block),
            mem(4, 128, 512),
            mem(2, 2, 512, 128),
            mem32(2, 2, 1, 512),
            mem32(4, 3, CHUNK, 128),
            mem(4, 2, CHUNK, 128),
            mem(2, 4, CHUNK, 128),
            mem(CHUNK, 1024),
            mem32(8, 1024),
            mem32(4, *block),
            DMA((8, 6)),
            DMA((8, 6)),
            DMA((2, 3)),
            DMA((2, 3)),
            DMA((8,)),
            DMA((8,)),
        ]
        + Pieces.semaphores() * 5
        + Sums.scratch(8, 512, 4)
        + Sums.scratch(8, 640, 4)
        + Sums.scratch(8, 1536, 4)
        + Sums.scratch(16, 1024, 1)
        + Sums.scratch(24, 1024, 1),
        compiler_params=params(0),
        name="whole_layer",
    )(tok, cot, wq, wk, wv, wg, wu, gains, wo, wd, segments.reshape(128, 128), *rope_tables())


def results_kernel(*refs):
    ins, outs = refs[:10], refs[10:]
    for src, dst in zip(ins[:9], outs):
        dst[...] = src[...]
    gains = ins[9][...]
    row = lax.broadcasted_iota(jnp.int32, (8, 128), 0)
    col = lax.broadcasted_iota(jnp.int32, (8, 128), 1)
    for kind, dst in enumerate(outs[9:]):
        for i in range(dst.shape[0]):
            dst[i] = jnp.sum(jnp.where((row == i) & (col == kind), gains, 0.0))


def results(*arrays):
    vectors = [jax.ShapeDtypeStruct((n,), F32) for n in (8, 8, 1, 1)]
    return pl.pallas_call(
        results_kernel,
        out_shape=tuple(jax.ShapeDtypeStruct(r.shape, r.dtype) for r in arrays[:9]) + tuple(vectors),
        in_specs=[VMEM] * 10,
        out_specs=(VMEM,) * 9 + (SMEM,) * 4,
        name="results",
    )(*arrays)


def local(
    tokens, cotangent, segments, attn_gain, w_query, key_matrix, value_matrix, query_gain, key_gain,
    w_out, ffn_gain, w_gate, w_up, w_down,
):
    gains = jnp.concatenate([attn_gain, ffn_gain, query_gain, key_gain]).astype(F32)
    output, input_grad, g_query, g_key, g_value, g_gate, g_up, g_out, g_down, g_attn, g_ffn, g_qg, g_kg = results(
        *whole_layer(
            tokens, cotangent, w_query, key_matrix, value_matrix, w_gate, w_up, gains, w_out, w_down, segments
        )
    )
    return (
        output, input_grad, g_attn, g_query, g_key, g_value, g_qg, g_kg, g_out, g_ffn, g_gate, g_up, g_down,
    )


def solution(mesh):
    rows = P(("blk", "head"), None)
    cut = P(("head", "blk"), None)
    vec = P(("head", "blk"))
    return jax.shard_map(
        local,
        mesh=mesh,
        in_specs=(rows, rows, P(), vec, cut, cut, cut, vec, vec, cut, vec, cut, cut, cut),
        out_specs=(rows, rows, vec, cut, cut, cut, vec, vec, cut, vec, cut, cut, cut),
        check_vma=False,
    )
```

```python
import math

import jax
import jax.numpy as jnp
import numpy as np
from jax import lax
from jax.experimental import pallas as pl
from jax.experimental.pallas import tpu as pltpu
from jax.sharding import PartitionSpec as P

HEAD_SIZE = 128
SPAN = 1024
CHUNK = 512
EPS = 1e-06
ROPE_BASE = 1000000.0
MASKED = -1e30
MESH = pl.DeviceIdType.MESH
BF = jnp.bfloat16
F32 = jnp.float32
VMEM = pl.BlockSpec(memory_space=pltpu.VMEM)
SMEM = pl.BlockSpec(memory_space=pltpu.SMEM)
DMA = pltpu.SemaphoreType.DMA
VMEM_LIMIT = 62 * 2**20


def coords():
    h = lax.axis_index("head")
    b = lax.axis_index("blk")
    x = 2 * lax.div(h, 4) + lax.div(b, 8)
    return x, lax.rem(h, 4), lax.rem(lax.div(b, 2), 4), lax.rem(b, 2)


def device(x, y, z, c):
    return (lax.div(x, 2) * 4 + y, lax.rem(x, 2) * 8 + z * 2 + c)


def wrap4(v):
    return lax.rem(v + 8, 4)


def send(src, dst, send_sem, recv_sem, to):
    copy = pltpu.make_async_remote_copy(
        src_ref=src, dst_ref=dst, send_sem=send_sem, recv_sem=recv_sem, device_id=to, device_id_type=MESH
    )
    copy.start()
    return copy


def arrived(dst, sem, anyone):
    pltpu.make_async_remote_copy(
        src_ref=dst, dst_ref=dst, send_sem=sem, recv_sem=sem, device_id=anyone, device_id_type=MESH
    ).wait_recv()


def greet(peers):
    barrier = pltpu.get_barrier_semaphore()
    for peer in peers:
        pl.semaphore_signal(barrier, inc=1, device_id=peer, device_id_type=MESH)
    return lambda: pl.semaphore_wait(barrier, len(peers))


def params(collective_id):
    return pltpu.CompilerParams(
        collective_id=collective_id, has_side_effects=True, vmem_limit_bytes=VMEM_LIMIT
    )


def chunk_number():
    return 2 * lax.axis_index("blk") + lax.div(lax.axis_index("head"), 4)


def chunk_device(step):
    chunk = lax.rem(chunk_number() + step + 32, 32)
    return (lax.rem(chunk, 2) * 4 + lax.rem(lax.axis_index("head"), 4), lax.div(chunk, 2))


def greet_all():
    x, y, z, c = coords()
    peers = [device(x, y, z, 1 - c)]
    for j in range(4):
        for r in range(4):
            if j or r:
                peers.append(device(wrap4(x + j * (1 - c)), wrap4(y + r), wrap4(z + j * c), c))
    peers += [device(wrap4(x + k * c), y, wrap4(z + k * (1 - c)), c) for k in range(1, 4)]
    return greet(peers + [chunk_device(s) for s in (-2, -1, 1, 2)])


def dot(a, b, ca, cb):
    return lax.dot_general(a, b, (((ca,), (cb,)), ((), ())), preferred_element_type=F32)


def rms_scale(rows):
    return lax.rsqrt(jnp.mean(rows * rows, axis=-1, keepdims=True) + EPS)


def rope_tables():
    freq = ROPE_BASE ** (-np.arange(0, HEAD_SIZE, 2, dtype=np.float64) / HEAD_SIZE)
    freq = np.concatenate([freq, freq])
    sign = np.where(np.arange(HEAD_SIZE) < 64, -1.0, 1.0)
    inner = np.arange(CHUNK)[:, None] * freq[None, :]
    outer = (np.arange(32) * CHUNK)[:, None] * freq[None, :]
    tables = [f(a) * s for a in (inner, outer) for f, s in ((np.cos, 1.0), (np.sin, sign))]
    return [jnp.asarray(t.astype(np.float32)) for t in tables]


def rope_of(step, ic, isn, oc, osn, cos, sin):
    n = lax.rem(chunk_number() + step + 32, 32)
    c0, s0 = oc[pl.ds(n, 1), :], osn[pl.ds(n, 1), :]
    cos[...] = c0 * ic[...] - s0 * isn[...]
    sin[...] = s0 * ic[...] + c0 * isn[...]


def rope(rows, cos, sin):
    return rows * cos + pltpu.roll(rows, 64, 1) * sin


def rope_back(rows, cos, sin):
    return rows * cos + pltpu.roll(rows * sin, 64, 1)


def prep_back(d, raw, gain, cos, sin):
    scale = rms_scale(raw)
    unit = raw * scale
    d = rope_back(d, cos, sin)
    d_gain = jnp.sum(d * unit, axis=0, keepdims=True)
    d = d * gain
    return scale * (d - unit * jnp.mean(d * unit, axis=-1, keepdims=True)), d_gain


def first_keys(seg, low):
    start = chunk_number() * 4 - 8
    rows = []
    for i in range(12):
        row = seg[pl.ds(jnp.maximum(start + i, 0), 1), :].astype(F32)
        rows.append(jnp.where(start + i < 0, -1.0, row))
    keys = jnp.transpose(jnp.concatenate(rows + [jnp.zeros((116, 128), F32)], axis=0))
    for t in range(2):
        for half in range(2):
            query = rows[8 + 2 * t + half]
            begins = jnp.zeros((1, 128), F32)
            for i in range(12):
                before = jnp.where(keys[:, i : i + 1] < query, 1.0, 0.0)
                begins = begins + jnp.sum(before, axis=0, keepdims=True)
            row = lax.broadcasted_iota(jnp.int32, (1, 128), 1) + (t * 256 + half * 128 + 1)
            for hd in range(2):
                at = hd * 256 + half * 128
                low[t, :, at : at + 128] = jnp.maximum(begins.astype(jnp.int32), row)


def gain_tile(gains):
    row = lax.broadcasted_iota(jnp.int32, (8, 128), 0)
    col = lax.broadcasted_iota(jnp.int32, (8, 128), 1)
    tile = jnp.where(col == 2, gains[16], jnp.where(col == 3, gains[17], 0.0))
    for i in range(8):
        tile = jnp.where((row == i) & (col == 0), gains[i], tile)
        tile = jnp.where((row == i) & (col == 1), gains[8 + i], tile)
    return tile.astype(BF)


REACH = (((0, 512), (256, 256)), ((0, 512), (0, 512)), ((0, 256), (0, 512)))
EXP_SCALE = HEAD_SIZE ** (-0.5) * math.log2(math.e)


def allowed(low, slot, t):
    first, count = REACH[slot][t]
    place = lax.broadcasted_iota(jnp.int32, (count, 512), 0) + (slot * CHUNK + first)
    ok = place >= low[t]
    if slot == 2:
        query = lax.rem(lax.broadcasted_iota(jnp.int32, (1, 512), 1), 256) + (t * 256 + SPAN)
        ok = ok & (place <= query)
    return ok


def attend(q, kvx, low, peak, total, acc, slot, fresh):
    def group(g, _):
        for t in range(2):
            first, count = REACH[slot][t]
            keys = kvx[2 * g, slot, first : first + count]
            values = kvx[2 * g + 1, slot, first : first + count]
            s = dot(keys, q[g, t], 1, 1)
            s = jnp.where(allowed(low, slot, t), s, MASKED)
            top = jnp.max(s, axis=0, keepdims=True)
            if not fresh:
                before = peak[g, t]
                top = jnp.maximum(top, before)
                fade = jnp.exp2((before - top) * EXP_SCALE)
            p = jnp.exp2((s - top) * EXP_SCALE)
            add = jnp.sum(p, axis=0, keepdims=True)
            o = dot(values, p.astype(BF), 0, 0)
            if not fresh:
                add = add + total[g, t] * fade
                o = o + acc[g, t] * fade
            peak[g, t] = top
            total[g, t] = add
            acc[g, t] = o
        return 0

    lax.fori_loop(0, 2, group, 0)


def attend_back(q, kvx, low, lse, do, inner, dq, dkv, slot, fresh, after=None):
    def group(g, _):
        for t in range(2):
            first, count = REACH[slot][t]
            rows = slice(first, first + count)
            keys = kvx[2 * g, slot, rows]
            values = kvx[2 * g + 1, slot, rows]
            s = dot(keys, q[g, t], 1, 1)
            p = jnp.where(allowed(low, slot, t), jnp.exp2(s * EXP_SCALE - lse[g, t]), 0.0)
            dp = dot(values, do[g, t], 1, 1)
            ds = (p * (dp - inner[g, t])).astype(BF)
            dv = dot(p.astype(BF), do[g, t], 1, 0)
            dk = dot(ds, q[g, t], 1, 0)
            for n, d in ((2 * g, dk), (2 * g + 1, dv)):
                if t == 0:
                    dkv[n, slot, rows] = d
                elif slot == 2:
                    dkv[n, slot, :256] = dkv[n, slot, :256] + d[:256]
                    dkv[n, slot, 256:] = d[256:]
                else:
                    dkv[n, slot, rows] = dkv[n, slot, rows] + d
            d = dot(keys, ds, 0, 0)
            dq[g, t] = d if fresh else dq[g, t] + d
        return 0

    if after is None:
        lax.fori_loop(0, 2, group, 0)
    else:
        for g in range(2):
            group(g, 0)
            after(g)


LOW, HIGH = pl.ds(0, 64), pl.ds(64, 64)


class Ring:
    def __init__(self, ssem, rsem):
        x, self.y, z, c = coords()
        self.next = device(x, wrap4(self.y + 1), z, c)
        self.last = device(x, wrap4(self.y + 3), z, c)
        self.ssem, self.rsem = ssem, rsem
        self.sends = []

    def send(self, n, src, dst, to):
        self.sends.append(send(src, dst, self.ssem.at[n], self.rsem.at[n], to))

    def wait(self, n, dst):
        arrived(dst, self.rsem.at[n], self.next)

    def done(self):
        for copy in self.sends:
            copy.wait_send()
        self.sends = []


class RingGather(Ring):
    def __init__(self, ref, ssem, rsem):
        super().__init__(ssem, rsem)
        self.ref = ref

    def half(self, back, rows):
        return self.ref.at[wrap4(self.y - back), rows]

    def start(self):
        low, high = self.half(0, LOW), self.half(0, HIGH)
        self.send(0, low, low, self.next)
        self.send(1, high, high, self.last)
        self.send(2, high, high, self.next)
        self.send(3, low, low, self.last)

    def pass_on(self):
        low, high = self.half(1, LOW), self.half(3, HIGH)
        self.wait(0, low)
        self.send(4, low, low, self.next)
        self.wait(1, high)
        self.send(5, high, high, self.last)

    def block(self, back):
        if back == 1:
            self.wait(2, self.half(1, HIGH))
        elif back == 3:
            self.wait(3, self.half(3, LOW))
        elif back == 2:
            self.wait(4, self.half(2, LOW))
            self.wait(5, self.half(2, HIGH))


class RingSum(Ring):
    def __init__(self, part, relayed, landed, ssem, rsem):
        super().__init__(ssem, rsem)
        self.part, self.relayed, self.landed = part, relayed, landed

    def give(self, k):
        part = self.part.at[k - 1]
        if k == 2:
            self.send(0, part.at[LOW], self.relayed.at[0], self.next)
            self.send(1, part.at[HIGH], self.relayed.at[1], self.last)
        elif k == 1:
            self.send(2, part.at[HIGH], self.landed.at[0, HIGH], self.next)
        else:
            self.send(3, part.at[LOW], self.landed.at[1, LOW], self.last)

    def relay(self):
        part, relayed, landed = self.part, self.relayed, self.landed
        self.wait(0, relayed.at[0])
        part[0, :64] = (part[0, :64].astype(F32) + relayed[0].astype(F32)).astype(BF)
        self.send(4, part.at[0, LOW], landed.at[0, LOW], self.next)
        self.wait(1, relayed.at[1])
        part[2, 64:] = (part[2, 64:].astype(F32) + relayed[1].astype(F32)).astype(BF)
        self.send(5, part.at[2, HIGH], landed.at[1, HIGH], self.last)

    def total(self, own):
        landed = self.landed
        self.wait(2, landed.at[0, HIGH])
        self.wait(3, landed.at[1, LOW])
        self.wait(4, landed.at[0, LOW])
        self.wait(5, landed.at[1, HIGH])
        return own + landed[0].astype(F32) + landed[1].astype(F32)


class Pieces:
    def __init__(self, ref, ssem, rsem):
        self.ref, self.wide, self.ssem, self.rsem = ref, ref.shape[3] == 4, ssem, rsem
        self.x, self.y, self.z, self.c = x, y, z, c = coords()
        self.d = 1 - c
        self.p1 = x * self.d + z * c
        self.p2 = x * c + z * self.d
        self.across = device(x, y, z, 1 - c)
        self.sends = []
        self.whole = False

    @staticmethod
    def semaphores():
        return [DMA((32,)), DMA((32,))]

    def piece(self, j, k):
        return self.ref.at[self.c, wrap4(self.p2 - k), wrap4(self.p1 - j)]

    def send(self, src, dst, n, to):
        self.sends.append(send(src, dst, self.ssem.at[n], self.rsem.at[n], to))

    def ahead(self, j, k, r=0):
        c, d = self.c, self.d
        return device(wrap4(self.x + j * d + k * c), wrap4(self.y + r), wrap4(self.z + j * c + k * d), c)

    def from_source(self, j, r):
        return self.ref.at[self.c, self.p2, wrap4(self.p1 - j), wrap4(self.y - r) if self.wide else 0]

    def start(self, parts):
        here = self.from_source(0, 0)
        for j in (2, 1, 3, 0):
            for r in (2, 1, 3, 0) if self.wide else (0,):
                if j or r:
                    src = parts.at[wrap4(self.y + r)] if self.wide else parts
                    self.send(src, here, 4 * j + r, self.ahead(j, 0, r))
        if self.wide:
            self.ref[self.c, self.p2, self.p1, self.y] = parts[self.y]
        else:
            self.ref[self.c, self.p2, self.p1, 0] = parts[...]

    def start_ring(self, parts):
        here = self.from_source(0, 0)
        for r in (2, 1, 3):
            self.send(parts.at[wrap4(self.y + r)], here, r, self.ahead(0, 0, r))
        self.ref[self.c, self.p2, self.p1, self.y] = parts[self.y]

    def pass_first(self):
        for r in (1, 3, 2):
            arrived(self.from_source(0, r), self.rsem.at[r], self.across)
        here = self.piece(0, 0)
        for j in (2, 1, 3):
            self.send(here, here, 4 * j, self.ahead(j, 0))
        self.whole = True

    def pass_all_on(self):
        for j in (0, 1, 3, 2):
            if self.whole:
                if j:
                    arrived(self.piece(j, 0), self.rsem.at[4 * j], self.across)
            else:
                for r in range(4) if self.wide else (0,):
                    if j or r:
                        arrived(self.from_source(j, r), self.rsem.at[4 * j + r], self.across)
            here = self.piece(j, 0)
            for k in (2, 1, 3):
                self.send(here, here, 15 + 3 * j + k, self.ahead(0, k))

    def pass_all_across(self):
        for j in (0, 1, 3, 2):
            for k in (1, 3, 2):
                arrived(self.piece(j, k), self.rsem.at[15 + 3 * j + k], self.across)
            here = self.ref.at[self.c, :, wrap4(self.p1 - j)]
            self.send(here, here, 28 + j, self.across)

    def all_here(self):
        for j in range(4):
            arrived(self.ref.at[self.d, :, wrap4(self.p2 - j)], self.rsem.at[28 + j], self.across)

    def done(self):
        for copy in self.sends:
            copy.wait_send()


def pack(src, dst):
    _, _, _, cut, rows, cols = src.shape

    def block(i, _):
        px, r = lax.div(i, cut), lax.rem(i, cut)
        both = jnp.stack([src[0, :, px, r].astype(F32), src[1, px, :, r].astype(F32)], axis=1)
        first = lax.div(px, 2) * (16 * cut * rows) + r * (16 * rows) + lax.rem(px, 2) * (8 * rows)
        dst[pl.ds(pl.multiple_of(first, 8 * rows), 8 * rows)] = both.reshape(8 * rows, cols).astype(BF)
        return 0

    lax.fori_loop(0, 4 * cut, block, 0)


def unpack(part, dst, xh, r):
    _, _, _, _, rows, cols = dst.shape
    part = part.reshape(2, 4, 2, rows, cols).astype(BF)
    for xl in range(2):
        px = 2 * xh + xl
        dst[0, :, px, r] = part[xl, :, 0]
        dst[1, px, :, r] = part[xl, :, 1]


class Sums:
    def __init__(self, grad, refs):
        self.grad, self.cut = grad, grad.shape[3]
        (self.rc, self.lb, self.lg, self.ss, self.rs) = refs
        x, y, z, c = coords()
        self.y, self.c, self.d = y, c, 1 - c
        d = self.d
        self.across = device(x, y, z, d)
        self.ahead = lambda j, k, r: device(wrap4(x + j * d + k * c), wrap4(y + r), wrap4(z + j * c + k * d), c)
        self.p1 = x * d + z * c
        self.p2 = x * c + z * d
        self.sends = []

    @staticmethod
    def scratch(rows, cols, cut):
        buffers = [(4, 4, cut), (3, 4, cut), (4, cut)]
        return [pltpu.VMEM(lead + (rows, cols), BF) for lead in buffers] + [DMA((20,)), DMA((20,))]

    def send(self, src, dst, n, to):
        self.sends.append(send(src, dst, self.ss.at[n], self.rs.at[n], to))

    def start(self):
        self.send(self.grad.at[self.d], self.rc, 0, self.across)

    def cores(self):
        arrived(self.rc, self.rs.at[0], self.across)
        for k in (2, 1, 3, 0):
            a2 = wrap4(self.p2 + k)
            self.rc[a2] = (self.rc[a2].astype(F32) + self.grad[self.c, a2].astype(F32)).astype(BF)
            if k:
                self.send(self.rc.at[a2], self.lb.at[k - 1], k, self.ahead(0, k, 0))

    def second(self):
        for k in (1, 3, 2):
            arrived(self.lb.at[k - 1], self.rs.at[k], self.across)
        total = self.rc[self.p2].astype(F32)
        for k in range(3):
            total = total + self.lb[k].astype(F32)
        self.rc[self.p2] = total.astype(BF)
        for j in (2, 1, 3, 0):
            for r in (2, 1, 3, 0) if self.cut > 1 else (0,):
                if j or r:
                    src = self.rc.at[self.p2, wrap4(self.p1 + j), wrap4(self.y + r) if self.cut > 1 else 0]
                    self.send(src, self.lg.at[j, r], 4 + 4 * j + r, self.ahead(j, 0, r))
        self.lg[0, 0] = self.rc[self.p2, self.p1, self.y if self.cut > 1 else 0]

    def last(self, r=0):
        total = 0.0
        for j in range(4):
            if j or r:
                arrived(self.lg.at[j, r], self.rs.at[4 + 4 * j + r], self.across)
            total = total + self.lg[j, r].astype(F32)
        return total

    def done(self):
        for copy in self.sends:
            copy.wait_send()


def layer_kernel(
    tok, cot, wq, wk, wv, wg, wu, gains, wop, wdp, seg, ic, isn, oc, osn,
    out, igrad, oq, ok, ov, og, ou, oo, od, ogain,
    kparts, qparts, bparts, wkl, wql, wbl, wdl, wol, wkv, wqs, wb, wd, wo, low, xs, xs_near, scales, cs, cos, sin, cos_near, sin_near, rows, xn, xnt, q, kvx, lse,
    peak, total, wide, att, part, relay1, land1, acc, unit, dhid, dgu, hid, dpart, relay2, land2, dbr, opart, scale_two, land3,
    dmid, datt, do, inner, dkv, dkvb, land, dqkv, grow, dxq, rsend, rrecv, ssem, rsem, hsem, hrem, *scratch,
):
    x, y, z, c = coords()
    ring = [device(x, wrap4(y + k), z, c) for k in range(1, 4)]
    take = lambda n: [scratch.pop(0) for _ in range(n)]
    scratch = list(scratch)
    kv, qw, b, o, w = [Pieces(ref, *take(2)) for ref in (wkl, wql, wbl, wol, wdl)]
    sq, sk, sb, so, sd = [Sums(ref, take(5)) for ref in (wql, wkl, wbl, wol, wdl)]
    sends = []

    def ring_send(n, k, src, dst):
        sends.append(send(src, dst, ssem.at[n, k - 1], rsem.at[n, k - 1], ring[k - 1]))
        return sends[-1]

    def ring_wait(n, k, dst):
        arrived(dst, rsem.at[n, k - 1], ring[0])

    mid = xs
    tokens_in = RingGather(xs, rsend.at[0], rrecv.at[0])
    sum_out = RingSum(part, relay1, land1, rsend.at[1], rrecv.at[1])
    mid_in = RingGather(mid, rsend.at[2], rrecv.at[2])
    sum_mid = RingSum(dpart, relay2, land2, rsend.at[3], rrecv.at[3])
    branch_in = RingGather(dbr, rsend.at[4], rrecv.at[4])
    sum_x = RingSum(part, relay1, land1, rsend.at[5], rrecv.at[5])
    near_in = RingGather(xs_near, rsend.at[6], rrecv.at[6])
    cot_in = RingGather(cs, rsend.at[7], rrecv.at[7])

    everyone = greet_all()
    for r in range(4):
        for g in range(2):
            h = g * 4 + r
            kparts[r, :, g * 256 : 128 + g * 256] = wk[:, h * 128 : h * 128 + 128]
            kparts[r, :, 128 + g * 256 : 256 + g * 256] = wv[:, h * 128 : h * 128 + 128]
            qparts[r, :, g * 256 : g * 256 + 256] = wq[:, h * 256 : h * 256 + 256]
        kparts[r, :, 512:] = gain_tile(gains)
    xs[y] = tok[...]
    everyone()
    kv.start(kparts)
    near_tok = send(tok, xs_near.at[y], hsem.at[0], hrem.at[0], chunk_device(1))
    sends.append(near_tok)
    tokens_in.start()
    qw.start(qparts)
    for r in range(4):
        for g in range(2):
            h = g * 4 + r
            bparts[r, :, g * 384 : g * 384 + 384] = wg[:, h * 384 : h * 384 + 384]
            bparts[r, :, 768 + g * 384 : 1152 + g * 384] = wu[:, h * 384 : h * 384 + 384]
    b.start_ring(bparts)
    o.start(wop)
    w.start(wdp)
    cs[y] = cot[...]
    first_keys(seg, low)
    rope_of(0, ic, isn, oc, osn, cos, sin)
    kv.pass_all_on()
    tokens_in.pass_on()
    near_tok.wait_recv()
    near_in.start()
    kv.pass_all_across()
    qw.pass_all_on()
    o.pass_all_on()
    b.pass_first()
    for back in (0, 1, 3, 2):
        tokens_in.block(back)
        r = wrap4(y - back)
        block = xs[r].astype(F32)
        scales[r] = rms_scale(block)
    kv.all_here()
    pack(wkl, wkv)

    pick = lax.broadcasted_iota(jnp.int32, (8, 128), 0) == lax.broadcasted_iota(jnp.int32, (8, 128), 1)
    by_row = dot(pick.astype(F32).astype(BF), wkv[:, 512:], 1, 1)
    rows[:, :1024] = by_row
    every = lax.broadcasted_iota(jnp.int32, (1024, 128), 0) == 8 * lax.broadcasted_iota(jnp.int32, (1024, 128), 1)
    rows[:, 1024:] = dot(by_row.astype(BF), every.astype(F32).astype(BF), 1, 0)
    attn_gain, ffn_gain = rows[0:1, :1024], rows[1:2, :1024]
    q_gain, k_gain = rows[2:3, 1024:], rows[3:4, 1024:]

    for r in range(4):
        xn[r * 128 : r * 128 + 128] = (xs[r].astype(F32) * scales[r] * attn_gain).astype(BF)

    def keys_values(rows_in, slot, cos_, sin_, g):
        raw = dot(rows_in, wkv[:, g * 256 : g * 256 + 256], 1, 0)
        k_raw = raw[:, :128]
        kvx[2 * g, slot] = rope(k_raw * rms_scale(k_raw) * k_gain, cos_[...], sin_[...]).astype(BF)
        kvx[2 * g + 1, slot] = raw[:, 128:].astype(BF)

    far = []
    for g in range(2):
        keys_values(xn[...], 2, cos, sin, g)
        pair = pl.ds(2 * g, 2)
        far.append(send(kvx.at[pair, 2], kvx.at[pair, 0], hsem.at[2 + g], hrem.at[2 + g], chunk_device(2)))
    sends += far
    near_in.pass_on()
    w.pass_all_on()
    qw.pass_all_across()
    rope_of(-1, ic, isn, oc, osn, cos_near, sin_near)
    qw.all_here()
    pack(wql, wqs)

    def queries(g, _):
        raw = dot(xn[...], wqs[:, pl.ds(pl.multiple_of(g * 256, 256), 256)], 1, 0)
        for hd in range(2):
            q_raw = raw[:, hd * 128 : hd * 128 + 128]
            rot = rope(q_raw * rms_scale(q_raw) * q_gain, cos[...], sin[...]).astype(BF)
            for t in range(2):
                q[g, t, hd * 256 : hd * 256 + 256] = rot[t * 256 : t * 256 + 256]
        return 0

    lax.fori_loop(0, 2, queries, 0)

    attend(q, kvx, low, peak, total, wide, 2, True)
    o.pass_all_across()
    for back in (1, 3, 2):
        near_in.block(back)
    cot_in.start()
    near_in.done()
    for r in range(4):
        block = xs_near[r].astype(F32)
        xs_near[r] = (block * rms_scale(block) * attn_gain).astype(BF)
    for g in range(2):
        keys_values(xs_near[...].reshape(CHUNK, 1024), 1, cos_near, sin_near, g)
    attend(q, kvx, low, peak, total, wide, 1, False)
    b.pass_all_on()
    cot_in.pass_on()
    for copy in far:
        copy.wait_recv()
    attend(q, kvx, low, peak, total, wide, 0, False)
    for g in range(2):
        for t in range(2):
            done = jnp.transpose(wide[g, t] / total[g, t]).astype(BF)
            lse[g, t] = peak[g, t] * EXP_SCALE + jnp.log(total[g, t]) * math.log2(math.e)
            for hd in range(2):
                cols = slice((g * 2 + hd) * 128, (g * 2 + hd) * 128 + 128)
                for half in range(2):
                    first = hd * 256 + half * 128
                    att[2 * t + half, :, cols] = done[first : first + 128]

    o.all_here()
    pack(wol, wo)
    tokens_in.done()
    for n in (2, 1, 3, 0):
        p = dot(att[wrap4(y + n)], wo[...], 1, 0)
        if n:
            part[n - 1] = p.astype(BF)
            sum_out.give(n)
        else:
            acc[...] = p + tok[...].astype(F32)
    for f in range(8):
        xnt[f * 128 : f * 128 + 128] = jnp.transpose(xn[:, f * 128 : f * 128 + 128])
    sum_out.relay()
    b.pass_all_across()
    w.pass_all_across()
    s = sum_out.total(acc[...])
    acc[...] = s
    scale = rms_scale(s)
    scale_two[...] = scale
    unit[...] = s * scale
    mid[y] = (s * scale * ffn_gain).astype(BF)
    mid_in.start()
    b.all_here()
    pack(wbl, wb)
    mid_in.pass_on()
    w.all_here()
    pack(wdl, wd)
    for back in (1, 3, 2):
        cot_in.block(back)
    for r in range(4):
        dhid[r] = dot(cs[r], wd[...], 1, 1)

    for k in (0, 1, 3, 2):
        r = wrap4(y - k)
        if k:
            mid_in.block(k)
        gu = dot(mid[r], wb[...], 1, 0)
        gate, up = gu[:, :768], gu[:, 768:]
        sig = 1.0 / (1.0 + jnp.exp(-gate))
        act = gate * sig
        dh = dhid[r]
        hid[r] = (act * up).astype(BF)
        dgu[r, :, :768] = (dh * up * sig * (1.0 + gate * (1.0 - sig))).astype(BF)
        dgu[r, :, 768:] = (dh * act).astype(BF)
        p = dot(dgu[r], wb[...], 1, 1)
        if k:
            dpart[3 - k] = p.astype(BF)
            sum_mid.give(4 - k)
        else:
            dmid[...] = p
    b.done()
    w.done()
    o.done()

    def gate_up_rows(f, _):
        span = pl.ds(pl.multiple_of(f * 128, 128), 128)
        lhs = mid[:, :, span].reshape(CHUNK, 128)
        g = dot(lhs, dgu[...].reshape(CHUNK, 1536), 0, 0)
        unpack(g, wbl, lax.div(f, 4), lax.rem(f, 4))
        return 0

    lax.fori_loop(0, 8, gate_up_rows, 0)
    sb.start()

    def down_rows(f, _):
        span = pl.ds(pl.multiple_of(f * 384, 384), 384)
        lhs = hid[:, :, span].reshape(CHUNK, 384)
        g = dot(lhs, cs[...].reshape(CHUNK, 1024), 0, 0)
        unpack(g, wdl, f, 0)
        return 0

    lax.fori_loop(0, 2, down_rows, 0)
    sd.start()
    sum_mid.relay()
    sb.cores()

    s = sum_mid.total(dmid[...])
    grow[...] = jnp.zeros_like(grow)
    grow[1:2] = jnp.sum(s * unit[...], axis=0, keepdims=True)
    s = s * ffn_gain
    mean = jnp.mean(s * unit[...], axis=-1, keepdims=True)
    s = cs[y].astype(F32) + scale_two[...] * (s - unit[...] * mean)
    dmid[...] = s
    dbr[y] = s.astype(BF)
    branch_in.start()
    for n in (2, 1, 3, 0):
        p = dot(hid[wrap4(y + n)], wd[...], 1, 0)
        if n:
            opart[n - 1] = p.astype(BF)
        else:
            acc[...] = acc[...] + p
    sd.cores()

    branch_in.pass_on()
    sb.second()
    for k in (0, 1, 3, 2):
        r = wrap4(y - k)
        if k:
            branch_in.block(k)
        datt[r] = dot(dbr[r], wo[...], 1, 1).astype(BF)
    for k in (2, 1, 3):
        ring_send(0, k, opart.at[k - 1], land3.at[k - 1])

    ones = jnp.ones((8, 128), BF)

    def prepare(g):
        for t in range(2):
            for hd in range(2):
                cols = slice((g * 2 + hd) * 128, (g * 2 + hd) * 128 + 128)
                for half in range(2):
                    first = hd * 256 + half * 128
                    d = datt[2 * t + half, :, cols]
                    do[g, t, first : first + 128] = d
                    prod = d.astype(F32) * att[2 * t + half, :, cols].astype(F32)
                    high = prod.astype(BF)
                    rest = (prod - high.astype(F32)).astype(BF)
                    inner[g, t, :, first : first + 128] = (dot(ones, high, 1, 1) + dot(ones, rest, 1, 1))[:1]

    prepare(0)
    dq = wide
    back_near, back_far = [], []

    def give_back(g, slot, step, copies):
        pair = pl.ds(2 * g, 2)
        dkvb[2 * g : 2 * g + 2, slot] = dkv[2 * g : 2 * g + 2, slot].astype(BF)
        n = 4 + 2 * slot + g
        copies.append(send(dkvb.at[pair, slot], land.at[slot, pair], hsem.at[n], hrem.at[n], chunk_device(step)))

    def near_done(g):
        give_back(g, 1, -1, back_near)
        if g == 0:
            prepare(1)

    attend_back(q, kvx, low, lse, do, inner, dq, dkv, 1, True, near_done)
    attend_back(q, kvx, low, lse, do, inner, dq, dkv, 0, False, lambda g: give_back(g, 0, -2, back_far))
    sd.second()
    sends += back_near + back_far

    def out_rows(f, _):
        span = pl.ds(pl.multiple_of(f * 256, 256), 256)
        lhs = att[:, :, span].reshape(CHUNK, 256)
        g = dot(lhs, dbr[...].reshape(CHUNK, 1024), 0, 0)
        unpack(g, wol, f, 0)
        return 0

    lax.fori_loop(0, 2, out_rows, 0)
    so.start()
    attend_back(q, kvx, low, lse, do, inner, dq, dkv, 2, False)

    scale = HEAD_SIZE ** (-0.5)
    raw = dhid
    raw[:, :, :512] = dot(xn[...], wqs[...], 1, 0).reshape(4, 128, 512)
    for g in range(2):
        raw[:, :, 512 + g * 128 : 640 + g * 128] = dot(xn[...], wkv[:, g * 256 : g * 256 + 128], 1, 0).reshape(4, 128, 128)
    kv.done()
    qw.done()
    g_q = jnp.zeros((1, 128), F32)
    for g in range(2):
        for t in range(2):
            d = jnp.transpose(dq[g, t] * scale).astype(BF).astype(F32)
            span = slice(t * 256, t * 256 + 256)
            for hd in range(2):
                cols = slice((g * 2 + hd) * 128, (g * 2 + hd) * 128 + 128)
                q_raw = raw[2 * t : 2 * t + 2, :, cols].reshape(256, 128)
                d_raw, d_gain = prep_back(d[hd * 256 : hd * 256 + 256], q_raw, q_gain, cos[span], sin[span])
                dqkv[span, cols] = d_raw.astype(BF)
                g_q = g_q + d_gain

    def query_rows(f, _):
        span = pl.ds(pl.multiple_of(f * 128, 128), 128)
        g = dot(xnt[span], dqkv[:, :512], 1, 0)
        unpack(g, wql, lax.div(f, 4), lax.rem(f, 4))
        of_gain = jnp.sum(g * wqs[span].astype(F32), axis=1, keepdims=True)
        grow[4:5, span] = jnp.transpose(jnp.broadcast_to(of_gain, (128, 128)))[:1]
        return 0

    lax.fori_loop(0, 8, query_rows, 0)
    sq.start()
    for r in range(4):
        dxq[r] = dot(dqkv[r * 128 : r * 128 + 128, :512], wqs[...], 1, 1)
    for n in (1, 3, 2):
        ring_wait(0, n, land3.at[n - 1])
    s = acc[...]
    for n in range(3):
        s = s + land3[n].astype(F32)
    out[...] = s.astype(BF)
    for r in range(4):
        gate_up = sb.last(r)
        h = wrap4(y - r)
        for g in range(2):
            span = pl.ds(pl.multiple_of((g * 4 + h) * 384, 128), 384)
            og[:, span] = gate_up[:, g * 384 : g * 384 + 384]
            ou[:, span] = gate_up[:, 768 + g * 384 : 1152 + g * 384]
    od[...] = sd.last()
    sum_out.done()
    for copy in back_near + back_far:
        copy.wait_recv()
    sq.cores()
    so.cores()
    g_k = jnp.zeros((1, 128), F32)
    for g in range(2):
        d = dkv[2 * g, 2] + land[0, 2 * g].astype(F32) + land[1, 2 * g].astype(F32)
        d = (d * scale).astype(BF).astype(F32)
        cols = slice(512 + g * 256, 640 + g * 256)
        k_raw = raw[:, :, 512 + g * 128 : 640 + g * 128].reshape(CHUNK, 128)
        d_raw, d_gain = prep_back(d, k_raw, k_gain, cos[...], sin[...])
        dqkv[:, cols] = d_raw.astype(BF)
        g_k = g_k + d_gain
        d = dkv[2 * g + 1, 2] + land[0, 2 * g + 1].astype(F32) + land[1, 2 * g + 1].astype(F32)
        dqkv[:, 640 + g * 256 : 768 + g * 256] = d.astype(BF)

    eight = lax.div(lax.broadcasted_iota(jnp.int32, (128, 1024), 1), 8) == lax.broadcasted_iota(jnp.int32, (128, 1024), 0)
    eight = eight.astype(F32).astype(BF)
    grow[2:3] = dot(jnp.broadcast_to(g_q, (8, 128)).astype(BF), eight, 1, 0)[:1]
    grow[3:4] = dot(jnp.broadcast_to(g_k, (8, 128)).astype(BF), eight, 1, 0)[:1]

    def key_rows(f, _):
        span = pl.ds(pl.multiple_of(f * 128, 128), 128)
        g = dot(xnt[span], dqkv[:, 512:], 1, 0)
        w_rows = wkv[span].astype(F32)
        tile = jnp.transpose(jnp.concatenate([grow[:, span], jnp.zeros((120, 128), F32)], axis=0))
        d_gain = (tile[:, 4:5] + jnp.sum(g * w_rows[:, :512], axis=1, keepdims=True)) / w_rows[:, 512:513]
        lane = lax.broadcasted_iota(jnp.int32, (128, 128), 1)
        tile = jnp.where(lane == 0, d_gain, tile)
        unpack(jnp.concatenate([g, tile], axis=1), wkl, lax.div(f, 4), lax.rem(f, 4))
        return 0

    lax.fori_loop(0, 8, key_rows, 0)
    sk.start()

    for n in (2, 1, 3, 0):
        r = wrap4(y + n)
        span = pl.ds(pl.multiple_of(r * 128, 128), 128)
        if n == 0:
            sk.cores()
            sum_x.relay()
        p = dxq[r] + dot(dqkv[span, 512:], wkv[:, :512], 1, 1)
        if n:
            part[n - 1] = p.astype(BF)
            sum_x.give(n)
        else:
            acc[...] = p
    sk.second()
    sq.second()
    so.second()
    s = sum_x.total(acc[...])
    own = tok[...].astype(F32)
    scale_own = rms_scale(own)
    own = own * scale_own
    s = s * attn_gain
    mean = jnp.mean(s * own, axis=-1, keepdims=True)
    igrad[...] = (dmid[...] + scale_own * (s - own * mean)).astype(BF)
    oo[...] = so.last()
    gain = jnp.zeros((8, 128), F32)
    for r in range(4):
        h = wrap4(y - r)
        queries_ = sq.last(r)
        keys_ = sk.last(r)
        for g in range(2):
            span = pl.ds(pl.multiple_of((g * 4 + h) * 128, 128), 128)
            oq[:, pl.ds(pl.multiple_of((g * 4 + h) * 256, 128), 256)] = queries_[:, g * 256 : g * 256 + 256]
            ok[:, span] = keys_[:, g * 256 : g * 256 + 128]
            ov[:, span] = keys_[:, g * 256 + 128 : g * 256 + 256]
        gain = gain + keys_[:, 512:640]
    ogain[...] = gain
    for copy in sends:
        copy.wait_send()
    for s in (sq, sk, sb, so, sd, tokens_in, mid_in, sum_mid, branch_in, sum_x, cot_in):
        s.done()


def whole_layer(tok, cot, wq, wk, wv, wg, wu, gains, wo, wd, segments):
    sds = jax.ShapeDtypeStruct
    block = (128, 1024)
    mem = lambda *shape: pltpu.VMEM(shape, BF)
    mem32 = lambda *shape: pltpu.VMEM(shape, F32)
    return pl.pallas_call(
        layer_kernel,
        out_shape=(
            sds(block, BF),
            sds(block, BF),
            sds((8, 2048), F32),
            sds((8, 1024), F32),
            sds((8, 1024), F32),
            sds((8, 3072), F32),
            sds((8, 3072), F32),
            sds((16, 1024), F32),
            sds((24, 1024), F32),
            sds((8, 128), F32),
        ),
        in_specs=[VMEM] * 7 + [SMEM] + [VMEM] * 7,
        out_specs=(VMEM,) * 10,
        scratch_shapes=[
            mem(4, 8, 640),
            mem(4, 8, 512),
            mem(4, 8, 1536),
            mem(2, 4, 4, 4, 8, 640),
            mem(2, 4, 4, 4, 8, 512),
            mem(2, 4, 4, 4, 8, 1536),
            mem(2, 4, 4, 1, 24, 1024),
            mem(2, 4, 4, 1, 16, 1024),
            mem(1024, 640),
            mem(1024, 512),
            mem(1024, 1536),
            mem(768, 1024),
            mem(512, 1024),
            pltpu.VMEM((2, 1, 512), jnp.int32),
            mem(4, *block),
            mem(4, *block),
            mem32(4, 128, 1),
            mem(4, *block),
            mem32(CHUNK, 128),
            mem32(CHUNK, 128),
            mem32(CHUNK, 128),
            mem32(CHUNK, 128),
            mem32(8, 1152),
            mem(CHUNK, 1024),
            mem(1024, CHUNK),
            mem(2, 2, 512, 128),
            mem(4, 3, CHUNK, 128),
            mem32(2, 2, 1, 512),
            mem32(2, 2, 1, 512),
            mem32(2, 2, 1, 512),
            mem32(2, 2, 128, 512),
            mem(4, 128, 512),
            mem(3, *block),
            mem(2, 64, 1024),
            mem(2, *block),
            mem32(*block),
            mem32(*block),
            mem32(4, 128, 768),
            mem(4, 128, 1536),
            mem(4, 128, 768),
            mem(3, *block),
            mem(2, 64, 1024),
            mem(2, *block),
            mem(4, *block),
            mem(3, *block),
            mem32(128, 1),
            mem(3, *block),
            mem32(*block),
            mem(4, 128, 512),
            mem(2, 2, 512, 128),
            mem32(2, 2, 1, 512),
            mem32(4, 3, CHUNK, 128),
            mem(4, 2, CHUNK, 128),
            mem(2, 4, CHUNK, 128),
            mem(CHUNK, 1024),
            mem32(8, 1024),
            mem32(4, *block),
            DMA((8, 6)),
            DMA((8, 6)),
            DMA((2, 3)),
            DMA((2, 3)),
            DMA((8,)),
            DMA((8,)),
        ]
        + Pieces.semaphores() * 5
        + Sums.scratch(8, 512, 4)
        + Sums.scratch(8, 640, 4)
        + Sums.scratch(8, 1536, 4)
        + Sums.scratch(16, 1024, 1)
        + Sums.scratch(24, 1024, 1),
        compiler_params=params(0),
        name="whole_layer",
    )(tok, cot, wq, wk, wv, wg, wu, gains, wo, wd, segments.reshape(128, 128), *rope_tables())


def results_kernel(*refs):
    ins, outs = refs[:10], refs[10:]
    for src, dst in zip(ins[:9], outs):
        dst[...] = src[...]
    gains = ins[9][...]
    row = lax.broadcasted_iota(jnp.int32, (8, 128), 0)
    col = lax.broadcasted_iota(jnp.int32, (8, 128), 1)
    for kind, dst in enumerate(outs[9:]):
        for i in range(dst.shape[0]):
            dst[i] = jnp.sum(jnp.where((row == i) & (col == kind), gains, 0.0))


def results(*arrays):
    vectors = [jax.ShapeDtypeStruct((n,), F32) for n in (8, 8, 1, 1)]
    return pl.pallas_call(
        results_kernel,
        out_shape=tuple(jax.ShapeDtypeStruct(r.shape, r.dtype) for r in arrays[:9]) + tuple(vectors),
        in_specs=[VMEM] * 10,
        out_specs=(VMEM,) * 9 + (SMEM,) * 4,
        name="results",
    )(*arrays)


def local(
    tokens, cotangent, segments, attn_gain, w_query, key_matrix, value_matrix, query_gain, key_gain,
    w_out, ffn_gain, w_gate, w_up, w_down,
):
    gains = jnp.concatenate([attn_gain, ffn_gain, query_gain, key_gain]).astype(F32)
    output, input_grad, g_query, g_key, g_value, g_gate, g_up, g_out, g_down, g_attn, g_ffn, g_qg, g_kg = results(
        *whole_layer(
            tokens, cotangent, w_query, key_matrix, value_matrix, w_gate, w_up, gains, w_out, w_down, segments
        )
    )
    return (
        output, input_grad, g_attn, g_query, g_key, g_value, g_qg, g_kg, g_out, g_ffn, g_gate, g_up, g_down,
    )


def solution(mesh):
    rows = P(("blk", "head"), None)
    cut = P(("head", "blk"), None)
    vec = P(("head", "blk"))
    return jax.shard_map(
        local,
        mesh=mesh,
        in_specs=(rows, rows, P(), vec, cut, cut, cut, vec, vec, cut, vec, cut, cut, cut),
        out_specs=(rows, rows, vec, cut, cut, cut, vec, vec, cut, vec, cut, cut, cut),
        check_vma=False,
    )
```
